32 devices in a mesh: dp: 8 (over z, x), tile: 4 (over y, core).
Axes of the slice: x: 2, y: 2, z: 4, core: 2. Of those that a mesh axis runs over, the one named last changes fastest.
Arguments:
- patch_in: bfloat16 [8, 4, 16, 16, 768], P('dp', 'tile'), may hold values from -6 to 6
- cls_in: bfloat16 [8, 768], P('dp'), may hold values from -6 to 6
- page_side: int32 [8], P('dp'), may hold values from 14 to 32, as said below
- norm_attn: float32 [2, 768], replicated, may hold values from 0.25 to 1.75
- qkv_weight: bfloat16 [2, 768, 2304], replicated, may hold values from -0.21875 to 0.21875
- rel_table: float32 [2, 12, 49], replicated, may hold values from -4 to 4
- out_weight: bfloat16 [2, 768, 768], replicated, may hold values from -0.4375 to 0.4375
- scale_attn: float32 [2, 768], replicated, may hold values from 0.5 to 1.5
- norm_mlp: float32 [2, 768], replicated, may hold values from 0.25 to 1.75
- up_weight: bfloat16 [2, 768, 3072], replicated, may hold values from -0.21875 to 0.21875
- down_weight: bfloat16 [2, 3072, 768], replicated, may hold values from -0.109375 to 0.109375
- scale_mlp: float32 [2, 768], replicated, may hold values from 0.5 to 1.5
- patch_cot: bfloat16 [8, 4, 16, 16, 768], P('dp', 'tile'), may hold values from -6 to 6
- cls_cot: bfloat16 [8, 768], P('dp'), may hold values from -6 to 6
Outputs:
- patch_out: bfloat16 [8, 4, 16, 16, 768], P('dp', 'tile')
- cls_out: bfloat16 [8, 768], P('dp')
- patch_grad: float32 [8, 4, 16, 16, 768], P('dp', 'tile')
- cls_grad: float32 [8, 768], P('dp')
- grad_norm_attn: float32 [2, 768], P(None, ('dp', 'tile'))
- grad_qkv: float32 [2, 768, 2304], P(None, ('dp', 'tile'))
- grad_table: float32 [2, 12, 49], replicated
- grad_out: float32 [2, 768, 768], P(None, ('dp', 'tile'))
- grad_scale_attn: float32 [2, 768], P(None, ('dp', 'tile'))
- grad_norm_mlp: float32 [2, 768], P(None, ('dp', 'tile'))
- grad_up: float32 [2, 768, 3072], P(None, ('dp', 'tile'))
- grad_down: float32 [2, 3072, 768], P(None, ('dp', 'tile'))
- grad_scale_mlp: float32 [2, 768], P(None, ('dp', 'tile'))
The draws below stay inside these ranges and needn't reach their ends.
Inputs may be any that keep to these rules, and one draw needn't show every extreme that they name: `page_side`: every side is one of 14, 24 and 32; each aligned group of 4 consecutive pages holds a page of side 32.
All inputs are finite; a program needn't handle non-finite values.
Results may differ from the reference program's by a relative error of at most 0.017.
Values may be sent and summed in bfloat16 or wider, within the bound.
No kernel may reach another device: no remote copies, remote signals or barrier semaphores. Data moves between devices by JAX's collectives and lax.ppermute only.
A program may use at most 320 MiB of HBM per device.

```python
import jax
import jax.numpy as jnp
from jax import lax

D = 768
HEADS = 12
FF = 3072
LAYERS = 2
RADIUS = 3
WIN2 = 49
TSIDE = 16
PAGES = 8


def draw_page_side(key, part):
    pick_key = jax.random.fold_in(key, 11)
    force_key = jax.random.fold_in(key, 23)
    grid_len = 2 * TSIDE
    options = jnp.array([grid_len * 7 // 16, 3 * grid_len // 4, grid_len], jnp.int32)
    picks = jax.random.randint(pick_key, (PAGES,), 0, 3)
    side_values = options[picks]
    group_count = PAGES // 4
    forced = jax.random.randint(force_key, (group_count,), 0, 4)
    page_pos = jnp.arange(PAGES, dtype=jnp.int32)
    is_forced = page_pos % 4 == forced[page_pos // 4]
    return jnp.where(is_forced, grid_len, side_values).astype(jnp.int32)


def level_of(key, extent, cuts, low, top_value):
    gain = 1.0
    for axis_at, parts in cuts:
        draws = jax.random.uniform(jax.random.fold_in(jax.random.fold_in(key, 6), axis_at), (parts,), jnp.float32, low / len(cuts), top_value / len(cuts))
        gain = gain * jnp.repeat(jnp.exp(draws), extent[axis_at] // parts).reshape((-1,) + (1,) * (len(extent) - 1 - axis_at))
    return gain


def scatter_about(key, dims, deviation, limit, pieces=(), kind=jnp.bfloat16):
    drawn = jax.random.normal(key, dims, jnp.float32) * deviation
    if len(pieces) > 0:
        drawn = level_of(key, dims, pieces, -0.22, 0.18) * drawn
    return jnp.clip(drawn, min=-limit, max=limit).astype(kind)


def setup_inputs(seed: int = 0) -> dict:
    splits = jax.random.split(jax.random.key(seed), 15)
    return {
        "patch_in": scatter_about(splits[0], (PAGES, 4, TSIDE, TSIDE, D), 1.0, 6.0, ((0, 8), (1, 4))),
        "cls_in": scatter_about(splits[1], (PAGES, D), 1.0, 6.0, ((0, 8),)),
        "page_side": draw_page_side(jax.random.fold_in(splits[14], 71), 0),
        "norm_attn": jnp.clip(1.0 + 0.15 * jax.random.normal(splits[3], (LAYERS, D), jnp.float32), 0.25, 1.75),
        "qkv_weight": scatter_about(splits[4], (LAYERS, D, 3 * D), D ** -0.5, 0.21875),
        "rel_table": scatter_about(splits[5], (LAYERS, HEADS, WIN2), 1.0, 4.0, (), jnp.float32),
        "out_weight": scatter_about(splits[6], (LAYERS, D, D), (D // 4) ** -0.5, 0.4375),
        "scale_attn": jnp.clip(jax.random.uniform(splits[7], (LAYERS, D), jnp.float32, 0.5, 1.5), 0.5, 1.5),
        "norm_mlp": jnp.clip(1.0 + 0.15 * jax.random.normal(splits[8], (LAYERS, D), jnp.float32), 0.25, 1.75),
        "up_weight": scatter_about(splits[9], (LAYERS, D, FF), D ** -0.5, 0.21875),
        "down_weight": scatter_about(splits[10], (LAYERS, FF, D), FF ** -0.5, 0.109375),
        "scale_mlp": jnp.clip(jax.random.uniform(splits[11], (LAYERS, D), jnp.float32, 0.5, 1.5), 0.5, 1.5),
        "patch_cot": scatter_about(splits[12], (PAGES, 4, TSIDE, TSIDE, D), 1.0, 6.0, ((0, 8), (1, 4))),
        "cls_cot": scatter_about(splits[13], (PAGES, D), 1.0, 6.0, ((0, 8),)),
    }


epsilon = 1e-06
masked_score = -1e+30
highest = lax.Precision.HIGHEST

@jax.custom_vjp
def low(v):
    return lax.optimization_barrier(v.astype(jnp.bfloat16)).astype(jnp.float32)

@jax.custom_vjp
def low_back(v):
    return v

def low_keep(v):
    return (low(v), None)

def low_pass(kept, grad):
    return (grad,)

def back_keep(v):
    return (v, None)

def back_low(kept, grad):
    return (low(grad),)
low.defvjp(low_keep, low_pass)
low_back.defvjp(back_keep, back_low)

def matmul_high(left_matrix, right_matrix):
    return jnp.dot(left_matrix, right_matrix, precision=highest, preferred_element_type=jnp.float32)

def layer_norm(values, gain_row):
    centre = lax.optimization_barrier(jnp.mean(values, axis=-1, keepdims=True))
    centred = values - centre
    spread = lax.optimization_barrier(jnp.mean(centred * centred, axis=-1, keepdims=True))
    return centred * lax.rsqrt(spread + epsilon) * gain_row

def page_layer(weight_set, page_grid, cls_row, side_value):
    norm_a, qkv_w, bias_table, out_w, scale_a, norm_m, up_w, down_w, scale_m = weight_set
    grid_len = page_grid.shape[0]
    model_width = page_grid.shape[-1]
    head_count = bias_table.shape[0]
    head_dim = model_width // head_count
    score_scale = head_dim ** (-0.5)
    window_span = 2 * RADIUS + 1
    cell_count = grid_len * grid_len
    residual = jnp.concatenate([page_grid.reshape(cell_count, model_width), cls_row[None]], axis=0)
    normed = low(layer_norm(residual, norm_a))
    qkv_rows = low_back(low(matmul_high(normed, qkv_w)))

    def heads_of(block_rows):
        return block_rows.reshape(block_rows.shape[0], head_count, head_dim)
    grid_shape = (grid_len, grid_len, head_count, head_dim)
    query_grid = heads_of(qkv_rows[:cell_count, :model_width]).reshape(grid_shape)
    key_grid = heads_of(qkv_rows[:cell_count, model_width:2 * model_width]).reshape(grid_shape)
    value_grid = heads_of(qkv_rows[:cell_count, 2 * model_width:]).reshape(grid_shape)
    cls_q = heads_of(qkv_rows[cell_count:, :model_width])[0]
    cls_k = heads_of(qkv_rows[cell_count:, model_width:2 * model_width])[0]
    cls_v = heads_of(qkv_rows[cell_count:, 2 * model_width:])[0]
    inside = jnp.arange(grid_len, dtype=jnp.int32) < side_value
    valid_cells = inside[:, None] & inside[None, :]
    pad_spec = ((RADIUS, RADIUS), (RADIUS, RADIUS), (0, 0), (0, 0))
    keys_pad = jnp.pad(key_grid, pad_spec)
    values_pad = jnp.pad(value_grid, pad_spec)
    valid_pad = jnp.pad(valid_cells, RADIUS)
    score_list = []
    for row_off in range(window_span):
        for col_off in range(window_span):
            keys_here = keys_pad[row_off:row_off + grid_len, col_off:col_off + grid_len]
            here_ok = valid_pad[row_off:row_off + grid_len, col_off:col_off + grid_len]
            score_here = score_scale * lax.optimization_barrier(jnp.sum(query_grid * keys_here, axis=-1)) + bias_table[:, row_off * window_span + col_off]
            score_list.append(jnp.where(here_ok[..., None], score_here, masked_score))
    score_list.append(score_scale * lax.optimization_barrier(jnp.sum(query_grid * cls_k, axis=-1)))
    stacked = jnp.stack(score_list)
    top_score = lax.optimization_barrier(jnp.max(stacked, axis=0))
    exponent = jnp.exp(stacked - top_score)
    soft_weights = exponent / lax.optimization_barrier(jnp.sum(exponent, axis=0))
    attended = soft_weights[-1][..., None] * cls_v
    offset_index = 0
    for row_off in range(window_span):
        for col_off in range(window_span):
            values_here = values_pad[row_off:row_off + grid_len, col_off:col_off + grid_len]
            attended = attended + soft_weights[offset_index][..., None] * values_here
            offset_index += 1
    cell_scores = jnp.where(valid_cells[..., None], score_scale * lax.optimization_barrier(jnp.sum(key_grid * cls_q, axis=-1)), masked_score)
    self_score = score_scale * lax.optimization_barrier(jnp.sum(cls_q * cls_k, axis=-1))
    all_scores = jnp.concatenate([cell_scores.reshape(cell_count, head_count), self_score[None]], axis=0)
    cls_top = lax.optimization_barrier(jnp.max(all_scores, axis=0))
    cls_exp = jnp.exp(all_scores - cls_top)
    cls_weights = cls_exp / lax.optimization_barrier(jnp.sum(cls_exp, axis=0))
    cls_attended = jnp.einsum('nh,nhd->hd', cls_weights[:-1], value_grid.reshape(cell_count, head_count, head_dim), precision=highest) + cls_weights[-1][:, None] * cls_v
    att_rows = low(jnp.concatenate([attended.reshape(cell_count, model_width), cls_attended.reshape(1, model_width)], axis=0))
    branch = low_back(matmul_high(att_rows, out_w))
    middle = residual + scale_a * branch
    normed_mlp = low(layer_norm(middle, norm_m))
    up_value = low_back(matmul_high(normed_mlp, up_w))
    activation = low(jax.nn.gelu(up_value))
    down_value = low_back(matmul_high(activation, down_w))
    result = middle + scale_m * down_value
    return (result[:cell_count].reshape(grid_len, grid_len, model_width), result[cell_count])

def one_page(weight_set, tile_block, cls_row, side_value):
    tile_len = tile_block.shape[1]
    grid_len = 2 * tile_len
    model_width = tile_block.shape[-1]
    page_grid = tile_block.reshape(2, 2, tile_len, tile_len, model_width).transpose(0, 2, 1, 3, 4).reshape(grid_len, grid_len, model_width)
    for layer_index in range(LAYERS):
        layer_set = tuple((stacked[layer_index] for stacked in weight_set))
        page_grid, cls_row = page_layer(layer_set, page_grid, cls_row, side_value)
    inside = jnp.arange(grid_len, dtype=jnp.int32) < side_value
    valid_cells = inside[:, None] & inside[None, :]
    page_grid = jnp.where(valid_cells[..., None], page_grid, 0.0)
    tile_out = page_grid.reshape(2, tile_len, 2, tile_len, model_width).transpose(0, 2, 1, 3, 4).reshape(4, tile_len, tile_len, model_width)
    return (tile_out, cls_row)

def reference(patch_in, cls_in, page_side, norm_attn, qkv_weight, rel_table, out_weight, scale_attn, norm_mlp, up_weight, down_weight, scale_mlp, patch_cot, cls_cot):
    weight_set = tuple((item.astype(jnp.float32) for item in (norm_attn, qkv_weight, rel_table, out_weight, scale_attn, norm_mlp, up_weight, down_weight, scale_mlp)))

    def forward(weight_vals, patch_vals, cls_vals):
        page_fn = jax.checkpoint(one_page)

        def page_step(scan_carry, page_item):
            tile_block, cls_row, side_value = page_item
            return (scan_carry, page_fn(weight_vals, tile_block, cls_row, side_value))
        _, page_outputs = lax.scan(page_step, jnp.float32(0.0), (patch_vals, cls_vals, page_side))
        return page_outputs
    (patch_out, cls_out), pullback = jax.vjp(forward, weight_set, patch_in.astype(jnp.float32), cls_in.astype(jnp.float32))
    grad_weights, patch_grad, cls_grad = pullback((patch_cot.astype(jnp.float32), cls_cot.astype(jnp.float32)))
    return (patch_out.astype(jnp.bfloat16), cls_out.astype(jnp.bfloat16), patch_grad, cls_grad, grad_weights[0], grad_weights[1], grad_weights[2], grad_weights[3], grad_weights[4], grad_weights[5], grad_weights[6], grad_weights[7], grad_weights[8])
```

```python
import functools

import jax
import jax.numpy as jnp
import numpy as np
from jax import lax
from jax.experimental import pallas as pl
from jax.experimental.pallas import tpu as pltpu
from jax.sharding import PartitionSpec as P

RADIUS = 3
SPAN = 2 * RADIUS + 1
PAD = 8
EPS = 1e-06
MASKED = -1e30
BF = jnp.bfloat16
F32 = jnp.float32
MIB = 1 << 20


def dot(a, b):
    return lax.dot_general(a, b, (((1,), (0,)), ((), ())), preferred_element_type=F32)


def dot_nt(a, b):
    return lax.dot_general(a, b, (((1,), (1,)), ((), ())), preferred_element_type=F32)


def dot_tn(a, b):
    return lax.dot_general(a, b, (((0,), (0,)), ((), ())), preferred_element_type=F32)


def normalized(x):
    centred = x - jnp.mean(x, axis=-1, keepdims=True)
    inverse = lax.rsqrt(jnp.mean(centred * centred, axis=-1, keepdims=True) + EPS)
    return centred * inverse, inverse


def norm_back(x, gain, d_out):
    unit, inverse = normalized(x)
    d_unit = d_out * gain
    d_x = inverse * (
        d_unit
        - jnp.mean(d_unit, axis=-1, keepdims=True)
        - unit * jnp.mean(d_unit * unit, axis=-1, keepdims=True)
    )
    return d_x, d_out * unit


def split3(x):
    high = x.astype(BF).astype(F32)
    rest = x - high
    middle = rest.astype(BF).astype(F32)
    return high, middle, rest - middle


def lane_heads(rows, lanes, width):
    return lax.broadcasted_iota(jnp.int32, (rows, lanes), 1) // width


def head_rows(rows, lanes, width):
    return lane_heads(rows, lanes, width) == lax.broadcasted_iota(jnp.int32, (rows, lanes), 0)


def stacked_heads(block, width):
    rows, lanes = block.shape
    heads = lane_heads(rows, lanes, width)
    zero = jnp.zeros_like(block)
    return jnp.concatenate(
        [jnp.where(heads == h, block, zero) for h in range(lanes // width)], axis=0
    )


def folded_heads(stack, width):
    count = stack.shape[1] // width
    rows = stack.shape[0] // count
    heads = lane_heads(rows, stack.shape[1], width)
    out = stack[:rows]
    for h in range(1, count):
        out = jnp.where(heads == h, stack[h * rows : (h + 1) * rows], out)
    return out


def keep_rows(rows, cells, class_weight):
    row = lax.broadcasted_iota(jnp.int32, (rows, 1), 0)
    return jnp.where(row < cells, 1.0, jnp.where(row == cells, class_weight, 0.0))


class Sizes:
    def __init__(self, side, width, hidden, heads, devices):
        self.side = side
        self.cells = side * side
        self.rows = self.cells + 16
        self.width = width
        self.hidden = hidden
        self.heads = heads
        self.head = width // heads
        self.pitch = side + PAD
        self.ext = side + 2 * RADIUS
        self.ext_rows = self.pitch * self.ext + PAD
        self.brows = 4
        self.blocks = side // self.brows
        self.bq = self.brows * side
        self.bk = 256
        self.class_slot = self.bk - PAD
        self.quad = 4 * self.head
        self.groups = width // self.quad
        self.devices = devices
        self.bits = devices.bit_length() - 1


def stat_rows(values):
    width = values[0].shape[1]
    parts = [split3(v) for v in values]
    flat = [p[k] for k in range(3) for p in parts]
    if len(flat) % 2:
        flat.append(jnp.zeros_like(flat[0]))
    row = lax.broadcasted_iota(jnp.int32, (16, 2 * width), 0)
    out = jnp.zeros((16, 2 * width), F32)
    for i in range(0, len(flat), 2):
        out = jnp.where(row == i // 2, jnp.concatenate(flat[i : i + 2], axis=1), out)
    return out.astype(BF)


def read_stats(block, count, width):
    rows = block.astype(F32)

    def piece(i):
        return rows[i // 2 : i // 2 + 1, (i % 2) * width : (i % 2 + 1) * width]

    return [piece(i) + piece(count + i) + piece(2 * count + i) for i in range(count)]


def in_tile_order(info, pieces):
    me = info[0] * 2 + info[1]
    out = []
    for t in range(4):
        d = me ^ t
        out.append(
            [
                jnp.where(d == 0, a, jnp.where(d == 1, b, jnp.where(d == 2, c, e)))
                for a, b, c, e in zip(*pieces)
            ]
        )
    return out


def class_scores(sz, info, qkv_ref, mask):
    cells, width = sz.cells, sz.width
    own = head_rows(16, width, sz.head)
    class_rows = qkv_ref[cells : cells + 16, :].astype(F32)
    q_c, k_c, v_c = (class_rows[0:1, i * width : (i + 1) * width] for i in range(3))
    q_heads = jnp.where(own, q_c, 0.0)
    scale = sz.head ** (-0.5)
    scores = dot_nt(q_heads.astype(BF), qkv_ref[0:cells, width : 2 * width]) * scale + mask
    self_score = jnp.sum(q_heads * k_c, axis=1, keepdims=True) * scale
    self_score = jnp.where(info[2] == 1, self_score, MASKED)
    return own, q_heads, k_c, v_c, scores, self_score


def write_left(sz, perm_ref, value, mine_ref, send_ref):
    turned = dot_nt(perm_ref[...], value).astype(BF)
    half = turned.shape[0] // 2
    mine_ref[...] = turned[:half]
    send_ref[...] = turned[half:]


def send_rims(sz, info, kv_half, kv_edge_rows, stats, pc_ref, pr_ref, pd_ref):
    side, width = sz.side, sz.width
    cells8 = [kv_half(r) for r in range(side)]
    pc_ref[0 : side * PAD, :] = jnp.concatenate(cells8, axis=0).astype(BF)
    pc_ref[side * PAD : side * PAD + 16, :] = stats
    edge, corner = kv_edge_rows()
    pr_ref[0 : RADIUS * side, :] = jnp.concatenate(edge, axis=0).astype(BF)
    pr_ref[RADIUS * side : RADIUS * side + 16, :] = stats
    zero = jnp.zeros((PAD, 2 * width), F32)
    pd_ref[0 : (RADIUS + 1) * PAD, :] = jnp.concatenate(corner + [zero], axis=0).astype(BF)
    pd_ref[(RADIUS + 1) * PAD : (RADIUS + 1) * PAD + 16, :] = stats


def qkv_kernel(sz, layer, info, x_ref, gain_ref, w_ref, perm_ref, mask_ref,
               h_ref, lm_ref, ls_ref, qkv_ref, pc_ref, pr_ref, pd_ref):
    step = pl.program_id(0)
    width, side, cells = sz.width, sz.side, sz.cells

    @pl.when(step == 0)
    def _():
        unit, _ = normalized(x_ref[...])
        h = (unit * gain_ref[layer : layer + 1, :]).astype(BF)
        h_ref[...] = h
        write_left(sz, perm_ref, h, lm_ref, ls_ref)

    cols = pl.ds(pl.multiple_of(step * width, width), width)
    qkv_ref[:, cols] = dot(h_ref[...], w_ref[...]).astype(BF)

    @pl.when(step == pl.num_programs(0) - 1)
    def _():
        mask = mask_ref[0:1, :]
        own, q_heads, k_c, v_c, scores, self_score = class_scores(sz, info, qkv_ref, mask)
        top = jnp.maximum(jnp.max(scores, axis=1, keepdims=True), self_score)
        probs = jnp.where(mask > -1.0, jnp.exp(scores - top), 0.0)
        self_prob = jnp.where(info[2] == 1, jnp.exp(self_score - top), 0.0)
        total = jnp.sum(probs, axis=1, keepdims=True) + self_prob
        part = dot(probs.astype(BF), qkv_ref[0:cells, 2 * width :]) + self_prob * v_c

        def to_row(v):
            return jnp.sum(jnp.where(own, v, 0.0), axis=0, keepdims=True)

        stats = stat_rows([to_row(part), to_row(top), to_row(total)])
        left_col = info[1] == 0

        def half(r):
            row = qkv_ref[r * side : (r + 1) * side, width:].astype(F32)
            return jnp.where(left_col, row[PAD:], row[:PAD])

        def edges():
            first = pl.multiple_of((1 - info[0]) * (side - RADIUS) * side, 16)
            rows = qkv_ref[pl.ds(first, RADIUS * side), width:].astype(F32)
            edge = [rows[t * side : (t + 1) * side] for t in range(RADIUS)]
            return edge, [jnp.where(left_col, e[PAD:], e[:PAD]) for e in edge]

        send_rims(sz, info, half, edges, stats, pc_ref, pr_ref, pd_ref)


def rim_places(sz, info):
    return sz.pitch * (1 - info[1]), (sz.side + RADIUS) * (1 - info[0])


def attention_kernel(sz, layer, info, qkv_ref, st_ref, rc_ref, rr_ref, rd_ref, bias_ref, mask_ref,
                     x_ref, w_ref, scale_ref, gain_ref, perm_ref,
                     p_ref, kb_ref, vb_ref, stat_ref, br_ref, x1_ref, h2_ref,
                     am_ref, as_ref, bm_ref, bs_ref, kext, vext, att):
    width, side, cells, pitch = sz.width, sz.side, sz.cells, sz.pitch
    beside, above = rim_places(sz, info)
    for ext, lo in ((kext, width), (vext, 2 * width)):
        at = lo - width
        ext[...] = jnp.zeros_like(ext)
        for r in range(side):
            base = pitch * (r + RADIUS)
            ext[base + PAD : base + PAD + side, :] = qkv_ref[r * side : (r + 1) * side, lo : lo + width].astype(F32)
        sides = rc_ref[0 : side * PAD, at : at + width].astype(F32)
        for r in range(side):
            ext[pl.ds(pl.multiple_of(pitch * (r + RADIUS) + beside, 8), PAD), :] = sides[r * PAD : (r + 1) * PAD]
        edge = rr_ref[0 : RADIUS * side, at : at + width].astype(F32)
        corner = rd_ref[0 : (RADIUS + 1) * PAD, at : at + width].astype(F32)
        for t in range(RADIUS):
            base = pitch * (above + t)
            ext[pl.ds(pl.multiple_of(base + PAD, 8), side), :] = edge[t * side : (t + 1) * side]
            ext[pl.ds(pl.multiple_of(base + beside, 8), PAD), :] = corner[t * PAD : (t + 1) * PAD]
    class_rows = qkv_ref[cells : cells + 16, :].astype(F32)[0:PAD]
    scale = sz.head ** (-0.5)
    for b in range(sz.blocks):
        first = b * sz.brows * pitch
        kb = jnp.concatenate([kext[first : first + sz.class_slot, :], class_rows[:, width : 2 * width]], axis=0).astype(BF)
        vb = jnp.concatenate([vext[first : first + sz.class_slot, :], class_rows[:, 2 * width :]], axis=0).astype(BF)
        kb_ref[b] = kb
        vb_ref[b] = vb
        q = qkv_ref[b * sz.bq : (b + 1) * sz.bq, 0:width] * jnp.asarray(scale, BF)
        mask = mask_ref[b]
        mask = jnp.concatenate([mask, mask], axis=1)
        for g in range(sz.groups):
            lanes = slice(g * sz.quad, (g + 1) * sz.quad)
            scores = dot_nt(kb[:, lanes], stacked_heads(q[:, lanes], sz.head)) + bias_ref[g] + mask
            top = jnp.max(scores, axis=0, keepdims=True)
            probs = jnp.exp(scores - top)
            total = jnp.sum(probs, axis=0, keepdims=True)
            probs = (probs * (1.0 / total)).astype(BF)
            p_ref[b * sz.groups + g] = probs
            out = folded_heads(dot_tn(probs, vb[:, lanes]), sz.head)
            att[b * sz.bq : (b + 1) * sz.bq, lanes] = out.astype(BF)
    own_stats = [read_stats(r, 3, width) for r in (
        st_ref[...],
        rc_ref[side * PAD : side * PAD + 16, :],
        rr_ref[RADIUS * side : RADIUS * side + 16, :],
        rd_ref[(RADIUS + 1) * PAD : (RADIUS + 1) * PAD + 16, :],
    )]
    ordered = in_tile_order(info, own_stats)
    top = functools.reduce(jnp.maximum, [s[1] for s in ordered])
    total = jnp.zeros_like(top)
    summed = jnp.zeros_like(top)
    for part, part_top, part_total in ordered:
        factor = jnp.exp(part_top - top)
        total = total + part_total * factor
        summed = summed + part * factor
    class_out = summed / total
    stat_ref[...] = jnp.zeros_like(stat_ref)
    stat_ref[0:1, :] = top
    stat_ref[1:2, :] = total
    stat_ref[2:3, :] = class_out
    row = lax.broadcasted_iota(jnp.int32, (16, width), 0)
    att[cells : cells + 16, :] = jnp.where(row == 0, class_out, 0.0).astype(BF)
    branch = dot(att[...], w_ref[...])
    br_ref[...] = branch
    x1 = x_ref[...] + scale_ref[layer : layer + 1, :] * branch
    x1_ref[...] = x1
    unit, _ = normalized(x1)
    h2 = (unit * gain_ref[layer : layer + 1, :]).astype(BF)
    h2_ref[...] = h2
    write_left(sz, perm_ref, att[...], am_ref, as_ref)
    write_left(sz, perm_ref, h2, bm_ref, bs_ref)


GELU_C = float(np.sqrt(2.0 / np.pi))


def mlp_kernel(sz, layer, info, h2_ref, up_w_ref, down_w_ref, x1_ref, scale_ref, perm_ref,
               up_ref, down_ref, x2_ref, lm_ref, ls_ref):
    step = pl.program_id(0)
    up = dot(h2_ref[...], up_w_ref[...])
    up_ref[...] = up
    act = (0.5 * up * (1.0 + jnp.tanh(GELU_C * (up + 0.044715 * (up * up * up))))).astype(BF)
    part = dot(act, down_w_ref[...])

    @pl.when(step == 0)
    def _():
        down_ref[...] = part

    @pl.when(step > 0)
    def _():
        down_ref[...] += part

    write_left(sz, perm_ref, act, lm_ref, ls_ref)

    @pl.when(step == pl.num_programs(0) - 1)
    def _():
        x2_ref[...] = x1_ref[...] + scale_ref[layer : layer + 1, :] * down_ref[...]


def mlp_back_kernel(sz, layer, info, g_ref, down_ref, scale_m_ref, up_ref, down_w_ref, up_w_ref,
                    x1_ref, gain_ref, scale_a_ref, br_ref,
                    ed_ref, eu_ref, g1_ref, eb_ref, vec_ref, d_h2):
    step = pl.program_id(0)
    keep = keep_rows(sz.rows, sz.cells, jnp.where(info[2] == 1, 1.0, 0.0))

    @pl.when(step == 0)
    def _():
        g = g_ref[...]
        ed_ref[...] = (scale_m_ref[layer : layer + 1, :] * g).astype(BF)
        vec_ref[...] = jnp.zeros_like(vec_ref)
        vec_ref[0:1, :] = jnp.sum(keep * g * down_ref[...], axis=0, keepdims=True)
        d_h2[...] = jnp.zeros_like(d_h2)

    d_act = dot_nt(ed_ref[...], down_w_ref[...])
    u = up_ref[...]
    square = u * u
    th = jnp.tanh(GELU_C * (u + 0.044715 * (square * u)))
    slope = 0.5 * (1.0 + th) + 0.5 * u * (1.0 - th * th) * (GELU_C * (1.0 + (3 * 0.044715) * square))
    e_up = (d_act * slope).astype(BF)
    eu_ref[...] = e_up
    d_h2[...] += dot_nt(e_up, up_w_ref[...])

    @pl.when(step == pl.num_programs(0) - 1)
    def _():
        d_x1, gain_rows = norm_back(x1_ref[...], gain_ref[layer : layer + 1, :], d_h2[...])
        g1 = g_ref[...] + d_x1
        g1_ref[...] = g1
        eb_ref[...] = (scale_a_ref[layer : layer + 1, :] * g1).astype(BF)
        vec_ref[1:2, :] = jnp.sum(keep * gain_rows, axis=0, keepdims=True)
        vec_ref[2:3, :] = jnp.sum(keep * g1 * br_ref[...], axis=0, keepdims=True)


def attention_back_kernel(sz, layer, info, eb_ref, w_ref, qkv_ref, p_ref, kb_ref, vb_ref, stat_ref, own_mask_ref,
                          dq_ref, dkv_ref, pc_ref, pr_ref, pd_ref, tab_ref, kext, vext, d_o, tab):
    width, side, cells, pitch = sz.width, sz.side, sz.cells, sz.pitch
    scale = sz.head ** (-0.5)
    d_o[...] = dot_nt(eb_ref[...], w_ref[...])
    kext[...] = jnp.zeros_like(kext)
    vext[...] = jnp.zeros_like(vext)
    class_k = [jnp.zeros((PAD, sz.quad), F32) for _ in range(sz.groups)]
    class_v = [jnp.zeros((PAD, sz.quad), F32) for _ in range(sz.groups)]
    for b in range(sz.blocks):
        first = b * sz.brows * pitch
        q = qkv_ref[b * sz.bq : (b + 1) * sz.bq, 0:width] * jnp.asarray(scale, BF)
        do = d_o[b * sz.bq : (b + 1) * sz.bq, :].astype(BF)
        for g in range(sz.groups):
            lanes = slice(g * sz.quad, (g + 1) * sz.quad)
            do_stack = stacked_heads(do[:, lanes], sz.head)
            q_stack = stacked_heads(q[:, lanes], sz.head)
            probs = p_ref[b * sz.groups + g]
            wide = probs.astype(F32)
            d_prob = dot_nt(vb_ref[b, :, lanes], do_stack)
            delta = jnp.sum(wide * d_prob, axis=0, keepdims=True)
            d_score = wide * (d_prob - delta)
            if b == 0:
                tab[g] = d_score
            else:
                tab[g] += d_score
            low = d_score.astype(BF)
            d_v = dot(probs, do_stack)
            d_k = dot(low, q_stack)
            vext[first : first + sz.class_slot, lanes] += d_v[: sz.class_slot]
            kext[first : first + sz.class_slot, lanes] += d_k[: sz.class_slot]
            class_v[g] = class_v[g] + d_v[sz.class_slot :]
            class_k[g] = class_k[g] + d_k[sz.class_slot :]
            d_q = folded_heads(dot_tn(low, kb_ref[b, :, lanes]), sz.head) * scale
            dq_ref[b * sz.bq : (b + 1) * sz.bq, lanes] = d_q.astype(BF)
    mask = own_mask_ref[0:1, :]
    own, q_heads, k_c, v_c, scores, self_score = class_scores(sz, info, qkv_ref, mask)
    top = jnp.max(jnp.where(own, stat_ref[0:1, :], MASKED), axis=1, keepdims=True)
    total = jnp.max(jnp.where(own, stat_ref[1:2, :], 0.0), axis=1, keepdims=True)
    real = lax.broadcasted_iota(jnp.int32, (16, 1), 0) < sz.heads
    probs = jnp.where((mask > -1.0) & real, jnp.exp(scores - top) / total, 0.0)
    self_prob = jnp.where((info[2] == 1) & real, jnp.exp(self_score - top) / total, 0.0)
    d_class = jnp.where(own, d_o[cells : cells + 1, :], 0.0)
    delta = jnp.sum(d_class * stat_ref[2:3, :], axis=1, keepdims=True)
    d_low = d_class.astype(BF)
    d_cell = probs * (dot_nt(d_low, qkv_ref[0:cells, 2 * width :]) - delta)
    d_cell_low = d_cell.astype(BF)
    d_self = self_prob * (jnp.sum(d_class * v_c, axis=1, keepdims=True) - delta)

    def to_row(v):
        return jnp.sum(jnp.where(own, v, 0.0), axis=0, keepdims=True)

    g_q = to_row(dot(d_cell_low, qkv_ref[0:cells, width : 2 * width]) + d_self * k_c) * scale
    g_k = to_row(d_self * q_heads) * scale + jnp.concatenate([c[0:1] for c in class_k], axis=1)
    g_v = to_row(self_prob * d_class) + jnp.concatenate([c[0:1] for c in class_v], axis=1)
    add_k = dot_tn(d_cell_low, q_heads.astype(BF)) * scale
    add_v = dot_tn(probs.astype(BF), d_low)
    beside, above = rim_places(sz, info)
    for r in range(side):
        base = pitch * (r + RADIUS) + PAD
        rows = slice(r * side, (r + 1) * side)
        dkv_ref[rows, 0:width] = kext[base : base + side, :] + add_k[rows]
        dkv_ref[rows, width:] = vext[base : base + side, :] + add_v[rows]

    def pair(at, count):
        at = pl.ds(pl.multiple_of(at, 8), count)
        return jnp.concatenate([kext[at, :], vext[at, :]], axis=1)

    def edges():
        return (
            [pair(pitch * (above + t) + PAD, side) for t in range(RADIUS)],
            [pair(pitch * (above + t) + beside, PAD) for t in range(RADIUS)],
        )

    send_rims(sz, info, lambda r: pair(pitch * (r + RADIUS) + beside, PAD), edges,
              stat_rows([g_q, g_k, g_v]), pc_ref, pr_ref, pd_ref)
    per_head = sz.bq
    for g in range(sz.groups):
        turned = tab[g].T
        for h in range(4):
            total_h = jnp.zeros((side, sz.bk), F32)
            for r in range(sz.brows):
                at = h * per_head + r * side
                piece = turned[at : at + side]
                shift = (sz.bk - pitch * r) % sz.bk
                total_h = total_h + (pltpu.roll(piece, shift, 1) if shift else piece)
            tab_row = jnp.zeros((1, sz.bk), F32)
            for c in range(side):
                one = total_h[c : c + 1]
                tab_row = tab_row + (pltpu.roll(one, sz.bk - c, 1) if c else one)
            tab_ref[4 * g + h : 4 * g + h + 1, :] = tab_row
    tab_ref[sz.heads : 16, :] = jnp.zeros((16 - sz.heads, sz.bk), F32)


def qkv_back_kernel(sz, layer, info, dq_ref, dkv_ref, st_ref, rc_ref, rr_ref, rd_ref, w_ref, x_ref, gain_ref, g1_ref,
                    eq_ref, g_ref, vec_ref, dkv, d_h):
    step = pl.program_id(0)
    width, side, cells = sz.width, sz.side, sz.cells

    @pl.when(step == 0)
    def _():
        dkv[...] = dkv_ref[...]
        beside = PAD * (1 - info[1])
        edge = (1 - info[0]) * (side - RADIUS) * side
        sides = rc_ref[0 : side * PAD, :].astype(F32)
        for r in range(side):
            dkv[pl.ds(pl.multiple_of(r * side + beside, 8), PAD), :] += sides[r * PAD : (r + 1) * PAD]
        dkv[pl.ds(pl.multiple_of(edge, 8), RADIUS * side), :] += rr_ref[0 : RADIUS * side, :].astype(F32)
        corner = rd_ref[0 : (RADIUS + 1) * PAD, :].astype(F32)
        for t in range(RADIUS):
            dkv[pl.ds(pl.multiple_of(edge + t * side + beside, 8), PAD), :] += corner[t * PAD : (t + 1) * PAD]
        pieces = [read_stats(r, 3, width) for r in (
            st_ref[...],
            rc_ref[side * PAD : side * PAD + 16, :],
            rr_ref[RADIUS * side : RADIUS * side + 16, :],
            rd_ref[(RADIUS + 1) * PAD : (RADIUS + 1) * PAD + 16, :],
        )]
        ordered = in_tile_order(info, pieces)
        class_row = jnp.concatenate(
            [functools.reduce(lambda a, b: a + b, [o[i] for o in ordered]) for i in range(3)], axis=1
        )
        row = lax.broadcasted_iota(jnp.int32, (16, 3 * width), 0)
        eq_ref[0:cells, 0:width] = dq_ref[...]
        eq_ref[0:cells, width:] = dkv[...].astype(BF)
        eq_ref[cells : cells + 16, :] = jnp.where(row == 0, class_row, 0.0).astype(BF)
        d_h[...] = jnp.zeros_like(d_h)

    cols = pl.ds(pl.multiple_of(step * width, width), width)
    d_h[...] += dot_nt(eq_ref[:, cols], w_ref[...])

    @pl.when(step == pl.num_programs(0) - 1)
    def _():
        keep = keep_rows(sz.rows, sz.cells, jnp.where(info[2] == 1, 1.0, 0.0))
        d_x, gain_rows = norm_back(x_ref[...], gain_ref[layer : layer + 1, :], d_h[...])
        g_ref[...] = g1_ref[...] + d_x
        vec_ref[...] = jnp.zeros_like(vec_ref)
        vec_ref[0:1, :] = jnp.sum(keep * gain_rows, axis=0, keepdims=True)


def product(sz, info, mine_ref, got_ref, own_ref, other_ref):
    row = lax.broadcasted_iota(jnp.int32, own_ref.shape, 0)
    own = own_ref[...]
    own = jnp.where((row < sz.cells) | (info[0] == 0), own, jnp.zeros_like(own))
    return (
        dot(mine_ref[...], own) + dot(got_ref[:, 0 : sz.cells], other_ref[0 : sz.cells, :])
    ).astype(BF)


def store_halves(value, outer, send_ref, keep_ref):
    n = value.shape[0] // 4
    if outer:
        keep_ref[...] = value[: 2 * n]
        send_ref[...] = value[2 * n :]
    else:
        keep_ref[0:n] = value[0:n]
        send_ref[0:n] = value[n : 2 * n]
        keep_ref[n : 2 * n] = value[2 * n : 3 * n]
        send_ref[n : 2 * n] = value[3 * n :]


def grad_kernel(sz, outer, info, mine_ref, got_ref, own_ref, other_ref, send_ref, keep_ref):
    store_halves(product(sz, info, mine_ref, got_ref, own_ref, other_ref), outer, send_ref, keep_ref)


def grad_attn_kernel(sz, info, hm, hg, qo, qg, am, ag, bo, bg, s0, k0, s1, k1):
    step = pl.program_id(0)

    @pl.when(step < 2)
    def _():
        store_halves(product(sz, info, hm, hg, qo, qg), True, s0, k0)

    @pl.when(step == 2)
    def _():
        store_halves(product(sz, info, hm, hg, qo, qg), False, s1, k1)

    @pl.when(step == 3)
    def _():
        store_halves(product(sz, info, am, ag, bo, bg), False, s1, k1)


def bias_kernel(sz, table_ref, out_ref, wide):
    slot = lax.broadcasted_iota(jnp.int32, (sz.side, sz.bk), 1)
    for g in range(sz.groups):
        for h in range(4):
            line = jnp.broadcast_to(table_ref[4 * g + h : 4 * g + h + 1, :], (sz.side, sz.bk))
            line = pltpu.roll(line, 0, 1, stride=1, stride_axis=0)
            for r in range(sz.brows):
                piece = pltpu.roll(line, sz.pitch * r, 1) if r else line
                at = h * sz.bq + r * sz.side
                wide[at : at + sz.side, :] = jnp.where(slot == sz.class_slot, 0.0, piece)
        out_ref[g] = wide[...].T


def shape(dims, dtype):
    return jax.ShapeDtypeStruct(dims, dtype)


def whole(dims):
    return pl.BlockSpec(dims, lambda *_: (0,) * len(dims))


SCALARS = pl.BlockSpec(memory_space=pltpu.SMEM)


def local(patch_in, cls_in, page_side, norm_attn, qkv_weight, rel_table, out_weight, scale_attn,
          norm_mlp, up_weight, down_weight, scale_mlp, patch_cot, cls_cot):
    tiles = lax.axis_size("tile")
    pages = lax.axis_size("dp")
    layers, heads = rel_table.shape[:2]
    sz = Sizes(patch_in.shape[2], patch_in.shape[4], up_weight.shape[2], heads, tiles * pages)
    side, cells, rows, width, hidden = sz.side, sz.cells, sz.rows, sz.width, sz.hidden
    chunks = hidden // width
    tile = lax.axis_index("tile")
    me = lax.axis_index("dp") * tiles + tile
    tile_row, tile_col = tile // 2, tile % 2
    page = page_side[0]

    chunk_bits = chunks.bit_length() - 1
    low_bits = sz.bits - chunk_bits
    info = jnp.stack([tile_row, tile_col, (tile == 0).astype(jnp.int32), me >> low_bits]).astype(jnp.int32)

    def permutation(bits, low):
        per = width >> bits
        order = np.array([int(format(p, f"0{bits}b")[::-1], 2) for p in range(1 << bits)])
        source = (jnp.asarray(np.repeat(order, per)) ^ low) * per + jnp.asarray(np.tile(np.arange(per), 1 << bits))
        return (source[:, None] == jnp.arange(width)[None]).astype(BF)

    perm = permutation(sz.bits, me)
    perm_ff = permutation(low_bits, me & ((1 << low_bits) - 1))

    cell = np.arange(cells)
    own_ok = (tile_row * side + cell // side < page) & (tile_col * side + cell % side < page)
    own_mask = jnp.broadcast_to(jnp.where(own_ok, 0.0, MASKED).astype(F32), (8, cells))
    slot = np.arange(sz.bk)[None] + np.arange(sz.blocks)[:, None] * sz.brows * sz.pitch - PAD + RADIUS
    key_row = tile_row * side + slot // sz.pitch - RADIUS
    key_col = tile_col * side + slot % sz.pitch - RADIUS
    is_class = (np.arange(sz.bk) == sz.class_slot)[None]
    key_ok = (key_row >= 0) & (key_row < page) & (key_col >= 0) & (key_col < page) | is_class
    key_mask = jnp.broadcast_to(
        jnp.where(key_ok, 0.0, MASKED).astype(F32)[:, :, None], (sz.blocks, sz.bk, sz.bk // 2)
    )

    lines = jnp.pad(rel_table.reshape(layers, heads, SPAN, SPAN), ((0, 0), (0, 16 - heads), (0, 0), (0, sz.pitch - SPAN)),
                    constant_values=MASKED).reshape(layers, 16, SPAN * sz.pitch)
    first_slot = PAD - RADIUS
    lines = jnp.pad(lines, ((0, 0), (0, 0), (first_slot, sz.bk - first_slot - SPAN * sz.pitch)), constant_values=MASKED)

    def call(kernel, grid, in_specs, out_specs, out_shape, scratch=(), vmem=40, flops=0, nbytes=0, **kw):
        return pl.pallas_call(
            kernel,
            grid=grid,
            in_specs=in_specs,
            out_specs=out_specs,
            out_shape=out_shape,
            scratch_shapes=list(scratch),
            compiler_params=pltpu.CompilerParams(vmem_limit_bytes=vmem * MIB),
            cost_estimate=pl.CostEstimate(flops=flops, bytes_accessed=nbytes, transcendentals=0),
            **kw,
        )

    bias = call(
        functools.partial(bias_kernel, sz),
        (layers,),
        [pl.BlockSpec((None, 16, sz.bk), lambda l: (l, 0, 0))],
        pl.BlockSpec((None, sz.groups, sz.bk, sz.bk), lambda l: (l, 0, 0, 0)),
        shape((layers, sz.groups, sz.bk, sz.bk), F32),
        [pltpu.VMEM((sz.bk, sz.bk), F32)],
        nbytes=4 << 20,
    )(lines)

    pc_rows, pr_rows, pd_rows = side * PAD + 16, RADIUS * side + 16, (RADIUS + 1) * PAD + 16
    rim_shapes = [shape((n, 2 * width), BF) for n in (pc_rows, pr_rows, pd_rows)]
    rim_specs = [whole(s.shape) for s in rim_shapes]
    half = width // 2
    left_shape = shape((half, rows), BF)
    left_spec = whole((half, rows))
    row_w = whole((rows, width))
    par = whole((layers, width))

    def partner(value, x):
        return lax.ppermute(value, "tile", [(t, t ^ x) for t in range(tiles)])

    def exchange(rims):
        return [partner(v, x + 1) for x, v in enumerate(rims)]

    def layer_forward(l, x):
        third = pl.BlockSpec((None, width, width), lambda i: (l, 0, i))
        h, lm, ls, qkv, *rims = call(
            functools.partial(qkv_kernel, sz, l),
            (3,),
            [SCALARS, row_w, par, third, whole((width, width)), whole((8, cells))],
            [row_w, left_spec, left_spec, whole((rows, 3 * width))] + rim_specs,
            [shape((rows, width), BF), left_shape, left_shape, shape((rows, 3 * width), BF)] + rim_shapes,
            flops=2 * rows * width * width * 4, nbytes=8 << 20,
        )(info, x, norm_attn, qkv_weight, perm, own_mask)
        got = exchange(rims)
        stat_spec = pl.BlockSpec((16, 2 * width), lambda i: (side * PAD // 16, 0))
        nb, ng = sz.blocks, sz.groups
        p, kb, vb, stats, branch, x1, h2, am, as_, bm, bs = call(
            functools.partial(attention_kernel, sz, l),
            (1,),
            [SCALARS, whole((rows, 3 * width)), stat_spec] + rim_specs
            + [pl.BlockSpec((None, ng, sz.bk, sz.bk), lambda i: (l, 0, 0, 0)), whole(key_mask.shape), row_w,
               pl.BlockSpec((None, width, width), lambda i: (l, 0, 0)), par, par, whole((width, width))],
            [whole((nb * ng, sz.bk, sz.bk)), whole((nb, sz.bk, width)), whole((nb, sz.bk, width)), whole((8, width)),
             row_w, row_w, row_w, left_spec, left_spec, left_spec, left_spec],
            [shape((nb * ng, sz.bk, sz.bk), BF), shape((nb, sz.bk, width), BF), shape((nb, sz.bk, width), BF),
             shape((8, width), F32), shape((rows, width), F32), shape((rows, width), F32), shape((rows, width), BF)]
            + [left_shape] * 4,
            [pltpu.VMEM((sz.ext_rows, width), F32), pltpu.VMEM((sz.ext_rows, width), F32), pltpu.VMEM((rows, width), BF)],
            flops=3 << 30, nbytes=20 << 20,
        )(info, qkv, rims[0], *got, bias, key_mask, x, out_weight, scale_attn, norm_mlp, perm)
        up_spec = pl.BlockSpec((None, width, width), lambda i, s: (l, 0, i))
        down_spec = pl.BlockSpec((None, width, width), lambda i, s: (l, i, 0))
        hid_spec = pl.BlockSpec((rows, width), lambda i, s: (0, i))
        act_spec = pl.BlockSpec((None, half, rows), lambda i, s: (i ^ s[3], 0, 0))
        up, down, x2, cm, cs = pl.pallas_call(
            functools.partial(mlp_kernel, sz, l),
            grid_spec=pltpu.PrefetchScalarGridSpec(
                num_scalar_prefetch=1,
                grid=(chunks,),
                in_specs=[row_w, up_spec, down_spec, row_w, par, whole((width, width))],
                out_specs=[hid_spec, row_w, row_w, act_spec, act_spec],
            ),
            out_shape=[shape((rows, hidden), F32), shape((rows, width), F32), shape((rows, width), F32),
                       shape((chunks, half, rows), BF), shape((chunks, half, rows), BF)],
            compiler_params=pltpu.CompilerParams(vmem_limit_bytes=40 * MIB),
            cost_estimate=pl.CostEstimate(flops=2 * rows * width * hidden * 3, bytes_accessed=16 << 20, transcendentals=0),
        )(info, h2, up_weight, down_weight, x1, scale_mlp, perm_ff)
        lefts = [(m, partner(s, 1)) for m, s in ((lm, ls), (am, as_), (bm, bs), (cm, cs))]
        return x2, (x, qkv, p, kb, vb, stats, branch, x1, up, down, lefts)

    def grads(outer, left, right, other):
        mine, got = left
        wide_left = mine.ndim == 3
        lspec = (pl.BlockSpec((None, half, rows), lambda i: (i, 0, 0)) if wide_left else left_spec)
        rspec = row_w if wide_left else pl.BlockSpec((rows, width), lambda i: (0, i))
        out = pl.BlockSpec((None, half // 2, width), lambda i: (i, 0, 0))
        return call(
            functools.partial(grad_kernel, sz, outer),
            (chunks,),
            [SCALARS, lspec, lspec, rspec, rspec],
            [out, out],
            [shape((chunks, half // 2, width), BF)] * 2,
            flops=2 * half * width * hidden * 2, nbytes=10 << 20,
        )(info, mine, got, right, other)

    def grads_attn(h_left, a_left, e_qkv, q_other, e_branch, b_other):
        def block(index):
            return pl.BlockSpec((None, half // 2, width), lambda i: (index(i), 0, 0))

        first, second = block(lambda i: jnp.minimum(i, 1)), block(lambda i: jnp.maximum(i - 2, 0))
        qspec = pl.BlockSpec((rows, width), lambda i: (0, jnp.minimum(i, 2)))
        return call(
            functools.partial(grad_attn_kernel, sz),
            (4,),
            [SCALARS, left_spec, left_spec, qspec, qspec, left_spec, left_spec, row_w, row_w],
            [first, first, second, second],
            [shape((2, half // 2, width), BF)] * 4,
            flops=2 * half * width * width * 8, nbytes=10 << 20,
        )(info, *h_left, e_qkv, q_other, *a_left, e_branch, b_other)

    def swap(value, bit):
        if bit < 2:
            return partner(value, 1 << bit)
        return lax.ppermute(value, "dp", [(d, d ^ (1 << (bit - 2))) for d in range(pages)])

    def scattered(send, keep, dims, first, order):
        bits = [d for d in dims if d[0] is not None]
        send = send.reshape([n for _, n in dims])
        keep = keep.reshape([n for _, n in dims])
        names = [b for b, _ in dims]
        got = swap(send, first)
        for bit in order:
            axis = names.index(bit)
            take = functools.partial(lax.index_in_dim, axis=axis, keepdims=False)
            send = (take(keep, 1).astype(F32) + take(got, 1).astype(F32)).astype(BF)
            keep = (take(keep, 0).astype(F32) + take(got, 0).astype(F32)).astype(BF)
            names.pop(axis)
            got = swap(send, bit)
        return keep.astype(F32) + got.astype(F32)

    rest = list(range(3, sz.bits))
    piece = width // sz.devices
    ff_piece = hidden // sz.devices

    def reduce_cols(halves, outer):
        send, keep = halves
        blocks = send.shape[0]
        kept, first = (2, 1) if outer else (1, 2)
        dims = [(None, blocks), (kept, 2)] + [(b, 2) for b in rest] + [(None, piece), (None, width)]
        out = scattered(send, keep, dims, first, [kept] + rest)
        return jnp.swapaxes(out, 0, 1)

    def reduce_rows(halves):
        send, keep = halves
        top = list(range(sz.bits - 1, low_bits - 1, -1))
        low = [b for b in range(1, low_bits) if b != 2]
        dims = [(b, 2) for b in top] + [(b, 2) for b in low] + [(None, ff_piece), (None, width)]
        return scattered(send, keep, dims, 2, [1] + rest)

    def layer_backward(l, g, kept):
        x, qkv, p, kb, vb, stats, branch, x1, up, down, lefts = kept
        hid_spec = pl.BlockSpec((rows, width), lambda i: (0, i))
        e_down, e_up, g1, e_branch, vec = call(
            functools.partial(mlp_back_kernel, sz, l),
            (chunks,),
            [SCALARS, row_w, row_w, par, hid_spec, pl.BlockSpec((None, width, width), lambda i: (l, i, 0)),
             pl.BlockSpec((None, width, width), lambda i: (l, 0, i)), row_w, par, par, row_w],
            [row_w, hid_spec, row_w, row_w, whole((8, width))],
            [shape((rows, width), BF), shape((rows, hidden), BF), shape((rows, width), F32), shape((rows, width), BF),
             shape((8, width), F32)],
            [pltpu.VMEM((rows, width), F32)],
            flops=2 * rows * width * hidden * 2, nbytes=18 << 20,
        )(info, g, down, scale_mlp, up, down_weight, up_weight, x1, norm_mlp, scale_attn, branch)
        h_left, a_left, b_left, c_left = lefts
        down_halves = grads(False, c_left, e_down, partner(e_down, 1))
        up_halves = grads(True, b_left, e_up, partner(e_up, 1))
        nb, ng = sz.blocks, sz.groups
        d_q, d_kv, *tail = call(
            functools.partial(attention_back_kernel, sz, l),
            (1,),
            [SCALARS, row_w, pl.BlockSpec((None, width, width), lambda i: (l, 0, 0)), whole((rows, 3 * width)),
             whole((nb * ng, sz.bk, sz.bk)), whole((nb, sz.bk, width)), whole((nb, sz.bk, width)), whole((8, width)),
             whole((8, cells))],
            [whole((cells, width)), whole((cells, 2 * width))] + rim_specs + [whole((16, sz.bk))],
            [shape((cells, width), BF), shape((cells, 2 * width), F32)] + rim_shapes + [shape((16, sz.bk), F32)],
            [pltpu.VMEM((sz.ext_rows, width), F32), pltpu.VMEM((sz.ext_rows, width), F32), pltpu.VMEM((rows, width), F32),
             pltpu.VMEM((ng, sz.bk, sz.bk), F32)],
            flops=3 << 30, nbytes=16 << 20,
        )(info, e_branch, out_weight, qkv, p, kb, vb, stats, own_mask)
        rims, table = tail[:3], tail[3]
        got = exchange(rims)
        stat_spec = pl.BlockSpec((16, 2 * width), lambda i: (side * PAD // 16, 0))
        e_qkv, g, vec2 = call(
            functools.partial(qkv_back_kernel, sz, l),
            (3,),
            [SCALARS, whole((cells, width)), whole((cells, 2 * width)), stat_spec] + rim_specs
            + [pl.BlockSpec((None, width, width), lambda i: (l, 0, i)), row_w, par, row_w],
            [whole((rows, 3 * width)), row_w, whole((8, width))],
            [shape((rows, 3 * width), BF), shape((rows, width), F32), shape((8, width), F32)],
            [pltpu.VMEM((cells, 2 * width), F32), pltpu.VMEM((rows, width), F32)],
            flops=2 * rows * width * width * 3, nbytes=12 << 20,
        )(info, d_q, d_kv, rims[0], *got, qkv_weight, x, norm_attn, g1)
        s0, k0, s1, k1 = grads_attn(h_left, a_left, e_qkv, partner(e_qkv, 1), e_branch, partner(e_branch, 1))
        g_down = reduce_rows(down_halves)
        g_up = reduce_cols(up_halves, True)
        first = reduce_cols((s0, k0), True)
        second = reduce_cols((s1, k1), False)
        g_qkv = jnp.concatenate([first, second[:, :1]], axis=1).reshape(piece, 3 * width)
        vectors = jnp.concatenate([vec2[:1], vec[:3]], axis=0)
        return g, (g_qkv, second[:, 1], g_up.reshape(piece, hidden), g_down, vectors, table)

    x = jnp.concatenate([patch_in.reshape(cells, width).astype(F32), cls_in.astype(F32),
                         jnp.zeros((rows - cells - 1, width), F32)], axis=0)
    saved = []
    for l in range(layers):
        x, kept = layer_forward(l, x)
        saved.append(kept)
    valid = own_ok[:, None]
    patch_out = jnp.where(valid, x[:cells], 0.0).astype(BF).reshape(patch_in.shape)
    cls_out = x[cells : cells + 1].astype(BF)
    g = jnp.concatenate([jnp.where(valid, patch_cot.reshape(cells, width).astype(F32), 0.0), cls_cot.astype(F32),
                         jnp.zeros((rows - cells - 1, width), F32)], axis=0)
    results = [None] * layers
    for l in reversed(range(layers)):
        g, results[l] = layer_backward(l, g, saved[l])
    g_qkv, g_out, g_up, g_down, vectors, tables = (jnp.stack([r[i] for r in results]) for i in range(6))
    vectors, tables = lax.psum((vectors, tables), ("dp", "tile"))
    mine = lax.dynamic_slice_in_dim(vectors, me * piece, piece, axis=2)
    tables = tables[:, :heads, first_slot : first_slot + SPAN * sz.pitch].reshape(layers, heads, SPAN, sz.pitch)
    g_table = tables[..., :SPAN].reshape(rel_table.shape)
    return (
        patch_out,
        cls_out,
        g[:cells].reshape(patch_in.shape),
        g[cells : cells + 1],
        mine[:, 0],
        g_qkv,
        g_table,
        g_out,
        mine[:, 3],
        mine[:, 2],
        g_up,
        g_down,
        mine[:, 1],
    )


def solution(mesh):
    tokens = P("dp", "tile", None, None, None)
    split = ("dp", "tile")
    in_specs = (tokens, P("dp", None), P("dp")) + (P(),) * 9 + (tokens, P("dp", None))
    out_specs = (
        tokens,
        P("dp", None),
        tokens,
        P("dp", None),
        P(None, split),
        P(None, split, None),
        P(),
        P(None, split, None),
        P(None, split),
        P(None, split),
        P(None, split, None),
        P(None, split, None),
        P(None, split),
    )
    return jax.shard_map(local, mesh=mesh, in_specs=in_specs, out_specs=out_specs, check_vma=False)
```

```python
import functools

import jax
import jax.numpy as jnp
import numpy as np
from jax import lax
from jax.experimental import pallas as pl
from jax.experimental.pallas import tpu as pltpu
from jax.sharding import PartitionSpec as P

RADIUS = 3
SPAN = 2 * RADIUS + 1
PAD = 8
EPS = 1e-06
MASKED = -1e30
BF = jnp.bfloat16
F32 = jnp.float32
MIB = 1 << 20


def dot(a, b):
    return lax.dot_general(a, b, (((1,), (0,)), ((), ())), preferred_element_type=F32)


def dot_nt(a, b):
    return lax.dot_general(a, b, (((1,), (1,)), ((), ())), preferred_element_type=F32)


def dot_tn(a, b):
    return lax.dot_general(a, b, (((0,), (0,)), ((), ())), preferred_element_type=F32)


def normalized(x):
    centred = x - jnp.mean(x, axis=-1, keepdims=True)
    inverse = lax.rsqrt(jnp.mean(centred * centred, axis=-1, keepdims=True) + EPS)
    return centred * inverse, inverse


def norm_back(x, gain, d_out):
    unit, inverse = normalized(x)
    d_unit = d_out * gain
    d_x = inverse * (
        d_unit
        - jnp.mean(d_unit, axis=-1, keepdims=True)
        - unit * jnp.mean(d_unit * unit, axis=-1, keepdims=True)
    )
    return d_x, d_out * unit


def split3(x):
    high = x.astype(BF).astype(F32)
    rest = x - high
    middle = rest.astype(BF).astype(F32)
    return high, middle, rest - middle


def lane_heads(rows, lanes, width):
    return lax.broadcasted_iota(jnp.int32, (rows, lanes), 1) // width


def head_rows(rows, lanes, width):
    return lane_heads(rows, lanes, width) == lax.broadcasted_iota(jnp.int32, (rows, lanes), 0)


def stacked_heads(block, width):
    rows, lanes = block.shape
    heads = lane_heads(rows, lanes, width)
    zero = jnp.zeros_like(block)
    return jnp.concatenate(
        [jnp.where(heads == h, block, zero) for h in range(lanes // width)], axis=0
    )


def folded_heads(stack, width):
    count = stack.shape[1] // width
    rows = stack.shape[0] // count
    heads = lane_heads(rows, stack.shape[1], width)
    out = stack[:rows]
    for h in range(1, count):
        out = jnp.where(heads == h, stack[h * rows : (h + 1) * rows], out)
    return out


def keep_rows(rows, cells, class_weight):
    row = lax.broadcasted_iota(jnp.int32, (rows, 1), 0)
    return jnp.where(row < cells, 1.0, jnp.where(row == cells, class_weight, 0.0))


class Sizes:
    def __init__(self, side, width, hidden, heads, devices):
        self.side = side
        self.cells = side * side
        self.rows = self.cells + 16
        self.width = width
        self.hidden = hidden
        self.heads = heads
        self.head = width // heads
        self.pitch = side + PAD
        self.ext = side + 2 * RADIUS
        self.ext_rows = self.pitch * self.ext + PAD
        self.brows = 4
        self.blocks = side // self.brows
        self.bq = self.brows * side
        self.bk = 256
        self.class_slot = self.bk - PAD
        self.quad = 4 * self.head
        self.groups = width // self.quad
        self.devices = devices
        self.bits = devices.bit_length() - 1


def stat_rows(values):
    width = values[0].shape[1]
    parts = [split3(v) for v in values]
    flat = [p[k] for k in range(3) for p in parts]
    if len(flat) % 2:
        flat.append(jnp.zeros_like(flat[0]))
    row = lax.broadcasted_iota(jnp.int32, (16, 2 * width), 0)
    out = jnp.zeros((16, 2 * width), F32)
    for i in range(0, len(flat), 2):
        out = jnp.where(row == i // 2, jnp.concatenate(flat[i : i + 2], axis=1), out)
    return out.astype(BF)


def read_stats(block, count, width):
    rows = block.astype(F32)

    def piece(i):
        return rows[i // 2 : i // 2 + 1, (i % 2) * width : (i % 2 + 1) * width]

    return [piece(i) + piece(count + i) + piece(2 * count + i) for i in range(count)]


def in_tile_order(info, pieces):
    me = info[0] * 2 + info[1]
    out = []
    for t in range(4):
        d = me ^ t
        out.append(
            [
                jnp.where(d == 0, a, jnp.where(d == 1, b, jnp.where(d == 2, c, e)))
                for a, b, c, e in zip(*pieces)
            ]
        )
    return out


def class_scores(sz, info, qkv_ref, mask):
    cells, width = sz.cells, sz.width
    own = head_rows(16, width, sz.head)
    class_rows = qkv_ref[cells : cells + 16, :].astype(F32)
    q_c, k_c, v_c = (class_rows[0:1, i * width : (i + 1) * width] for i in range(3))
    q_heads = jnp.where(own, q_c, 0.0)
    scale = sz.head ** (-0.5)
    scores = dot_nt(q_heads.astype(BF), qkv_ref[0:cells, width : 2 * width]) * scale + mask
    self_score = jnp.sum(q_heads * k_c, axis=1, keepdims=True) * scale
    self_score = jnp.where(info[2] == 1, self_score, MASKED)
    return own, q_heads, k_c, v_c, scores, self_score


def send_rims(sz, info, kv_half, kv_edge_rows, stats, pc_ref, pr_ref, pd_ref):
    side, width = sz.side, sz.width
    cells8 = [kv_half(r) for r in range(side)]
    pc_ref[0 : side * PAD, :] = jnp.concatenate(cells8, axis=0).astype(BF)
    pc_ref[side * PAD : side * PAD + 16, :] = stats
    edge, corner = kv_edge_rows()
    pr_ref[0 : RADIUS * side, :] = jnp.concatenate(edge, axis=0).astype(BF)
    pr_ref[RADIUS * side : RADIUS * side + 16, :] = stats
    zero = jnp.zeros((PAD, 2 * width), F32)
    pd_ref[0 : (RADIUS + 1) * PAD, :] = jnp.concatenate(corner + [zero], axis=0).astype(BF)
    pd_ref[(RADIUS + 1) * PAD : (RADIUS + 1) * PAD + 16, :] = stats


def rim_places(sz, info):
    return sz.pitch * (1 - info[1]), (sz.side + RADIUS) * (1 - info[0])


GELU_C = float(np.sqrt(2.0 / np.pi))


class Copies:
    def __init__(self, sems):
        self.sems, self.count, self.out = sems, 0, []

    def load(self, src, dst):
        copy = pltpu.make_async_copy(src, dst, self.sems.at[self.count])
        self.count += 1
        copy.start()
        return copy

    def store(self, src, dst):
        self.out.append(self.load(src, dst))

    def finish(self):
        for copy in self.out:
            copy.wait()


def qkv_part(sz, info, x, gain, wq, loads, mask, h_ref, qkv_ref, pc_ref, pr_ref, pd_ref):
    width, side, cells = sz.width, sz.side, sz.cells
    unit, _ = normalized(x)
    h = (unit * gain).astype(BF)
    h_ref[...] = h
    for i in range(3):
        loads[i].wait()
        cols = slice(i * width, (i + 1) * width)
        qkv_ref[:, cols] = dot(h, wq[:, cols]).astype(BF)
    own, q_heads, k_c, v_c, scores, self_score = class_scores(sz, info, qkv_ref, mask)
    top = jnp.maximum(jnp.max(scores, axis=1, keepdims=True), self_score)
    probs = jnp.where(mask > -1.0, jnp.exp(scores - top), 0.0)
    self_prob = jnp.where(info[2] == 1, jnp.exp(self_score - top), 0.0)
    total = jnp.sum(probs, axis=1, keepdims=True) + self_prob
    part = dot(probs.astype(BF), qkv_ref[0:cells, 2 * width :]) + self_prob * v_c

    def to_row(v):
        return jnp.sum(jnp.where(own, v, 0.0), axis=0, keepdims=True)

    stats = stat_rows([to_row(part), to_row(top), to_row(total)])
    left_col = info[1] == 0

    def half(r):
        row = qkv_ref[r * side : (r + 1) * side, width:].astype(F32)
        return jnp.where(left_col, row[PAD:], row[:PAD])

    def edges():
        first = pl.multiple_of((1 - info[0]) * (side - RADIUS) * side, 16)
        rows = qkv_ref[pl.ds(first, RADIUS * side), width:].astype(F32)
        edge = [rows[t * side : (t + 1) * side] for t in range(RADIUS)]
        return edge, [jnp.where(left_col, e[PAD:], e[:PAD]) for e in edge]

    send_rims(sz, info, half, edges, stats, pc_ref, pr_ref, pd_ref)


def first_kernel(sz, info, patch_ref, cls_ref, gain_ref, mask_ref, w_any,
                 x_ref, qkv_ref, pc_ref, pr_ref, pd_ref, h_v, wq, sems):
    copies = Copies(sems)
    width = sz.width
    loads = [copies.load(w_any.at[0, :, pl.ds(i * width, width)], wq.at[:, pl.ds(i * width, width)]) for i in range(3)]
    row = lax.broadcasted_iota(jnp.int32, (16, width), 0)
    x_ref[0 : sz.cells, :] = patch_ref[...].astype(F32)
    x_ref[sz.cells :, :] = jnp.where(row == 0, cls_ref[...].astype(F32), 0.0)
    qkv_part(sz, info, x_ref[...], gain_ref[0:1, :], wq, loads, mask_ref[0:1, :], h_v, qkv_ref, pc_ref, pr_ref, pd_ref)


def extended(sz, info, qkv_ref, rc_ref, rr_ref, rd_ref, kext, vext):
    width, side, pitch = sz.width, sz.side, sz.pitch
    beside, above = rim_places(sz, info)
    for ext, lo in ((kext, width), (vext, 2 * width)):
        at = lo - width
        ext[...] = jnp.zeros_like(ext)
        for r in range(side):
            base = pitch * (r + RADIUS)
            ext[base + PAD : base + PAD + side, :] = qkv_ref[r * side : (r + 1) * side, lo : lo + width].astype(F32)
        sides = rc_ref[0 : side * PAD, at : at + width].astype(F32)
        for r in range(side):
            ext[pl.ds(pl.multiple_of(pitch * (r + RADIUS) + beside, 8), PAD), :] = sides[r * PAD : (r + 1) * PAD]
        edge = rr_ref[0 : RADIUS * side, at : at + width].astype(F32)
        corner = rd_ref[0 : (RADIUS + 1) * PAD, at : at + width].astype(F32)
        for t in range(RADIUS):
            base = pitch * (above + t)
            ext[pl.ds(pl.multiple_of(base + PAD, 8), side), :] = edge[t * side : (t + 1) * side]
            ext[pl.ds(pl.multiple_of(base + beside, 8), PAD), :] = corner[t * PAD : (t + 1) * PAD]


def all_stats(sz, info, st_ref, rc_ref, rr_ref, rd_ref):
    side, width = sz.side, sz.width
    return in_tile_order(info, [read_stats(r, 3, width) for r in (
        st_ref[...],
        rc_ref[side * PAD : side * PAD + 16, :],
        rr_ref[RADIUS * side : RADIUS * side + 16, :],
        rd_ref[(RADIUS + 1) * PAD : (RADIUS + 1) * PAD + 16, :],
    )])


def middle_kernel(sz, layer, last, info, *refs):
    refs = list(refs)

    def take(n):
        out = refs[:n]
        del refs[:n]
        return out

    (qkv_ref, st_ref, rc_ref, rr_ref, rd_ref, bias_ref, mask_ref, x_ref, own_mask_ref,
     scale_a_ref, gain_m_ref, scale_m_ref, gain_a_ref) = take(13)
    out_w, up_w, down_w = take(3)
    if last:
        cot_ref, cls_cot_ref, valid_ref = take(3)
    else:
        (qkv_w,) = take(1)
    p_out, kb_out, vb_out, slope_out, x1_out, br_out, down_out, left_out, stat_ref = take(9)
    if last:
        po_ref, co_ref, right_out, g1_ref, vec_ref = take(5)
    else:
        x2_ref, next_ref, pc_ref, pr_ref, pd_ref = take(5)
    (kext, vext, w_out, w_up, w_down, p_v, kb_v, vb_v, slope_v, x1_v, br_v, down_v, att, h2_v, act_v, acc) = take(16)
    if last:
        ed_v, eu_v, eb_v = take(3)
    else:
        w_qkv, h_v = take(2)
    if layer == 0:
        (first_v,) = take(1)
    (sems,) = take(1)
    width, side, cells, pitch, hidden = sz.width, sz.side, sz.cells, sz.pitch, sz.hidden
    chunks = hidden // width
    copies = Copies(sems)
    out_load = copies.load(out_w.at[layer], w_out)
    up_loads, down_loads = [], []
    for c in range(chunks):
        at = pl.ds(c * width, width)
        up_loads.append(copies.load(up_w.at[layer, :, at], w_up.at[:, at]))
        down_loads.append(copies.load(down_w.at[layer, at, :], w_down.at[at, :]))
    if not last:
        qkv_loads = [
            copies.load(qkv_w.at[layer + 1, :, pl.ds(i * width, width)], w_qkv.at[:, pl.ds(i * width, width)])
            for i in range(3)
        ]
    extended(sz, info, qkv_ref, rc_ref, rr_ref, rd_ref, kext, vext)
    if layer == 0:
        first_v[...] = (normalized(x_ref[...])[0] * gain_a_ref[0:1, :]).astype(BF)
        copies.store(first_v, left_out.at[:, pl.ds(left_out.shape[1] - width, width)])
    class_rows = qkv_ref[cells : cells + 16, :].astype(F32)[0:PAD]
    scale = sz.head ** (-0.5)
    for b in range(sz.blocks):
        first = b * sz.brows * pitch
        kb = jnp.concatenate([kext[first : first + sz.class_slot, :], class_rows[:, width : 2 * width]], axis=0).astype(BF)
        vb = jnp.concatenate([vext[first : first + sz.class_slot, :], class_rows[:, 2 * width :]], axis=0).astype(BF)
        kb_v[b] = kb
        vb_v[b] = vb
        q = qkv_ref[b * sz.bq : (b + 1) * sz.bq, 0:width] * jnp.asarray(scale, BF)
        mask = mask_ref[b]
        mask = jnp.concatenate([mask, mask], axis=1)
        for g in range(sz.groups):
            lanes = slice(g * sz.quad, (g + 1) * sz.quad)
            scores = dot_nt(kb[:, lanes], stacked_heads(q[:, lanes], sz.head)) + bias_ref[g] + mask
            top = jnp.max(scores, axis=0, keepdims=True)
            probs = jnp.exp(scores - top)
            total = jnp.sum(probs, axis=0, keepdims=True)
            probs = (probs * (1.0 / total)).astype(BF)
            p_v[b * sz.groups + g] = probs
            out = folded_heads(dot_tn(probs, vb[:, lanes]), sz.head)
            att[b * sz.bq : (b + 1) * sz.bq, lanes] = out.astype(BF)
    copies.store(kb_v, kb_out)
    copies.store(vb_v, vb_out)
    copies.store(p_v, p_out)
    ordered = all_stats(sz, info, st_ref, rc_ref, rr_ref, rd_ref)
    top = functools.reduce(jnp.maximum, [s[1] for s in ordered])
    total = jnp.zeros_like(top)
    summed = jnp.zeros_like(top)
    for part, part_top, part_total in ordered:
        factor = jnp.exp(part_top - top)
        total = total + part_total * factor
        summed = summed + part * factor
    class_out = summed / total
    stat_ref[...] = jnp.zeros_like(stat_ref)
    stat_ref[0:1, :] = top
    stat_ref[1:2, :] = total
    stat_ref[2:3, :] = class_out
    row = lax.broadcasted_iota(jnp.int32, (16, width), 0)
    att[cells : cells + 16, :] = jnp.where(row == 0, class_out, 0.0).astype(BF)
    copies.store(att, left_out.at[:, pl.ds(0, width)])
    out_load.wait()
    branch = dot(att[...], w_out[...])
    br_v[...] = branch.astype(BF)
    x1_v[...] = x_ref[...] + scale_a_ref[layer : layer + 1, :] * branch
    copies.store(br_v, br_out)
    copies.store(x1_v, x1_out)
    unit, _ = normalized(x1_v[...])
    h2_v[...] = (unit * gain_m_ref[layer : layer + 1, :]).astype(BF)
    copies.store(h2_v, left_out.at[:, pl.ds(width, width)])
    for c in range(chunks):
        at = slice(c * width, (c + 1) * width)
        up_loads[c].wait()
        u = dot(h2_v[...], w_up[:, at])
        square = u * u
        th = jnp.tanh(GELU_C * u * (1.0 + 0.044715 * square))
        half = 0.5 * (1.0 + th)
        act_v[:, at] = (u * half).astype(BF)
        slope = half + (0.5 * u) * (1.0 - th * th) * (GELU_C + (3 * 0.044715 * GELU_C) * square)
        slope_v[:, at] = slope.astype(BF)
        down_loads[c].wait()
        part = dot(act_v[:, at], w_down[at, :])
        if c == 0:
            acc[...] = part
        else:
            acc[...] += part
    copies.store(act_v, left_out.at[:, pl.ds(2 * width, hidden)])
    copies.store(slope_v, slope_out)
    down_v[...] = acc[...].astype(BF)
    copies.store(down_v, down_out)
    x2 = x1_v[...] + scale_m_ref[layer : layer + 1, :] * acc[...]
    if last:
        po_ref[...] = (x2[0:cells] * valid_ref[...]).astype(BF)
        co_ref[...] = x2[cells : cells + 1].astype(BF)
        g_cells = cot_ref[...].astype(F32) * valid_ref[...]
        g_class = jnp.where(row == 0, cls_cot_ref[...].astype(F32), 0.0)
        g = jnp.concatenate([g_cells, g_class], axis=0)
        keep = keep_rows(sz.rows, cells, jnp.where(info[2] == 1, 1.0, 0.0))
        vec_ref[...] = jnp.zeros_like(vec_ref)
        mlp_back_part(sz, layer, g, acc[...], keep, ed_v, eu_v, eb_v, right_out, 0, g1_ref, vec_ref, x1_v, br_v, slope_v,
                      w_up, w_down, None, None, gain_m_ref, scale_a_ref, scale_m_ref, acc, copies)
    else:
        x2_ref[...] = x2
        qkv_part(sz, info, x2, gain_a_ref[layer + 1 : layer + 2, :], w_qkv, qkv_loads, own_mask_ref[0:1, :],
                 h_v, next_ref, pc_ref, pr_ref, pd_ref)
        copies.store(h_v, left_out.at[:, pl.ds(2 * width + hidden, width)])
    copies.finish()


def mlp_back_part(sz, layer, g, down, keep, ed_ref, eu_v, eb_ref, right_out, at0, g1_ref, vec_ref, x1_ref, br_ref, slope_ref,
                  w_up, w_down, up_loads, down_loads, gain_m_ref, scale_a_ref, scale_m_ref, acc, copies):
    width = sz.width
    vec_ref[0:1, :] = jnp.sum(keep * g * down, axis=0, keepdims=True)
    e_down = (scale_m_ref[layer : layer + 1, :] * g).astype(BF)
    ed_ref[...] = e_down
    copies.store(ed_ref, right_out.at[:, pl.ds(at0, width)])
    g1_ref[...] = g
    for c in range(sz.hidden // width):
        at = slice(c * width, (c + 1) * width)
        if down_loads is not None:
            for copy in down_loads[c]:
                copy.wait()
        e_up = (dot_nt(ed_ref[...], w_down[at, :]) * slope_ref[:, at].astype(F32)).astype(BF)
        eu_v[:, at] = e_up
        if up_loads is not None:
            up_loads[c].wait()
        part = dot_nt(eu_v[:, at], w_up[:, at])
        if c == 0:
            acc[...] = part
        else:
            acc[...] += part
    copies.store(eu_v, right_out.at[:, pl.ds(at0 + width, sz.hidden)])
    d_x1, gain_rows = norm_back(x1_ref[...], gain_m_ref[layer : layer + 1, :], acc[...])
    vec_ref[1:2, :] = jnp.sum(keep * gain_rows, axis=0, keepdims=True)
    g1 = g1_ref[...] + d_x1
    g1_ref[...] = g1
    eb_ref[...] = (scale_a_ref[layer : layer + 1, :] * g1).astype(BF)
    copies.store(eb_ref, right_out.at[:, pl.ds(at0 + width + sz.hidden, width)])
    vec_ref[2:3, :] = jnp.sum(keep * g1 * br_ref[...].astype(F32), axis=0, keepdims=True)


def attention_back_kernel(sz, layer, info, eb_ref, qkv_ref, stat_ref, own_mask_ref, w_any, p_any, kb_any, vb_any,
                          dq_ref, dkv_ref, pc_ref, pr_ref, pd_ref, tab_ref,
                          kext, vext, d_o, tab, w, p_v, kb_v, vb_v, sems):
    width, side, cells, pitch = sz.width, sz.side, sz.cells, sz.pitch
    scale = sz.head ** (-0.5)
    copies = Copies(sems)
    w_load = copies.load(w_any.at[layer], w)
    loads = []
    for b in range(sz.blocks):
        at = pl.ds(b * sz.groups, sz.groups)
        loads.append([
            copies.load(vb_any.at[b], vb_v.at[b]),
            copies.load(p_any.at[at], p_v.at[at]),
            copies.load(kb_any.at[b], kb_v.at[b]),
        ])
    kext[...] = jnp.zeros_like(kext)
    vext[...] = jnp.zeros_like(vext)
    w_load.wait()
    d_o[...] = dot_nt(eb_ref[...], w[...])
    class_k = [jnp.zeros((PAD, sz.quad), F32) for _ in range(sz.groups)]
    class_v = [jnp.zeros((PAD, sz.quad), F32) for _ in range(sz.groups)]
    for b in range(sz.blocks):
        for copy in loads[b]:
            copy.wait()
        first = b * sz.brows * pitch
        q = qkv_ref[b * sz.bq : (b + 1) * sz.bq, 0:width] * jnp.asarray(scale, BF)
        do = d_o[b * sz.bq : (b + 1) * sz.bq, :].astype(BF)
        for g in range(sz.groups):
            lanes = slice(g * sz.quad, (g + 1) * sz.quad)
            do_stack = stacked_heads(do[:, lanes], sz.head)
            q_stack = stacked_heads(q[:, lanes], sz.head)
            probs = p_v[b * sz.groups + g]
            wide = probs.astype(F32)
            d_prob = dot_nt(vb_v[b, :, lanes], do_stack)
            delta = jnp.sum(wide * d_prob, axis=0, keepdims=True)
            d_score = wide * (d_prob - delta)
            if b == 0:
                tab[g] = d_score
            else:
                tab[g] += d_score
            low = d_score.astype(BF)
            d_v = dot(probs, do_stack)
            d_k = dot(low, q_stack)
            vext[first : first + sz.class_slot, lanes] += d_v[: sz.class_slot]
            kext[first : first + sz.class_slot, lanes] += d_k[: sz.class_slot]
            class_v[g] = class_v[g] + d_v[sz.class_slot :]
            class_k[g] = class_k[g] + d_k[sz.class_slot :]
            d_q = folded_heads(dot_tn(low, kb_v[b, :, lanes]), sz.head) * scale
            dq_ref[b * sz.bq : (b + 1) * sz.bq, lanes] = d_q.astype(BF)
    mask = own_mask_ref[0:1, :]
    own, q_heads, k_c, v_c, scores, self_score = class_scores(sz, info, qkv_ref, mask)
    top = jnp.max(jnp.where(own, stat_ref[0:1, :], MASKED), axis=1, keepdims=True)
    total = jnp.max(jnp.where(own, stat_ref[1:2, :], 0.0), axis=1, keepdims=True)
    real = lax.broadcasted_iota(jnp.int32, (16, 1), 0) < sz.heads
    probs = jnp.where((mask > -1.0) & real, jnp.exp(scores - top) / total, 0.0)
    self_prob = jnp.where((info[2] == 1) & real, jnp.exp(self_score - top) / total, 0.0)
    d_class = jnp.where(own, d_o[cells : cells + 1, :], 0.0)
    delta = jnp.sum(d_class * stat_ref[2:3, :], axis=1, keepdims=True)
    d_low = d_class.astype(BF)
    d_cell = probs * (dot_nt(d_low, qkv_ref[0:cells, 2 * width :]) - delta)
    d_cell_low = d_cell.astype(BF)
    d_self = self_prob * (jnp.sum(d_class * v_c, axis=1, keepdims=True) - delta)

    def to_row(v):
        return jnp.sum(jnp.where(own, v, 0.0), axis=0, keepdims=True)

    g_q = to_row(dot(d_cell_low, qkv_ref[0:cells, width : 2 * width]) + d_self * k_c) * scale
    g_k = to_row(d_self * q_heads) * scale + jnp.concatenate([c[0:1] for c in class_k], axis=1)
    g_v = to_row(self_prob * d_class) + jnp.concatenate([c[0:1] for c in class_v], axis=1)
    add_k = dot_tn(d_cell_low, q_heads.astype(BF)) * scale
    add_v = dot_tn(probs.astype(BF), d_low)
    beside, above = rim_places(sz, info)
    for r in range(side):
        base = pitch * (r + RADIUS) + PAD
        rows = slice(r * side, (r + 1) * side)
        dkv_ref[rows, 0:width] = kext[base : base + side, :] + add_k[rows]
        dkv_ref[rows, width:] = vext[base : base + side, :] + add_v[rows]

    def pair(at, count):
        at = pl.ds(pl.multiple_of(at, 8), count)
        return jnp.concatenate([kext[at, :], vext[at, :]], axis=1)

    def edges():
        return (
            [pair(pitch * (above + t) + PAD, side) for t in range(RADIUS)],
            [pair(pitch * (above + t) + beside, PAD) for t in range(RADIUS)],
        )

    send_rims(sz, info, lambda r: pair(pitch * (r + RADIUS) + beside, PAD), edges,
              stat_rows([g_q, g_k, g_v]), pc_ref, pr_ref, pd_ref)
    per_head = sz.bq
    for g in range(sz.groups):
        turned = tab[g].T
        for h in range(4):
            total_h = jnp.zeros((side, sz.bk), F32)
            for r in range(sz.brows):
                at = h * per_head + r * side
                piece = turned[at : at + side]
                shift = (sz.bk - pitch * r) % sz.bk
                total_h = total_h + (pltpu.roll(piece, shift, 1) if shift else piece)
            tab_row = jnp.zeros((1, sz.bk), F32)
            for c in range(side):
                one = total_h[c : c + 1]
                tab_row = tab_row + (pltpu.roll(one, sz.bk - c, 1) if c else one)
            tab_ref[4 * g + h : 4 * g + h + 1, :] = tab_row
    tab_ref[sz.heads : 16, :] = jnp.zeros((16 - sz.heads, sz.bk), F32)


def qkv_back_part(sz, info, dq_ref, dkv_ref, st_ref, rc_ref, rr_ref, rd_ref, x_ref, gain, g1_ref, eq_ref, dkv, acc, wq, loads):
    width, side, cells = sz.width, sz.side, sz.cells
    dkv[...] = dkv_ref[...]
    beside = PAD * (1 - info[1])
    edge = (1 - info[0]) * (side - RADIUS) * side
    sides = rc_ref[0 : side * PAD, :].astype(F32)
    for r in range(side):
        dkv[pl.ds(pl.multiple_of(r * side + beside, 8), PAD), :] += sides[r * PAD : (r + 1) * PAD]
    dkv[pl.ds(pl.multiple_of(edge, 8), RADIUS * side), :] += rr_ref[0 : RADIUS * side, :].astype(F32)
    corner = rd_ref[0 : (RADIUS + 1) * PAD, :].astype(F32)
    for t in range(RADIUS):
        dkv[pl.ds(pl.multiple_of(edge + t * side + beside, 8), PAD), :] += corner[t * PAD : (t + 1) * PAD]
    ordered = all_stats(sz, info, st_ref, rc_ref, rr_ref, rd_ref)
    class_row = jnp.concatenate(
        [functools.reduce(lambda a, b: a + b, [o[i] for o in ordered]) for i in range(3)], axis=1
    )
    row = lax.broadcasted_iota(jnp.int32, (16, 3 * width), 0)
    eq_ref[0:cells, 0:width] = dq_ref[...]
    eq_ref[0:cells, width:] = dkv[...].astype(BF)
    eq_ref[cells : cells + 16, :] = jnp.where(row == 0, class_row, 0.0).astype(BF)
    for i in range(3):
        cols = slice(i * width, (i + 1) * width)
        loads[i].wait()
        part = dot_nt(eq_ref[:, cols], wq[:, cols])
        if i == 0:
            acc[...] = part
        else:
            acc[...] += part
    d_x, gain_rows = norm_back(x_ref[...], gain, acc[...])
    return g1_ref[...] + d_x, gain_rows


def small_rows(sz, small_ref, vec_ref, tab_ref, gain_sum):
    small_ref[...] = jnp.zeros_like(small_ref)
    small_ref[0:3, :] = vec_ref[0:3, :]
    small_ref[3:4, :] = gain_sum
    small_ref[8:24, 0 : sz.bk] = tab_ref[...]


def qkv_back_kernel(sz, layer, info, dq_ref, dkv_ref, st_ref, rc_ref, rr_ref, rd_ref, x_ref, g1_ref, vec_ref, tab_ref,
                    gain_a_ref, qkv_w, eq_ref, ek_ref, ev_ref, small_ref, g_ref, dkv, acc, wq, eq_v, sems):
    width = sz.width
    copies = Copies(sems)
    loads = [copies.load(qkv_w.at[layer, :, pl.ds(i * width, width)], wq.at[:, pl.ds(i * width, width)]) for i in range(3)]
    g, gain_rows = qkv_back_part(sz, info, dq_ref, dkv_ref, st_ref, rc_ref, rr_ref, rd_ref, x_ref,
                                 gain_a_ref[layer : layer + 1, :], g1_ref, eq_v, dkv, acc, wq, loads)
    for i, ref in enumerate((eq_ref, ek_ref, ev_ref)):
        ref[...] = eq_v[:, i * width : (i + 1) * width]
    keep = keep_rows(sz.rows, sz.cells, jnp.where(info[2] == 1, 1.0, 0.0))
    small_rows(sz, small_ref, vec_ref, tab_ref, jnp.sum(keep * gain_rows, axis=0, keepdims=True))
    g_ref[...] = g


def mlp_back_kernel(sz, layer, info, g_ref, gain_m_ref, scale_a_ref, scale_m_ref, x1_ref, br_ref, down_ref,
                    up_w, down_w, slope_any, right_out, g1_out, vec_out, acc, w_up, w_down, slope_v, ed_v, eu_v, eb_v, sems):
    width = sz.width
    copies = Copies(sems)
    up_loads, down_loads, slope_loads = [], [], []
    for c in range(sz.hidden // width):
        at = pl.ds(c * width, width)
        down_loads.append(copies.load(down_w.at[layer, at, :], w_down.at[at, :]))
        slope_loads.append(copies.load(slope_any.at[:, at], slope_v.at[:, at]))
        up_loads.append(copies.load(up_w.at[layer, :, at], w_up.at[:, at]))
    keep = keep_rows(sz.rows, sz.cells, jnp.where(info[2] == 1, 1.0, 0.0))
    vec_out[...] = jnp.zeros_like(vec_out)
    mlp_back_part(sz, layer, g_ref[...], down_ref[...].astype(F32), keep, ed_v, eu_v, eb_v, right_out, 0, g1_out, vec_out,
                  x1_ref, br_ref, slope_v, w_up, w_down, up_loads, [(a, b) for a, b in zip(down_loads, slope_loads)],
                  gain_m_ref, scale_a_ref, scale_m_ref, acc, copies)
    copies.finish()


def last_kernel(sz, info, dq_ref, dkv_ref, st_ref, rc_ref, rr_ref, rd_ref, x_ref, g1_ref, vec_ref, tab_ref, gain_a_ref, qkv_w,
                eq_ref, ek_ref, ev_ref, small_ref, pg_ref, cg_ref, dkv, acc, wq, eq_v, sems):
    width = sz.width
    copies = Copies(sems)
    loads = [copies.load(qkv_w.at[0, :, pl.ds(i * width, width)], wq.at[:, pl.ds(i * width, width)]) for i in range(3)]
    g, gain_rows = qkv_back_part(sz, info, dq_ref, dkv_ref, st_ref, rc_ref, rr_ref, rd_ref, x_ref,
                                 gain_a_ref[0:1, :], g1_ref, eq_v, dkv, acc, wq, loads)
    for i, ref in enumerate((eq_ref, ek_ref, ev_ref)):
        ref[...] = eq_v[:, i * width : (i + 1) * width]
    keep = keep_rows(sz.rows, sz.cells, jnp.where(info[2] == 1, 1.0, 0.0))
    small_rows(sz, small_ref, vec_ref, tab_ref, jnp.sum(keep * gain_rows, axis=0, keepdims=True))
    pg_ref[...] = g[0 : sz.cells]
    cg_ref[...] = g[sz.cells : sz.cells + 1]


def product(sz, info, left_ref, left_got, own_ref, other_ref):
    cells = sz.cells
    row = lax.broadcasted_iota(jnp.int32, (16, own_ref.shape[1]), 0)
    tail = own_ref[cells : cells + 16, :]
    tail = jnp.where((row < 0) | (info[0] == 0), tail, jnp.zeros_like(tail))
    left = jnp.concatenate([left_ref[0:cells, :], left_got[0:cells, :], left_ref[cells : cells + 16, :]], axis=0)
    right = jnp.concatenate([own_ref[0:cells, :], other_ref[0:cells, :], tail], axis=0)
    return dot_tn(left, right)


def store_pieces(value, count, pairs, bit, place, send_ref, keep_ref):
    per = value.shape[0] // count
    for a, b in pairs:
        one, two = value[a * per : (a + 1) * per], value[b * per : (b + 1) * per]
        at = place(a)
        keep_ref[at] = jnp.where(bit == 0, one, two).astype(BF)
        send_ref[at] = jnp.where(bit == 0, two, one).astype(BF)


def pairs_of(bits, bit):
    return [(a, a | 1 << bit) for a in range(1 << bits) if not a >> bit & 1]


def place_of(bits, skip, me):
    def place(a):
        names = [b for b in range(bits - 1, -1, -1) if b != skip]
        at = 0
        for b in names:
            mine = (a >> b) & 1
            at = at * 2 + (mine if b == 0 else mine ^ ((me >> b) & 1))
        return at

    return place


def order_of(bits, skip, first):
    def place(a, me):
        names = [first] + [b for b in range(bits - 1, -1, -1) if b not in (skip, first)]
        at = 0
        for b in names:
            mine = (a >> b) & 1
            at = at * 2 + (mine if b == 0 else mine ^ ((me >> b) & 1))
        return at

    return place


def down_kernel(sz, info, act_ref, act_got, own_ref, other_ref, send_ref, keep_ref):
    bits = sz.bits - 2
    me = info[4]
    value = product(sz, info, act_ref, act_got, own_ref, other_ref)
    place = order_of(bits, 2, 1)
    store_pieces(value, 1 << bits, pairs_of(bits, 2), (me >> 2) & 1, lambda a: place(a, me), send_ref, keep_ref)


def columns_step(sz, info, outer, value, send_ref, keep_ref):
    bits = sz.bits - 1
    me = info[4]
    bit, other = (1, 2) if outer else (2, 1)
    place = order_of(bits, bit, other)
    store_pieces(value, 1 << bits, pairs_of(bits, bit), (me >> bit) & 1, lambda a: place(a, me), send_ref, keep_ref)


def up_kernel(sz, info, h_ref, h_got, own_ref, other_ref, send_ref, keep_ref):
    columns_step(sz, info, True, product(sz, info, h_ref, h_got, own_ref, other_ref), send_ref, keep_ref)


def attn_grad_kernel(sz, info, h_ref, h_got, qo, qg, ko, kg, vo, vg, a_ref, a_got, bo, bg, s0, k0, s1, k1):
    step = pl.program_id(0)

    @pl.when(step == 0)
    def _():
        columns_step(sz, info, True, product(sz, info, h_ref, h_got, qo, qg), s0, k0)

    @pl.when(step == 1)
    def _():
        columns_step(sz, info, True, product(sz, info, h_ref, h_got, ko, kg), s0, k0)

    @pl.when(step == 2)
    def _():
        columns_step(sz, info, False, product(sz, info, h_ref, h_got, vo, vg), s1, k1)

    @pl.when(step == 3)
    def _():
        columns_step(sz, info, False, product(sz, info, a_ref, a_got, bo, bg), s1, k1)


def plus(a, b):
    return a.astype(F32) + b.astype(F32)


def second_kernel(info, k0, g0, k1, g1, s0_ref, k0_ref, s1_ref, k1_ref):
    s0_ref[...] = plus(k0[:, 1], g0[:, 1]).astype(BF)
    k0_ref[...] = plus(k0[:, 0], g0[:, 0]).astype(BF)
    s1_ref[...] = plus(k1[:, 1], g1[:, 1]).astype(BF)
    k1_ref[...] = plus(k1[:, 0], g1[:, 0]).astype(BF)


def third_kernel(info, k0, g0, k1, g1, s_ref, k_ref):
    s_ref[0] = plus(k0[1], g0[1]).astype(BF)
    k_ref[0] = plus(k0[0], g0[0]).astype(BF)
    s_ref[1] = plus(k1[1], g1[1]).astype(BF)
    k_ref[1] = plus(k1[0], g1[0]).astype(BF)


def more_kernel(info, k, g, s_ref, k_ref):
    s_ref[...] = plus(k[:, 1], g[:, 1]).astype(BF)
    k_ref[...] = plus(k[:, 0], g[:, 0]).astype(BF)


def fourth_kernel(sz, info, k, g, a_ref, b_ref):
    high = (info[4] >> (sz.bits - 1)) & 1
    one, two = plus(k[:, 0], g[:, 0]), plus(k[:, 1], g[:, 1])
    a_ref[...] = jnp.where(high == 0, one, two).astype(BF)
    b_ref[...] = jnp.where(high == 0, two, one).astype(BF)


def bias_kernel(sz, table_ref, out_ref, wide):
    slot = lax.broadcasted_iota(jnp.int32, (sz.side, sz.bk), 1)
    for g in range(sz.groups):
        for h in range(4):
            line = jnp.broadcast_to(table_ref[4 * g + h : 4 * g + h + 1, :], (sz.side, sz.bk))
            line = pltpu.roll(line, 0, 1, stride=1, stride_axis=0)
            for r in range(sz.brows):
                piece = pltpu.roll(line, sz.pitch * r, 1) if r else line
                at = h * sz.bq + r * sz.side
                wide[at : at + sz.side, :] = jnp.where(slot == sz.class_slot, 0.0, piece)
        out_ref[g] = wide[...].T


def shape(dims, dtype):
    return jax.ShapeDtypeStruct(dims, dtype)


def kept(dims, dtype):
    return pltpu.HBM(dims, dtype)


def whole(dims):
    return pl.BlockSpec(dims, lambda *_: (0,) * len(dims))


ANY = pl.BlockSpec(memory_space=pl.ANY)
LONG = 10**11


def local(patch_in, cls_in, page_side, norm_attn, qkv_weight, rel_table, out_weight, scale_attn,
          norm_mlp, up_weight, down_weight, scale_mlp, patch_cot, cls_cot):
    tiles = lax.axis_size("tile")
    pages = lax.axis_size("dp")
    layers, heads = rel_table.shape[:2]
    sz = Sizes(patch_in.shape[2], patch_in.shape[4], up_weight.shape[2], heads, tiles * pages)
    side, cells, rows, width, hidden = sz.side, sz.cells, sz.rows, sz.width, sz.hidden
    chunks = hidden // width
    tile = lax.axis_index("tile")
    me = lax.axis_index("dp") * tiles + tile
    tile_row, tile_col = tile // 2, tile % 2
    page = page_side[0]
    bits = sz.bits
    top_bit, next_bit = bits - 1, bits - 2
    info = jnp.stack([tile_row, tile_col, (tile == 0).astype(jnp.int32), (me >> next_bit) & 1, me]).astype(jnp.int32)

    cell = np.arange(cells)
    own_ok = (tile_row * side + cell // side < page) & (tile_col * side + cell % side < page)
    own_mask = jnp.broadcast_to(jnp.where(own_ok, 0.0, MASKED).astype(F32), (8, cells))
    valid = own_ok.astype(F32)[:, None]
    slot = np.arange(sz.bk)[None] + np.arange(sz.blocks)[:, None] * sz.brows * sz.pitch - PAD + RADIUS
    key_row = tile_row * side + slot // sz.pitch - RADIUS
    key_col = tile_col * side + slot % sz.pitch - RADIUS
    is_class = (np.arange(sz.bk) == sz.class_slot)[None]
    key_ok = (key_row >= 0) & (key_row < page) & (key_col >= 0) & (key_col < page) | is_class
    key_mask = jnp.broadcast_to(
        jnp.where(key_ok, 0.0, MASKED).astype(F32)[:, :, None], (sz.blocks, sz.bk, sz.bk // 2)
    )
    lines = jnp.pad(rel_table.reshape(layers, heads, SPAN, SPAN), ((0, 0), (0, 16 - heads), (0, 0), (0, sz.pitch - SPAN)),
                    constant_values=MASKED).reshape(layers, 16, SPAN * sz.pitch)
    first_slot = PAD - RADIUS
    lines = jnp.pad(lines, ((0, 0), (0, 0), (first_slot, sz.bk - first_slot - SPAN * sz.pitch)), constant_values=MASKED)

    before = []

    def call(kernel, grid, in_specs, out_specs, out_shape, scratch=(), vmem=56, weight=1, also=()):
        deps = list(before) + list(also)
        count = len(in_specs)

        def body(*refs):
            return kernel(*refs[: 1 + count], *refs[1 + count + len(deps) :])

        run = pl.pallas_call(
            body,
            grid_spec=pltpu.PrefetchScalarGridSpec(
                num_scalar_prefetch=1,
                grid=grid,
                in_specs=list(in_specs) + [ANY] * len(deps),
                out_specs=out_specs,
                scratch_shapes=list(scratch),
            ),
            out_shape=out_shape,
            compiler_params=pltpu.CompilerParams(vmem_limit_bytes=vmem * MIB),
            cost_estimate=pl.CostEstimate(flops=weight, bytes_accessed=1, transcendentals=0),
        )

        def go(*args):
            pinned = [pltpu.with_memory_space_constraint(a, pltpu.HBM) for a in args]
            out = run(info, *pinned, *deps)
            before[:] = [out[-1] if isinstance(out, (list, tuple)) else out]
            return out

        return go

    def partner(value, x):
        return lax.ppermute(value, "tile", [(t, t ^ x) for t in range(tiles)])

    def exchange(rims):
        return [partner(v, x + 1) for x, v in enumerate(rims)]

    def swap(value, bit):
        if bit < 2:
            return partner(value, 1 << bit)
        return lax.ppermute(value, "dp", [(d, d ^ (1 << (bit - 2))) for d in range(pages)])

    def both(value):
        return value, partner(value, 1)

    def vm(dims, dtype):
        return pltpu.VMEM(dims, dtype)

    sems = pltpu.SemaphoreType.DMA((40,))
    row_w, par = whole((rows, width)), whole((layers, width))
    wide = whole((rows, 3 * width))
    pc_rows, pr_rows, pd_rows = side * PAD + 16, RADIUS * side + 16, (RADIUS + 1) * PAD + 16
    rim_shapes = [kept((n, 2 * width), BF) for n in (pc_rows, pr_rows, pd_rows)]
    rim_specs = [whole(s.shape) for s in rim_shapes]
    stat_spec = pl.BlockSpec((16, 2 * width), lambda *_: (side * PAD // 16, 0))
    nb, ng = sz.blocks, sz.groups
    square = (width, width)

    x, qkv, *rims = call(
        functools.partial(first_kernel, sz),
        (1,),
        [whole((cells, width)), whole((1, width)), par, whole((8, cells)), ANY],
        [row_w, wide] + rim_specs,
        [kept((rows, width), F32), kept((rows, 3 * width), BF)] + rim_shapes,
        [vm((rows, width), BF), vm((width, 3 * width), BF), sems],
    )(patch_in.reshape(cells, width), cls_in, norm_attn, own_mask, qkv_weight)
    got = exchange(rims)
    bias = call(
        lambda info, *refs: bias_kernel(sz, *refs),
        (layers,),
        [pl.BlockSpec((None, 16, sz.bk), lambda l, s: (l, 0, 0))],
        pl.BlockSpec((None, ng, sz.bk, sz.bk), lambda l, s: (l, 0, 0, 0)),
        kept((layers, ng, sz.bk, sz.bk), F32),
        [vm((sz.bk, sz.bk), F32)],
    )(lines)
    saved = []
    for l in range(layers):
        last = l == layers - 1
        ins = [wide, stat_spec] + rim_specs + [
            pl.BlockSpec((None, ng, sz.bk, sz.bk), lambda i, s, l=l: (l, 0, 0, 0)), whole(key_mask.shape), row_w,
            whole((8, cells)), par, par, par, par, ANY, ANY, ANY]
        args = [qkv, rims[0], *got, bias, key_mask, x, own_mask, scale_attn, norm_mlp, scale_mlp, norm_attn,
                out_weight, up_weight, down_weight]
        held = [((nb * ng, sz.bk, sz.bk), BF), ((nb, sz.bk, width), BF), ((nb, sz.bk, width), BF), ((rows, hidden), BF),
                ((rows, width), F32), ((rows, width), BF), ((rows, width), BF)]
        left_width = 2 * width + hidden + (0 if last else width) + (0 if l else width)
        scratch = [vm((sz.ext_rows, width), F32)] * 2 + [vm(square, BF), vm((width, hidden), BF), vm((hidden, width), BF)]
        scratch += [vm(d, t) for d, t in held]
        scratch += [vm((rows, width), BF), vm((rows, width), BF), vm((rows, hidden), BF), vm((rows, width), F32)]
        outs = [kept(d, t) for d, t in held] + [kept((rows, left_width), BF), kept((8, width), F32)]
        out_specs = [ANY] * (len(held) + 1) + [whole((8, width))]
        if last:
            ins += [whole((cells, width)), whole((1, width)), whole((cells, 1))]
            args += [patch_cot.reshape(cells, width), cls_cot, valid]
            out_specs += [whole((cells, width)), whole((1, width)), ANY, row_w, whole((8, width))]
            outs += [kept((cells, width), BF), kept((1, width), BF), kept((rows, 2 * width + hidden), BF),
                     kept((rows, width), F32), kept((8, width), F32)]
            scratch += [vm((rows, width), BF), vm((rows, hidden), BF), vm((rows, width), BF)]
        else:
            ins += [ANY]
            args += [qkv_weight]
            out_specs += [row_w, wide] + rim_specs
            outs += [kept((rows, width), F32), kept((rows, 3 * width), BF)] + rim_shapes
            scratch += [vm((width, 3 * width), BF), vm((rows, width), BF)]
        if l == 0:
            scratch += [vm((rows, width), BF)]
        out = call(functools.partial(middle_kernel, sz, l, last), (1,), ins, out_specs, outs, scratch + [sems],
                   )(*args)
        p, kb, vb, slope, x1, branch, down, left, stats = out[:9]
        saved.append(dict(x=x, qkv=qkv, p=p, kb=kb, vb=vb, slope=slope, x1=x1, branch=branch, down=down, stats=stats,
                          left=both(left), h=None))
        if l == 0:
            saved[0]["h"] = (saved[0]["left"], left_width // width - 1)
        else:
            saved[l]["h"] = (saved[l - 1]["left"], 2 + chunks)
        if last:
            patch_out, cls_out, right, g1, vec = out[9:]
        else:
            x, qkv, *rims = out[9:]
            got = exchange(rims)

    def attention_back(l, right, at, also):
        kept_l = saved[l]
        return call(
            functools.partial(attention_back_kernel, sz, l),
            (1,),
            [pl.BlockSpec((rows, width), lambda i, s: (0, at)), wide, whole((8, width)), whole((8, cells)), ANY, ANY, ANY, ANY],
            [whole((cells, width)), whole((cells, 2 * width))] + rim_specs + [whole((16, sz.bk))],
            [kept((cells, width), BF), kept((cells, 2 * width), F32)] + rim_shapes + [kept((16, sz.bk), F32)],
            [vm((sz.ext_rows, width), F32)] * 2 + [vm((rows, width), F32), vm((ng, sz.bk, sz.bk), F32), vm(square, BF),
             vm((nb * ng, sz.bk, sz.bk), BF), vm((nb, sz.bk, width), BF), vm((nb, sz.bk, width), BF), sems],
            also=also,
        )(right, kept_l["qkv"], kept_l["stats"], own_mask, out_weight, kept_l["p"], kept_l["kb"], kept_l["vb"])

    back_ins = [whole((cells, width)), whole((cells, 2 * width)), stat_spec] + rim_specs + [
        row_w, row_w, whole((8, width)), whole((16, sz.bk))]
    back_scratch = [vm((cells, 2 * width), F32), vm((rows, width), F32), vm((width, 3 * width), BF)]

    def qkv_back(l, d_q, d_kv, own, got, g1, vec, table):
        *e_qkv, rows_small, g = call(
            functools.partial(qkv_back_kernel, sz, l),
            (1,),
            back_ins + [par, ANY],
            [row_w, row_w, row_w, whole((24, width)), row_w],
            [kept((rows, width), BF)] * 3 + [kept((24, width), F32), kept((rows, width), F32)],
            back_scratch + [vm((rows, 3 * width), BF), sems],
            weight=LONG,
        )(d_q, d_kv, own, *got, saved[l]["x"], g1, vec, table, norm_attn, qkv_weight)
        return [both(e) for e in e_qkv], rows_small, g

    def mlp_back(l, g):
        low = saved[l]
        return call(
            functools.partial(mlp_back_kernel, sz, l),
            (1,),
            [row_w, par, par, par, row_w, row_w, row_w, ANY, ANY, ANY],
            [ANY, row_w, whole((8, width))],
            [kept((rows, 2 * width + hidden), BF), kept((rows, width), F32), kept((8, width), F32)],
            [vm((rows, width), F32), vm((width, hidden), BF), vm((hidden, width), BF), vm((rows, hidden), BF),
             vm((rows, width), BF), vm((rows, hidden), BF), vm((rows, width), BF), sems],
        )(g, norm_mlp, scale_attn, scale_mlp, low["x1"], low["branch"], low["down"], up_weight, down_weight, low["slope"])

    def finish(d_q, d_kv, own, got, g1, vec, table):
        return call(
            functools.partial(last_kernel, sz),
            (1,),
            back_ins + [par, ANY],
            [row_w, row_w, row_w, whole((24, width)), whole((cells, width)), whole((1, width))],
            [kept((rows, width), BF)] * 3 + [kept((24, width), F32), kept((cells, width), F32), kept((1, width), F32)],
            back_scratch + [vm((rows, 3 * width), BF), sems],
        )(d_q, d_kv, own, *got, saved[0]["x"], g1, vec, table, norm_attn, qkv_weight)

    piece, ff_piece = width // sz.devices, hidden // sz.devices
    half = width // 2
    quarter = sz.devices // 4

    def halves(start):
        return pl.BlockSpec((rows, half), lambda i, s: (0, 2 * start + s[1]))

    def grad_down(act, e_down, weight=1, also=()):
        lspec = pl.BlockSpec((rows, width), lambda i, s: (0, act[1] + s[1] * (chunks // 2) + i))
        rspec = pl.BlockSpec((rows, width), lambda i, s: (0, e_down[1]))
        out = pl.BlockSpec((None, quarter // 2, ff_piece, width), lambda i, s: (i ^ s[3], 0, 0, 0))
        return call(
            functools.partial(down_kernel, sz),
            (2,),
            [lspec, lspec, rspec, rspec],
            [out, out],
            [kept((2, quarter // 2, ff_piece, width), BF)] * 2,
            weight=weight, also=also,
        )(*act[0], *e_down[0])

    def grad_up(h2, e_up):
        lspec = halves(h2[1])
        rspec = pl.BlockSpec((rows, width), lambda i, s: (0, e_up[1] + i))
        out = pl.BlockSpec((quarter, None, piece, width), lambda i, s: (0, i, 0, 0))
        return call(
            functools.partial(up_kernel, sz),
            (chunks,),
            [lspec, lspec, rspec, rspec],
            [out, out],
            [kept((quarter, chunks, piece, width), BF)] * 2,
        )(*h2[0], *e_up[0])

    def grad_attn(h, e_qkv, att, e_branch, weight=1):
        def block(index):
            return pl.BlockSpec((quarter, None, piece, width), lambda i, s: (0, index(i), 0, 0))

        first, second = block(lambda i: jnp.minimum(i, 1)), block(lambda i: jnp.maximum(i - 2, 0))
        hspec, aspec = halves(h[1]), halves(att[1])
        bspec = pl.BlockSpec((rows, width), lambda i, s: (0, e_branch[1]))
        return call(
            functools.partial(attn_grad_kernel, sz),
            (4,),
            [hspec, hspec] + [row_w] * 6 + [aspec, aspec, bspec, bspec],
            [first, first, second, second],
            [kept((quarter, 2, piece, width), BF)] * 4,
            weight=weight,
        )(*h[0], *(v for pair in e_qkv for v in pair), *att[0], *e_branch[0])

    class Sums:
        def __init__(self, y_first, x_first, split):
            (s0, k0), (s1, k1) = y_first, x_first
            self.got = [swap(s0, 1), swap(s1, 2)]
            total = s0.size // width
            self.block = total // (quarter // 2)
            self.outer = split
            self.rows = total
            self.keep = [k0.reshape(1, 2, total // 2, width), k1.reshape(split, 2, total // 2 // split, width)]

        def second(self, weight=1):
            n = self.rows // 4
            got = [g.reshape(k.shape) for g, k in zip(self.got, self.keep)]
            sp = self.outer
            if sp == 1:
                other = pl.BlockSpec((1, 2, n, width), lambda i, s: (0, 0, i, 0))
                other_out = pl.BlockSpec((1, n, width), lambda i, s: (0, i, 0))
            else:
                other = pl.BlockSpec((1, 2, n, width), lambda i, s: (i, 0, 0, 0))
                other_out = pl.BlockSpec((1, n, width), lambda i, s: (i, 0, 0))
            spec = pl.BlockSpec((1, 2, n, width), lambda i, s: (0, 0, i, 0))
            spec_out = pl.BlockSpec((1, n, width), lambda i, s: (0, i, 0))
            s0, k0, s1, k1 = call(
                second_kernel, (2,), [spec, spec, other, other], [spec_out, spec_out, other_out, other_out],
                [kept((1, 2 * n, width), BF)] * 2 + [kept((sp, 2 * n // sp, width), BF)] * 2, weight=weight,
            )(self.keep[0], got[0], self.keep[1], got[1])
            self.got = [swap(s0, 2), swap(s1, 1)]
            self.keep = [k0, k1]
            self.rows //= 2

        def third(self, weight=1):
            n = self.rows // 2
            args = [v.reshape(2, n, width) for pair in zip(self.keep, self.got) for v in pair]
            s, k = call(
                third_kernel, (1,), [whole((2, n, width))] * 4, [whole((2, n, width))] * 2,
                [kept((2, n, width), BF)] * 2, weight=weight,
            )(*args)
            self.rows = n
            self.keep = k
            self.got = swap(s, bits - 2)
            for bit in range(bits - 3, 2, -1):
                n = self.rows // 2
                spec = whole((2, 2, n, width))
                s, k = call(
                    more_kernel, (1,), [spec, spec], [whole((2, n, width))] * 2, [kept((2, n, width), BF)] * 2,
                )(self.keep.reshape(2, 2, n, width), self.got.reshape(2, 2, n, width))
                self.rows = n
                self.keep = k
                self.got = swap(s, bit)

        def fourth(self):
            n = self.rows // 2
            spec = whole((2, 2, n, width))
            a, b = call(
                functools.partial(fourth_kernel, sz), (1,), [spec, spec], [whole((2, n, width))] * 2,
                [kept((2, n, width), BF)] * 2,
            )(self.keep.reshape(2, 2, n, width), self.got.reshape(2, 2, n, width))

            def route(flip):
                out = []
                for d in range(sz.devices):
                    high, core = d >> top_bit, d & 1
                    to = (d & ~(1 << top_bit) & ~1) | core << top_bit | (high ^ flip)
                    out.append((d, to))
                return out

            self.got = [lax.ppermute(a, ("dp", "tile"), route(0)), lax.ppermute(b, ("dp", "tile"), route(1))]

        def result(self):
            return self.got[0].astype(F32) + self.got[1].astype(F32)

    sums = {}
    small = [None] * layers
    early = [v["left"][1] for v in saved[:-1]]
    waiting = None
    for l in reversed(range(layers)):
        left = saved[l]["left"]
        if waiting is not None:
            quads = grad_attn(*waiting)
            sums["attn", l + 1] = Sums(quads[0:2], quads[2:4], 1)
        d_q, d_kv, *rims, table = attention_back(l, right, 1 + chunks, early)
        early = []
        if l + 1 < layers:
            right = both(lax.optimization_barrier((right, table))[0])
            got = exchange(rims)
            sums["mlp", l + 1].second()
            sums["attn", l + 1].second(LONG)
            x_first = grad_down((left, 2), (right, 0), 1, got)
        else:
            right = both(right)
            got = exchange(rims)
            x_first = grad_down((left, 2), (right, 0))
        y_first = grad_up((left, 1), (right, 1))
        sums["mlp", l] = Sums(y_first, x_first, 2)
        if l + 1 < layers:
            sums["mlp", l + 1].third(LONG)
            sums["attn", l + 1].third()
        if l > 0:
            e_qkv, small[l], g = qkv_back(l, d_q, d_kv, rims[0], got, g1, vec, table)
            waiting = (saved[l]["h"], e_qkv, (left, 0), (right, 1 + chunks))
            right, g1, vec = mlp_back(l - 1, g)
        else:
            *e_qkv, small[0], patch_grad, cls_grad = finish(d_q, d_kv, rims[0], got, g1, vec, table)
            waiting = (saved[0]["h"], [both(e) for e in e_qkv], (left, 0), (right, 1 + chunks))
    if layers > 1:
        sums["mlp", 1].fourth()
        sums["attn", 1].fourth()
    sums["mlp", 0].second(LONG)
    quads = grad_attn(*waiting)
    sums["attn", 0] = Sums(quads[0:2], quads[2:4], 1)
    total = jnp.stack(small)
    bit = 0
    for run in (sums["mlp", 0].third, sums["attn", 0].second, sums["mlp", 0].fourth, sums["attn", 0].third, sums["attn", 0].fourth):
        if bit < bits:
            total = lax.optimization_barrier((total, before[0]))[0]
            total = total + swap(total, bit)
            bit += 1
        run()
    for bit in range(bit, bits):
        total = total + swap(total, bit)
    ups, downs, firsts, seconds = [], [], [], []
    for l in range(layers):
        mlp, attn = sums["mlp", l].result(), sums["attn", l].result()
        ups.append(jnp.swapaxes(mlp[0].reshape(chunks, piece, width), 0, 1).reshape(piece, hidden))
        downs.append(mlp[1])
        attn = attn.reshape(4, piece, width)
        firsts.append(jnp.swapaxes(attn[:3], 0, 1).reshape(piece, 3 * width))
        seconds.append(attn[3])
    g_qkv, g_out, g_up, g_down = (jnp.stack(v) for v in (firsts, seconds, ups, downs))
    vectors, tables = total[:, 0:4], total[:, 8 : 8 + heads, 0 : sz.bk]
    mine = lax.dynamic_slice_in_dim(vectors, me * piece, piece, axis=2)
    tables = tables[:, :, first_slot : first_slot + SPAN * sz.pitch].reshape(layers, heads, SPAN, sz.pitch)
    g_table = tables[..., :SPAN].reshape(rel_table.shape)
    return (
        patch_out.reshape(patch_in.shape),
        cls_out,
        patch_grad.reshape(patch_in.shape),
        cls_grad,
        mine[:, 3],
        g_qkv,
        g_table,
        g_out,
        mine[:, 2],
        mine[:, 1],
        g_up,
        g_down,
        mine[:, 0],
    )


def solution(mesh):
    tokens = P("dp", "tile", None, None, None)
    split = ("dp", "tile")
    in_specs = (tokens, P("dp", None), P("dp")) + (P(),) * 9 + (tokens, P("dp", None))
    out_specs = (
        tokens,
        P("dp", None),
        tokens,
        P("dp", None),
        P(None, split),
        P(None, split, None),
        P(),
        P(None, split, None),
        P(None, split),
        P(None, split),
        P(None, split, None),
        P(None, split, None),
        P(None, split),
    )
    return jax.shard_map(local, mesh=mesh, in_specs=in_specs, out_specs=out_specs, check_vma=False)
```

```python
import functools

import jax
import jax.numpy as jnp
import numpy as np
from jax import lax
from jax.experimental import pallas as pl
from jax.experimental.pallas import tpu as pltpu
from jax.sharding import PartitionSpec as P

RADIUS = 3
SPAN = 2 * RADIUS + 1
PAD = 8
EPS = 1e-06
MASKED = -1e30
BF = jnp.bfloat16
F32 = jnp.float32
MIB = 1 << 20


def dot(a, b):
    return lax.dot_general(a, b, (((1,), (0,)), ((), ())), preferred_element_type=F32)


def dot_nt(a, b):
    return lax.dot_general(a, b, (((1,), (1,)), ((), ())), preferred_element_type=F32)


def dot_tn(a, b):
    return lax.dot_general(a, b, (((0,), (0,)), ((), ())), preferred_element_type=F32)


def normalized(x):
    centred = x - jnp.mean(x, axis=-1, keepdims=True)
    inverse = lax.rsqrt(jnp.mean(centred * centred, axis=-1, keepdims=True) + EPS)
    return centred * inverse, inverse


def norm_back(x, gain, d_out):
    unit, inverse = normalized(x)
    d_unit = d_out * gain
    d_x = inverse * (
        d_unit
        - jnp.mean(d_unit, axis=-1, keepdims=True)
        - unit * jnp.mean(d_unit * unit, axis=-1, keepdims=True)
    )
    return d_x, d_out * unit


def split3(x):
    high = x.astype(BF).astype(F32)
    rest = x - high
    middle = rest.astype(BF).astype(F32)
    return high, middle, rest - middle


def lane_heads(rows, lanes, width):
    return lax.broadcasted_iota(jnp.int32, (rows, lanes), 1) // width


def head_rows(rows, lanes, width):
    return lane_heads(rows, lanes, width) == lax.broadcasted_iota(jnp.int32, (rows, lanes), 0)


def stacked_heads(block, width):
    rows, lanes = block.shape
    heads = lane_heads(rows, lanes, width)
    zero = jnp.zeros_like(block)
    return jnp.concatenate(
        [jnp.where(heads == h, block, zero) for h in range(lanes // width)], axis=0
    )


def folded_heads(stack, width):
    count = stack.shape[1] // width
    rows = stack.shape[0] // count
    heads = lane_heads(rows, stack.shape[1], width)
    out = stack[:rows]
    for h in range(1, count):
        out = jnp.where(heads == h, stack[h * rows : (h + 1) * rows], out)
    return out


def keep_rows(rows, cells, class_weight):
    row = lax.broadcasted_iota(jnp.int32, (rows, 1), 0)
    return jnp.where(row < cells, 1.0, jnp.where(row == cells, class_weight, 0.0))


class Sizes:
    def __init__(self, side, width, hidden, heads, devices):
        self.side = side
        self.cells = side * side
        self.rows = self.cells + 16
        self.width = width
        self.hidden = hidden
        self.heads = heads
        self.head = width // heads
        self.pitch = side + PAD
        self.ext = side + 2 * RADIUS
        self.ext_rows = self.pitch * self.ext + PAD
        self.brows = 4
        self.blocks = side // self.brows
        self.bq = self.brows * side
        self.bk = 256
        self.class_slot = self.bk - PAD
        self.quad = 4 * self.head
        self.groups = width // self.quad
        self.devices = devices
        self.bits = devices.bit_length() - 1


def stat_rows(values):
    width = values[0].shape[1]
    parts = [split3(v) for v in values]
    flat = [p[k] for k in range(3) for p in parts]
    if len(flat) % 2:
        flat.append(jnp.zeros_like(flat[0]))
    row = lax.broadcasted_iota(jnp.int32, (16, 2 * width), 0)
    out = jnp.zeros((16, 2 * width), F32)
    for i in range(0, len(flat), 2):
        out = jnp.where(row == i // 2, jnp.concatenate(flat[i : i + 2], axis=1), out)
    return out.astype(BF)


def read_stats(block, count, width):
    rows = block.astype(F32)

    def piece(i):
        return rows[i // 2 : i // 2 + 1, (i % 2) * width : (i % 2 + 1) * width]

    return [piece(i) + piece(count + i) + piece(2 * count + i) for i in range(count)]


def in_tile_order(info, pieces):
    me = info[0] * 2 + info[1]
    out = []
    for t in range(4):
        d = me ^ t
        out.append(
            [
                jnp.where(d == 0, a, jnp.where(d == 1, b, jnp.where(d == 2, c, e)))
                for a, b, c, e in zip(*pieces)
            ]
        )
    return out


def class_scores(sz, info, qkv_ref, mask):
    cells, width = sz.cells, sz.width
    own = head_rows(16, width, sz.head)
    class_rows = qkv_ref[cells : cells + 16, :].astype(F32)
    q_c, k_c, v_c = (class_rows[0:1, i * width : (i + 1) * width] for i in range(3))
    q_heads = jnp.where(own, q_c, 0.0)
    scale = sz.head ** (-0.5)
    scores = dot_nt(q_heads.astype(BF), qkv_ref[0:cells, width : 2 * width]) * scale + mask
    self_score = jnp.sum(q_heads * k_c, axis=1, keepdims=True) * scale
    self_score = jnp.where(info[2] == 1, self_score, MASKED)
    return own, q_heads, k_c, v_c, scores, self_score


def send_rims(sz, info, kv_half, kv_edge_rows, stats, pc_ref, pr_ref, pd_ref):
    side, width = sz.side, sz.width
    cells8 = [kv_half(r) for r in range(side)]
    pc_ref[0 : side * PAD, :] = jnp.concatenate(cells8, axis=0).astype(BF)
    pc_ref[side * PAD : side * PAD + 16, :] = stats
    edge, corner = kv_edge_rows()
    pr_ref[0 : RADIUS * side, :] = jnp.concatenate(edge, axis=0).astype(BF)
    pr_ref[RADIUS * side : RADIUS * side + 16, :] = stats
    zero = jnp.zeros((PAD, 2 * width), F32)
    pd_ref[0 : (RADIUS + 1) * PAD, :] = jnp.concatenate(corner + [zero], axis=0).astype(BF)
    pd_ref[(RADIUS + 1) * PAD : (RADIUS + 1) * PAD + 16, :] = stats


def rim_places(sz, info):
    return sz.pitch * (1 - info[1]), (sz.side + RADIUS) * (1 - info[0])


GELU_C = float(np.sqrt(2.0 / np.pi))


class Copies:
    def __init__(self, sems):
        self.sems, self.count, self.out = sems, 0, []

    def load(self, src, dst):
        copy = pltpu.make_async_copy(src, dst, self.sems.at[self.count])
        self.count += 1
        copy.start()
        return copy

    def store(self, src, dst):
        self.out.append(self.load(src, dst))

    def finish(self):
        for copy in self.out:
            copy.wait()


def qkv_part(sz, info, x, gain, wq, loads, mask, h_ref, qkv_ref, pc_ref, pr_ref, pd_ref):
    width, side, cells = sz.width, sz.side, sz.cells
    unit, _ = normalized(x)
    h = (unit * gain).astype(BF)
    h_ref[...] = h
    for i in range(3):
        loads[i].wait()
        cols = slice(i * width, (i + 1) * width)
        qkv_ref[:, cols] = dot(h, wq[:, cols]).astype(BF)
    own, q_heads, k_c, v_c, scores, self_score = class_scores(sz, info, qkv_ref, mask)
    top = jnp.maximum(jnp.max(scores, axis=1, keepdims=True), self_score)
    probs = jnp.where(mask > -1.0, jnp.exp(scores - top), 0.0)
    self_prob = jnp.where(info[2] == 1, jnp.exp(self_score - top), 0.0)
    total = jnp.sum(probs, axis=1, keepdims=True) + self_prob
    part = dot(probs.astype(BF), qkv_ref[0:cells, 2 * width :]) + self_prob * v_c

    def to_row(v):
        return jnp.sum(jnp.where(own, v, 0.0), axis=0, keepdims=True)

    stats = stat_rows([to_row(part), to_row(top), to_row(total)])
    left_col = info[1] == 0

    def half(r):
        row = qkv_ref[r * side : (r + 1) * side, width:].astype(F32)
        return jnp.where(left_col, row[PAD:], row[:PAD])

    def edges():
        first = pl.multiple_of((1 - info[0]) * (side - RADIUS) * side, 16)
        rows = qkv_ref[pl.ds(first, RADIUS * side), width:].astype(F32)
        edge = [rows[t * side : (t + 1) * side] for t in range(RADIUS)]
        return edge, [jnp.where(left_col, e[PAD:], e[:PAD]) for e in edge]

    send_rims(sz, info, half, edges, stats, pc_ref, pr_ref, pd_ref)


def first_kernel(sz, info, patch_ref, cls_ref, gain_ref, mask_ref, w_any,
                 x_ref, qkv_ref, pc_ref, pr_ref, pd_ref, h_v, wq, sems):
    copies = Copies(sems)
    width = sz.width
    loads = [copies.load(w_any.at[0, :, pl.ds(i * width, width)], wq.at[:, pl.ds(i * width, width)]) for i in range(3)]
    row = lax.broadcasted_iota(jnp.int32, (16, width), 0)
    x_ref[0 : sz.cells, :] = patch_ref[...].astype(F32)
    x_ref[sz.cells :, :] = jnp.where(row == 0, cls_ref[...].astype(F32), 0.0)
    qkv_part(sz, info, x_ref[...], gain_ref[0:1, :], wq, loads, mask_ref[0:1, :], h_v, qkv_ref, pc_ref, pr_ref, pd_ref)


def extended(sz, info, qkv_ref, rc_ref, rr_ref, rd_ref, kext, vext):
    width, side, pitch = sz.width, sz.side, sz.pitch
    beside, above = rim_places(sz, info)
    for ext, lo in ((kext, width), (vext, 2 * width)):
        at = lo - width
        ext[...] = jnp.zeros_like(ext)
        for r in range(side):
            base = pitch * (r + RADIUS)
            ext[base + PAD : base + PAD + side, :] = qkv_ref[r * side : (r + 1) * side, lo : lo + width].astype(F32)
        sides = rc_ref[0 : side * PAD, at : at + width].astype(F32)
        for r in range(side):
            ext[pl.ds(pl.multiple_of(pitch * (r + RADIUS) + beside, 8), PAD), :] = sides[r * PAD : (r + 1) * PAD]
        edge = rr_ref[0 : RADIUS * side, at : at + width].astype(F32)
        corner = rd_ref[0 : (RADIUS + 1) * PAD, at : at + width].astype(F32)
        for t in range(RADIUS):
            base = pitch * (above + t)
            ext[pl.ds(pl.multiple_of(base + PAD, 8), side), :] = edge[t * side : (t + 1) * side]
            ext[pl.ds(pl.multiple_of(base + beside, 8), PAD), :] = corner[t * PAD : (t + 1) * PAD]


def all_stats(sz, info, st_ref, rc_ref, rr_ref, rd_ref):
    side, width = sz.side, sz.width
    return in_tile_order(info, [read_stats(r, 3, width) for r in (
        st_ref[side * PAD : side * PAD + 16, :],
        rc_ref[side * PAD : side * PAD + 16, :],
        rr_ref[RADIUS * side : RADIUS * side + 16, :],
        rd_ref[(RADIUS + 1) * PAD : (RADIUS + 1) * PAD + 16, :],
    )])


def middle_kernel(sz, layer, last, names, info, *refs):
    r = dict(zip(names, refs))
    qkv_ref, rc_ref, rr_ref, rd_ref = r["qkv"], r["rc"], r["rr"], r["rd"]
    st_ref, bias_ref, mask_ref, x_ref = r["pc"], r["bias"], r["mask"], r["x"]
    scale_a_ref, gain_m_ref, scale_m_ref, gain_a_ref = r["scale_a"], r["gain_m"], r["scale_m"], r["gain_a"]
    w_out, w_up, w_down, stat_ref = r["w_out"], r["w_up"], r["w_down"], r["stats"]
    p_v, kb_v, vb_v, slope_v, x1_v, br_v, down_v, left = (r[n] for n in ("p", "kb", "vb", "slope", "x1", "br", "down", "left"))
    kext, vext, acc = r["kext"], r["vext"], r["acc"]
    width, side, cells, pitch, hidden = sz.width, sz.side, sz.cells, sz.pitch, sz.hidden
    chunks = hidden // width
    copies = Copies(r["sems"])

    def hold(name, cols=None):
        if not last:
            src, dst = r[name], r[name + "_out"]
            if cols is not None:
                at = pl.ds(cols[0], cols[1])
                src, dst = src.at[:, at], dst.at[:, at]
            copies.store(src, dst)

    if not last:
        qkv_loads = [
            copies.load(r["qkv_w"].at[layer + 1, :, pl.ds(i * width, width)], r["w_qkv"].at[:, pl.ds(i * width, width)])
            for i in range(3)
        ]
        hold("qkv")
    extended(sz, info, qkv_ref, rc_ref, rr_ref, rd_ref, kext, vext)
    if layer == 0:
        left[:, left.shape[1] - width :] = (normalized(x_ref[...])[0] * gain_a_ref[0:1, :]).astype(BF)
    class_rows = qkv_ref[cells : cells + 16, :].astype(F32)[0:PAD]
    scale = sz.head ** (-0.5)
    for b in range(sz.blocks):
        first = b * sz.brows * pitch
        kb = jnp.concatenate([kext[first : first + sz.class_slot, :], class_rows[:, width : 2 * width]], axis=0).astype(BF)
        vb = jnp.concatenate([vext[first : first + sz.class_slot, :], class_rows[:, 2 * width :]], axis=0).astype(BF)
        kb_v[b] = kb
        vb_v[b] = vb
        q = qkv_ref[b * sz.bq : (b + 1) * sz.bq, 0:width] * jnp.asarray(scale, BF)
        mask = mask_ref[b]
        mask = jnp.concatenate([mask, mask], axis=1)
        for g in range(sz.groups):
            lanes = slice(g * sz.quad, (g + 1) * sz.quad)
            scores = dot_nt(kb[:, lanes], stacked_heads(q[:, lanes], sz.head)) + bias_ref[layer, g] + mask
            top = jnp.max(scores, axis=0, keepdims=True)
            probs = jnp.exp(scores - top)
            total = jnp.sum(probs, axis=0, keepdims=True)
            probs = (probs * (1.0 / total)).astype(BF)
            p_v[b * sz.groups + g] = probs
            out = folded_heads(dot_tn(probs, vb[:, lanes]), sz.head)
            left[b * sz.bq : (b + 1) * sz.bq, lanes] = out.astype(BF)
    for name in ("p", "kb", "vb"):
        hold(name)
    ordered = all_stats(sz, info, st_ref, rc_ref, rr_ref, rd_ref)
    top = functools.reduce(jnp.maximum, [s[1] for s in ordered])
    total = jnp.zeros_like(top)
    summed = jnp.zeros_like(top)
    for part, part_top, part_total in ordered:
        factor = jnp.exp(part_top - top)
        total = total + part_total * factor
        summed = summed + part * factor
    class_out = summed / total
    stat_ref[...] = jnp.zeros_like(stat_ref)
    stat_ref[0:1, :] = top
    stat_ref[1:2, :] = total
    stat_ref[2:3, :] = class_out
    row = lax.broadcasted_iota(jnp.int32, (16, width), 0)
    left[cells : cells + 16, 0:width] = jnp.where(row == 0, class_out, 0.0).astype(BF)
    branch = dot(left[:, 0:width], w_out[...])
    br_v[...] = branch.astype(BF)
    x1_v[...] = x_ref[...] + scale_a_ref[layer : layer + 1, :] * branch
    unit, _ = normalized(x1_v[...])
    left[:, width : 2 * width] = (unit * gain_m_ref[layer : layer + 1, :]).astype(BF)
    hold("br")
    hold("x1")
    hold("left", (0, 2 * width))
    for c in range(chunks):
        at = slice(c * width, (c + 1) * width)
        u = dot(left[:, width : 2 * width], w_up[:, at])
        square = u * u
        th = jnp.tanh(GELU_C * u * (1.0 + 0.044715 * square))
        half = 0.5 * (1.0 + th)
        here = slice((c + 2) * width, (c + 3) * width)
        left[:, here] = (u * half).astype(BF)
        slope = half + (0.5 * u) * (1.0 - th * th) * (GELU_C + (3 * 0.044715 * GELU_C) * square)
        slope_v[:, at] = slope.astype(BF)
        part = dot(left[:, here], w_down[at, :])
        if c == 0:
            acc[...] = part
        else:
            acc[...] += part
    down_v[...] = acc[...].astype(BF)
    hold("slope")
    hold("down")
    hold("left", (2 * width, hidden))
    x2 = x1_v[...] + scale_m_ref[layer : layer + 1, :] * acc[...]
    if last:
        valid_ref, vec_ref = r["valid"], r["vec"]
        r["patch_out"][...] = (x2[0:cells] * valid_ref[...]).astype(BF)
        r["cls_out"][...] = x2[cells : cells + 1].astype(BF)
        g_cells = r["cot"][...].astype(F32) * valid_ref[...]
        g_class = jnp.where(row == 0, r["cls_cot"][...].astype(F32), 0.0)
        g = jnp.concatenate([g_cells, g_class], axis=0)
        keep = keep_rows(sz.rows, cells, jnp.where(info[2] == 1, 1.0, 0.0))
        vec_ref[...] = jnp.zeros_like(vec_ref)
        mlp_back_part(sz, layer, g, acc[...], keep, r["right"], r["g1"], vec_ref, x1_v, br_v, slope_v,
                      w_up, w_down, gain_m_ref, scale_a_ref, scale_m_ref, acc)
    else:
        r["x2"][...] = x2
        qkv_part(sz, info, x2, gain_a_ref[layer + 1 : layer + 2, :], r["w_qkv"], qkv_loads, r["own_mask"][0:1, :],
                 left.at[:, pl.ds(2 * width + hidden, width)], r["next"], r["pc_out"], r["pr_out"], r["pd_out"])
        hold("left", (2 * width + hidden, left.shape[1] - 2 * width - hidden))
    copies.finish()


def mlp_back_part(sz, layer, g, down, keep, right, g1_ref, vec_ref, x1_ref, br_ref, slope_ref,
                  w_up, w_down, gain_m_ref, scale_a_ref, scale_m_ref, acc):
    width = sz.width
    vec_ref[0:1, :] = jnp.sum(keep * g * down, axis=0, keepdims=True)
    right[:, 0:width] = (scale_m_ref[layer : layer + 1, :] * g).astype(BF)
    g1_ref[...] = g
    for c in range(sz.hidden // width):
        at = slice(c * width, (c + 1) * width)
        e_up = (dot_nt(right[:, 0:width], w_down[at, :]) * slope_ref[:, at].astype(F32)).astype(BF)
        here = slice((c + 1) * width, (c + 2) * width)
        right[:, here] = e_up
        part = dot_nt(right[:, here], w_up[:, at])
        if c == 0:
            acc[...] = part
        else:
            acc[...] += part
    d_x1, gain_rows = norm_back(x1_ref[...], gain_m_ref[layer : layer + 1, :], acc[...])
    vec_ref[1:2, :] = jnp.sum(keep * gain_rows, axis=0, keepdims=True)
    g1 = g1_ref[...] + d_x1
    g1_ref[...] = g1
    right[:, width + sz.hidden :] = (scale_a_ref[layer : layer + 1, :] * g1).astype(BF)
    vec_ref[2:3, :] = jnp.sum(keep * g1 * br_ref[...].astype(F32), axis=0, keepdims=True)


def attention_back_kernel(sz, layer, info, right, qkv_ref, stat_ref, own_mask_ref, p_v, kb_v, vb_v, w,
                          dq_ref, dkv_ref, pc_ref, pr_ref, pd_ref, tab_ref,
                          kext, vext, d_o, tab):
    width, side, cells, pitch = sz.width, sz.side, sz.cells, sz.pitch
    scale = sz.head ** (-0.5)
    kext[...] = jnp.zeros_like(kext)
    vext[...] = jnp.zeros_like(vext)
    d_o[...] = dot_nt(right[:, right.shape[1] - width :], w[...])
    class_k = [jnp.zeros((PAD, sz.quad), F32) for _ in range(sz.groups)]
    class_v = [jnp.zeros((PAD, sz.quad), F32) for _ in range(sz.groups)]
    for b in range(sz.blocks):
        first = b * sz.brows * pitch
        q = qkv_ref[b * sz.bq : (b + 1) * sz.bq, 0:width] * jnp.asarray(scale, BF)
        do = d_o[b * sz.bq : (b + 1) * sz.bq, :].astype(BF)
        for g in range(sz.groups):
            lanes = slice(g * sz.quad, (g + 1) * sz.quad)
            do_stack = stacked_heads(do[:, lanes], sz.head)
            q_stack = stacked_heads(q[:, lanes], sz.head)
            probs = p_v[b * sz.groups + g]
            wide = probs.astype(F32)
            d_prob = dot_nt(vb_v[b, :, lanes], do_stack)
            delta = jnp.sum(wide * d_prob, axis=0, keepdims=True)
            d_score = wide * (d_prob - delta)
            if b == 0:
                tab[g] = d_score
            else:
                tab[g] += d_score
            low = d_score.astype(BF)
            d_v = dot(probs, do_stack)
            d_k = dot(low, q_stack)
            vext[first : first + sz.class_slot, lanes] += d_v[: sz.class_slot]
            kext[first : first + sz.class_slot, lanes] += d_k[: sz.class_slot]
            class_v[g] = class_v[g] + d_v[sz.class_slot :]
            class_k[g] = class_k[g] + d_k[sz.class_slot :]
            d_q = folded_heads(dot_tn(low, kb_v[b, :, lanes]), sz.head) * scale
            dq_ref[b * sz.bq : (b + 1) * sz.bq, lanes] = d_q.astype(BF)
    mask = own_mask_ref[0:1, :]
    own, q_heads, k_c, v_c, scores, self_score = class_scores(sz, info, qkv_ref, mask)
    top = jnp.max(jnp.where(own, stat_ref[0:1, :], MASKED), axis=1, keepdims=True)
    total = jnp.max(jnp.where(own, stat_ref[1:2, :], 0.0), axis=1, keepdims=True)
    real = lax.broadcasted_iota(jnp.int32, (16, 1), 0) < sz.heads
    probs = jnp.where((mask > -1.0) & real, jnp.exp(scores - top) / total, 0.0)
    self_prob = jnp.where((info[2] == 1) & real, jnp.exp(self_score - top) / total, 0.0)
    d_class = jnp.where(own, d_o[cells : cells + 1, :], 0.0)
    delta = jnp.sum(d_class * stat_ref[2:3, :], axis=1, keepdims=True)
    d_low = d_class.astype(BF)
    d_cell = probs * (dot_nt(d_low, qkv_ref[0:cells, 2 * width :]) - delta)
    d_cell_low = d_cell.astype(BF)
    d_self = self_prob * (jnp.sum(d_class * v_c, axis=1, keepdims=True) - delta)

    def to_row(v):
        return jnp.sum(jnp.where(own, v, 0.0), axis=0, keepdims=True)

    g_q = to_row(dot(d_cell_low, qkv_ref[0:cells, width : 2 * width]) + d_self * k_c) * scale
    g_k = to_row(d_self * q_heads) * scale + jnp.concatenate([c[0:1] for c in class_k], axis=1)
    g_v = to_row(self_prob * d_class) + jnp.concatenate([c[0:1] for c in class_v], axis=1)
    add_k = dot_tn(d_cell_low, q_heads.astype(BF)) * scale
    add_v = dot_tn(probs.astype(BF), d_low)
    beside, above = rim_places(sz, info)
    for r in range(side):
        base = pitch * (r + RADIUS) + PAD
        rows = slice(r * side, (r + 1) * side)
        dkv_ref[rows, 0:width] = kext[base : base + side, :] + add_k[rows]
        dkv_ref[rows, width:] = vext[base : base + side, :] + add_v[rows]

    def pair(at, count):
        at = pl.ds(pl.multiple_of(at, 8), count)
        return jnp.concatenate([kext[at, :], vext[at, :]], axis=1)

    def edges():
        return (
            [pair(pitch * (above + t) + PAD, side) for t in range(RADIUS)],
            [pair(pitch * (above + t) + beside, PAD) for t in range(RADIUS)],
        )

    send_rims(sz, info, lambda r: pair(pitch * (r + RADIUS) + beside, PAD), edges,
              stat_rows([g_q, g_k, g_v]), pc_ref, pr_ref, pd_ref)
    per_head = sz.bq
    for g in range(sz.groups):
        turned = tab[g].T
        for h in range(4):
            total_h = jnp.zeros((side, sz.bk), F32)
            for r in range(sz.brows):
                at = h * per_head + r * side
                piece = turned[at : at + side]
                shift = (sz.bk - pitch * r) % sz.bk
                total_h = total_h + (pltpu.roll(piece, shift, 1) if shift else piece)
            tab_row = jnp.zeros((1, sz.bk), F32)
            for c in range(side):
                one = total_h[c : c + 1]
                tab_row = tab_row + (pltpu.roll(one, sz.bk - c, 1) if c else one)
            tab_ref[4 * g + h : 4 * g + h + 1, :] = tab_row
    tab_ref[sz.heads : 16, :] = jnp.zeros((16 - sz.heads, sz.bk), F32)


def qkv_back_part(sz, info, dq_ref, dkv_ref, st_ref, rc_ref, rr_ref, rd_ref, x_ref, gain, g1_ref, eq_ref, dkv, acc, wq):
    width, side, cells = sz.width, sz.side, sz.cells
    dkv[...] = dkv_ref[...]
    beside = PAD * (1 - info[1])
    edge = (1 - info[0]) * (side - RADIUS) * side
    sides = rc_ref[0 : side * PAD, :].astype(F32)
    for r in range(side):
        dkv[pl.ds(pl.multiple_of(r * side + beside, 8), PAD), :] += sides[r * PAD : (r + 1) * PAD]
    dkv[pl.ds(pl.multiple_of(edge, 8), RADIUS * side), :] += rr_ref[0 : RADIUS * side, :].astype(F32)
    corner = rd_ref[0 : (RADIUS + 1) * PAD, :].astype(F32)
    for t in range(RADIUS):
        dkv[pl.ds(pl.multiple_of(edge + t * side + beside, 8), PAD), :] += corner[t * PAD : (t + 1) * PAD]
    ordered = all_stats(sz, info, st_ref, rc_ref, rr_ref, rd_ref)
    class_row = jnp.concatenate(
        [functools.reduce(lambda a, b: a + b, [o[i] for o in ordered]) for i in range(3)], axis=1
    )
    row = lax.broadcasted_iota(jnp.int32, (16, 3 * width), 0)
    eq_ref[0:cells, 0:width] = dq_ref[...]
    eq_ref[0:cells, width:] = dkv[...].astype(BF)
    eq_ref[cells : cells + 16, :] = jnp.where(row == 0, class_row, 0.0).astype(BF)
    for i in range(3):
        cols = slice(i * width, (i + 1) * width)
        part = dot_nt(eq_ref[:, cols], wq[:, cols])
        if i == 0:
            acc[...] = part
        else:
            acc[...] += part
    d_x, gain_rows = norm_back(x_ref[...], gain, acc[...])
    return g1_ref[...] + d_x, gain_rows


def small_rows(sz, small_ref, vec_ref, tab_ref, gain_sum):
    small_ref[...] = jnp.zeros_like(small_ref)
    small_ref[0:3, :] = vec_ref[0:3, :]
    small_ref[3:4, :] = gain_sum
    small_ref[8:24, 0 : sz.bk] = tab_ref[...]


def qkv_back_kernel(sz, layer, info, dq_ref, dkv_ref, st_ref, rc_ref, rr_ref, rd_ref, x_ref, g1_ref, vec_ref, tab_ref,
                    gain_a_ref, wq, eq_ref, ek_ref, ev_ref, small_ref, g_ref, dkv, acc, eq_v):
    width = sz.width
    g, gain_rows = qkv_back_part(sz, info, dq_ref, dkv_ref, st_ref, rc_ref, rr_ref, rd_ref, x_ref,
                                 gain_a_ref[layer : layer + 1, :], g1_ref, eq_v, dkv, acc, wq)
    for i, ref in enumerate((eq_ref, ek_ref, ev_ref)):
        ref[...] = eq_v[:, i * width : (i + 1) * width]
    keep = keep_rows(sz.rows, sz.cells, jnp.where(info[2] == 1, 1.0, 0.0))
    small_rows(sz, small_ref, vec_ref, tab_ref, jnp.sum(keep * gain_rows, axis=0, keepdims=True))
    g_ref[...] = g


def mlp_back_kernel(sz, layer, info, g_ref, gain_m_ref, scale_a_ref, scale_m_ref, x1_ref, br_ref, down_ref,
                    slope_ref, w_up, w_down, right, g1_out, vec_out, acc):
    keep = keep_rows(sz.rows, sz.cells, jnp.where(info[2] == 1, 1.0, 0.0))
    vec_out[...] = jnp.zeros_like(vec_out)
    mlp_back_part(sz, layer, g_ref[...], down_ref[...].astype(F32), keep, right, g1_out, vec_out,
                  x1_ref, br_ref, slope_ref, w_up, w_down, gain_m_ref, scale_a_ref, scale_m_ref, acc)


def last_kernel(sz, info, dq_ref, dkv_ref, st_ref, rc_ref, rr_ref, rd_ref, patch_ref, cls_ref, g1_ref, vec_ref, tab_ref,
                gain_a_ref, wq, eq_ref, ek_ref, ev_ref, small_ref, pg_ref, cg_ref, dkv, acc, x_ref, eq_v):
    width = sz.width
    row = lax.broadcasted_iota(jnp.int32, (16, width), 0)
    x_ref[0 : sz.cells, :] = patch_ref[...].astype(F32)
    x_ref[sz.cells :, :] = jnp.where(row == 0, cls_ref[...].astype(F32), 0.0)
    g, gain_rows = qkv_back_part(sz, info, dq_ref, dkv_ref, st_ref, rc_ref, rr_ref, rd_ref, x_ref,
                                 gain_a_ref[0:1, :], g1_ref, eq_v, dkv, acc, wq)
    for i, ref in enumerate((eq_ref, ek_ref, ev_ref)):
        ref[...] = eq_v[:, i * width : (i + 1) * width]
    keep = keep_rows(sz.rows, sz.cells, jnp.where(info[2] == 1, 1.0, 0.0))
    small_rows(sz, small_ref, vec_ref, tab_ref, jnp.sum(keep * gain_rows, axis=0, keepdims=True))
    pg_ref[...] = g[0 : sz.cells]
    cg_ref[...] = g[sz.cells : sz.cells + 1]


def product(sz, info, left_ref, left_got, own_ref, other_ref):
    cells = sz.cells
    row = lax.broadcasted_iota(jnp.int32, (16, own_ref.shape[1]), 0)
    tail = own_ref[cells : cells + 16, :]
    tail = jnp.where((row < 0) | (info[0] == 0), tail, jnp.zeros_like(tail))
    left = jnp.concatenate([left_ref[0:cells, :], left_got[0:cells, :], left_ref[cells : cells + 16, :]], axis=0)
    right = jnp.concatenate([own_ref[0:cells, :], other_ref[0:cells, :], tail], axis=0)
    return dot_tn(left, right)


def store_pieces(value, count, pairs, bit, place, send_ref, keep_ref):
    per = value.shape[0] // count
    for a, b in pairs:
        one, two = value[a * per : (a + 1) * per], value[b * per : (b + 1) * per]
        at = place(a)
        keep_ref[at] = jnp.where(bit == 0, one, two).astype(BF)
        send_ref[at] = jnp.where(bit == 0, two, one).astype(BF)


def pairs_of(bits, bit):
    return [(a, a | 1 << bit) for a in range(1 << bits) if not a >> bit & 1]


def order_of(bits, skip, first):
    def place(a, me):
        names = list(first) + [b for b in range(bits - 1, -1, -1) if b != skip and b not in first]
        at = 0
        for b in names:
            mine = (a >> b) & 1
            at = at * 2 + (mine if b == 0 else mine ^ ((me >> b) & 1))
        return at

    return place


def down_kernel(sz, info, act_ref, act_got, own_ref, other_ref, send_ref, keep_ref):
    bits = sz.bits - 2
    me = info[4]
    value = product(sz, info, act_ref, act_got, own_ref, other_ref)
    place = order_of(bits, 2, (1,))
    store_pieces(value, 1 << bits, pairs_of(bits, 2), (me >> 2) & 1, lambda a: place(a, me), send_ref, keep_ref)


def columns_step(sz, info, bit, order, value, send_ref, keep_ref):
    bits = sz.bits - 1
    me = info[4]
    place = order_of(bits, bit, order)
    store_pieces(value, 1 << bits, pairs_of(bits, bit), (me >> bit) & 1, lambda a: place(a, me), send_ref, keep_ref)


def up_kernel(sz, info, h_ref, h_got, own_ref, other_ref, send_ref, keep_ref):
    columns_step(sz, info, 1, (2,), product(sz, info, h_ref, h_got, own_ref, other_ref), send_ref, keep_ref)


def attn_grad_kernel(sz, info, h_ref, h_got, qo, qg, ko, kg, vo, vg, a_ref, a_got, bo, bg, send_ref, keep_ref):
    step = pl.program_id(0)
    bit = sz.bits - 2
    cases = [(h_ref, h_got, qo, qg, (1, 2)), (h_ref, h_got, ko, kg, (1, 2)), (h_ref, h_got, vo, vg, (2, 1)),
             (a_ref, a_got, bo, bg, (2, 1))]
    for i, (*factors, order) in enumerate(cases):
        @pl.when(step == i)
        def _():
            columns_step(sz, info, bit, order, product(sz, info, *factors), send_ref, keep_ref)


def plus(a, b):
    return a.astype(F32) + b.astype(F32)


def second_kernel(info, k0, g0, k1, g1, s0_ref, k0_ref, s1_ref, k1_ref):
    s0_ref[...] = plus(k0[:, 1], g0[:, 1]).astype(BF)
    k0_ref[...] = plus(k0[:, 0], g0[:, 0]).astype(BF)
    s1_ref[...] = plus(k1[:, 1], g1[:, 1]).astype(BF)
    k1_ref[...] = plus(k1[:, 0], g1[:, 0]).astype(BF)


def third_kernel(info, k0, g0, k1, g1, s_ref, k_ref):
    s_ref[0] = plus(k0[1], g0[1]).astype(BF)
    k_ref[0] = plus(k0[0], g0[0]).astype(BF)
    s_ref[1] = plus(k1[1], g1[1]).astype(BF)
    k_ref[1] = plus(k1[0], g1[0]).astype(BF)


def more_kernel(info, k, g, s_ref, k_ref):
    s_ref[...] = plus(k[:, 1], g[:, 1]).astype(BF)
    k_ref[...] = plus(k[:, 0], g[:, 0]).astype(BF)


def z_second_kernel(info, k, g, s0_ref, s1_ref, k_ref):
    for i, ref in enumerate((s0_ref, s1_ref)):
        ref[...] = plus(k[i, 1], g[i, 1]).astype(BF)
        k_ref[i] = plus(k[i, 0], g[i, 0]).astype(BF)


def z_third_kernel(info, k, g0, g1, s0_ref, s1_ref, k_ref):
    for i, (g, ref) in enumerate(((g0, s0_ref), (g1, s1_ref))):
        ref[...] = plus(k[i, 1], g[1]).astype(BF)
        k_ref[i] = plus(k[i, 0], g[0]).astype(BF)


def z_fourth_kernel(sz, info, k, g0, g1, a_ref, b_ref):
    high = (info[4] >> (sz.bits - 1)) & 1
    for i, g in enumerate((g0, g1)):
        one, two = plus(k[i, 0], g[0]), plus(k[i, 1], g[1])
        a_ref[i] = jnp.where(high == 0, one, two).astype(BF)
        b_ref[i] = jnp.where(high == 0, two, one).astype(BF)


def fourth_kernel(sz, info, k, g, a_ref, b_ref):
    high = (info[4] >> (sz.bits - 1)) & 1
    one, two = plus(k[:, 0], g[:, 0]), plus(k[:, 1], g[:, 1])
    a_ref[...] = jnp.where(high == 0, one, two).astype(BF)
    b_ref[...] = jnp.where(high == 0, two, one).astype(BF)


def bias_kernel(sz, table_ref, out_ref, wide):
    slot = lax.broadcasted_iota(jnp.int32, (sz.side, sz.bk), 1)
    for g in range(sz.groups):
        for h in range(4):
            line = jnp.broadcast_to(table_ref[4 * g + h : 4 * g + h + 1, :], (sz.side, sz.bk))
            line = pltpu.roll(line, 0, 1, stride=1, stride_axis=0)
            for r in range(sz.brows):
                piece = pltpu.roll(line, sz.pitch * r, 1) if r else line
                at = h * sz.bq + r * sz.side
                wide[at : at + sz.side, :] = jnp.where(slot == sz.class_slot, 0.0, piece)
        out_ref[g] = wide[...].T


def shape(dims, dtype):
    return jax.ShapeDtypeStruct(dims, dtype)


def kept(dims, dtype):
    return pltpu.HBM(dims, dtype)


def inside(dims, dtype):
    return pltpu.VMEM(dims, dtype)


def whole(dims):
    return pl.BlockSpec(dims, lambda *_: (0,) * len(dims))


IN = pl.BlockSpec(memory_space=pltpu.VMEM)


ANY = pl.BlockSpec(memory_space=pl.ANY)
MEDIUM = 4 * 10**9
LONG = 10**11


def local(patch_in, cls_in, page_side, norm_attn, qkv_weight, rel_table, out_weight, scale_attn,
          norm_mlp, up_weight, down_weight, scale_mlp, patch_cot, cls_cot):
    tiles = lax.axis_size("tile")
    pages = lax.axis_size("dp")
    layers, heads = rel_table.shape[:2]
    sz = Sizes(patch_in.shape[2], patch_in.shape[4], up_weight.shape[2], heads, tiles * pages)
    side, cells, rows, width, hidden = sz.side, sz.cells, sz.rows, sz.width, sz.hidden
    chunks = hidden // width
    tile = lax.axis_index("tile")
    me = lax.axis_index("dp") * tiles + tile
    tile_row, tile_col = tile // 2, tile % 2
    page = page_side[0]
    bits = sz.bits
    top_bit, next_bit = bits - 1, bits - 2
    info = jnp.stack([tile_row, tile_col, (tile == 0).astype(jnp.int32), (me >> next_bit) & 1, me]).astype(jnp.int32)

    cell = np.arange(cells)
    own_ok = (tile_row * side + cell // side < page) & (tile_col * side + cell % side < page)
    own_mask = jnp.broadcast_to(jnp.where(own_ok, 0.0, MASKED).astype(F32), (8, cells))
    valid = own_ok.astype(F32)[:, None]
    slot = np.arange(sz.bk)[None] + np.arange(sz.blocks)[:, None] * sz.brows * sz.pitch - PAD + RADIUS
    key_row = tile_row * side + slot // sz.pitch - RADIUS
    key_col = tile_col * side + slot % sz.pitch - RADIUS
    is_class = (np.arange(sz.bk) == sz.class_slot)[None]
    key_ok = (key_row >= 0) & (key_row < page) & (key_col >= 0) & (key_col < page) | is_class
    key_mask = jnp.broadcast_to(
        jnp.where(key_ok, 0.0, MASKED).astype(F32)[:, :, None], (sz.blocks, sz.bk, sz.bk // 2)
    )
    lines = jnp.pad(rel_table.reshape(layers, heads, SPAN, SPAN), ((0, 0), (0, 16 - heads), (0, 0), (0, sz.pitch - SPAN)),
                    constant_values=MASKED).reshape(layers, 16, SPAN * sz.pitch)
    first_slot = PAD - RADIUS
    lines = jnp.pad(lines, ((0, 0), (0, 0), (first_slot, sz.bk - first_slot - SPAN * sz.pitch)), constant_values=MASKED)

    resident = {}
    before = []

    def call(kernel, grid, in_specs, out_specs, out_shape, scratch=(), vmem=12, weight=1, also=(), place=pltpu.HBM, ahead=()):
        deps = list(before) + list(also)
        count = len(in_specs)

        results = list(out_shape) if isinstance(out_shape, (list, tuple)) else [out_shape]
        result_specs = list(out_specs) if isinstance(out_specs, (list, tuple)) else [out_specs]
        more, own = len(ahead), len(results)

        def body(*refs):
            refs = list(refs)
            mine, refs = refs[: 1 + count], refs[1 + count + len(deps) :]
            sources, refs = refs[:more], refs[more:]
            made, refs = refs[:own], refs[own:]
            targets, refs = refs[:more], refs[more:]
            if not more:
                return kernel(*mine, *made, *refs)
            sem = refs.pop()
            copies = [
                pltpu.make_async_copy(src if index is None else src.at[index], dst, sem.at[n])
                for n, (src, dst, (_, index)) in enumerate(zip(sources, targets, ahead))
            ]

            @pl.when(pl.program_id(0) == 0)
            def _():
                for copy in copies:
                    copy.start()

            kernel(*mine, *made, *refs)

            @pl.when(pl.program_id(0) == pl.num_programs(0) - 1)
            def _():
                for copy in copies:
                    copy.wait()

        results += [inside(a.shape if index is None else a.shape[1:], a.dtype) for a, index in ahead]
        if more:
            scratch = list(scratch) + [pltpu.SemaphoreType.DMA((more,))]

        run = pl.pallas_call(
            body,
            grid_spec=pltpu.PrefetchScalarGridSpec(
                num_scalar_prefetch=1,
                grid=grid,
                in_specs=list(in_specs) + [ANY] * (len(deps) + more),
                out_specs=result_specs + [IN] * more,
                scratch_shapes=list(scratch),
            ),
            out_shape=results,
            compiler_params=pltpu.CompilerParams(vmem_limit_bytes=vmem * MIB),
            cost_estimate=pl.CostEstimate(flops=weight, bytes_accessed=1, transcendentals=0),
        )

        def go(*args):
            pinned = []
            for a, spec in zip(args, in_specs):
                if id(a) in resident:
                    a = pltpu.with_memory_space_constraint(a, pltpu.VMEM)
                elif spec is not IN and place is not None:
                    a = pltpu.with_memory_space_constraint(a, pltpu.HBM if spec is ANY else place)
                pinned.append(a)
            sources = [pltpu.with_memory_space_constraint(a, pltpu.HBM) for a, _ in ahead]
            out = run(info, *pinned, *deps, *sources)
            for a, like in zip(out, results):
                if not isinstance(like, jax.ShapeDtypeStruct) and like.memory_space == pltpu.VMEM:
                    resident[id(a)] = a
            before[:] = [out[own - 1]]
            return out if len(results) > 1 else out[0]

        return go

    def partner(value, x):
        return lax.ppermute(value, "tile", [(t, t ^ x) for t in range(tiles)])

    def exchange(rims):
        return [partner(v, x + 1) for x, v in enumerate(rims)]

    def swap(value, bit):
        if bit < 2:
            return partner(value, 1 << bit)
        return lax.ppermute(value, "dp", [(d, d ^ (1 << (bit - 2))) for d in range(pages)])

    def both(value):
        return value, partner(value, 1)

    def vm(dims, dtype):
        return pltpu.VMEM(dims, dtype)

    sems = pltpu.SemaphoreType.DMA((40,))
    row_w, par = whole((rows, width)), whole((layers, width))
    wide = whole((rows, 3 * width))
    pc_rows, pr_rows, pd_rows = side * PAD + 16, RADIUS * side + 16, (RADIUS + 1) * PAD + 16
    rim_shapes = [shape((n, 2 * width), BF) for n in (pc_rows, pr_rows, pd_rows)]
    rim_specs = [whole(s.shape) for s in rim_shapes]
    stat_spec = pl.BlockSpec((16, 2 * width), lambda *_: (side * PAD // 16, 0))
    nb, ng = sz.blocks, sz.groups
    square = (width, width)

    x, qkv, *rims = call(
        functools.partial(first_kernel, sz),
        (1,),
        [whole((cells, width)), whole((1, width)), par, whole((8, cells)), ANY],
        [IN] * 5,
        [inside((rows, width), F32), inside((rows, 3 * width), BF)] + rim_shapes,
        [vm((rows, width), BF), vm((width, 3 * width), BF), sems],
    )(patch_in.reshape(cells, width), cls_in, norm_attn, own_mask, qkv_weight)
    got = exchange(rims)
    bias, w_out, w_up, w_down, gain_a, scale_a, gain_m, scale_m = call(
        lambda info, *refs: bias_kernel(sz, *refs),
        (layers,),
        [pl.BlockSpec((None, 16, sz.bk), lambda l, s: (l, 0, 0))],
        pl.BlockSpec((None, ng, sz.bk, sz.bk), lambda l, s: (l, 0, 0, 0)),
        inside((layers, ng, sz.bk, sz.bk), F32),
        [vm((sz.bk, sz.bk), F32)],
        ahead=[(out_weight, 0), (up_weight, 0), (down_weight, 0)]
        + [(v, None) for v in (norm_attn, scale_attn, norm_mlp, scale_mlp)],
    )(lines)
    saved = []
    for l in range(layers):
        last = l == layers - 1
        given = dict(qkv=qkv, pc=rims[0], rc=got[0], rr=got[1], rd=got[2], bias=bias, mask=key_mask, x=x, own_mask=own_mask,
                     scale_a=scale_a, gain_m=gain_m, scale_m=scale_m, gain_a=gain_a,
                     w_out=w_out, w_up=w_up, w_down=w_down)
        left_width = 2 * width + hidden + (0 if last else width) + (0 if l else width)
        held = dict(p=((nb * ng, sz.bk, sz.bk), BF), kb=((nb, sz.bk, width), BF), vb=((nb, sz.bk, width), BF),
                    left=((rows, left_width), BF))
        local_only = dict(slope=((rows, hidden), BF), x1=((rows, width), F32), br=((rows, width), BF), down=((rows, width), BF))
        made = dict(stats=inside((8, width), F32))
        spots = dict(kext=vm((sz.ext_rows, width), F32), vext=vm((sz.ext_rows, width), F32), acc=vm((rows, width), F32))
        spots.update({n: vm(*d) for n, d in local_only.items()})
        if last:
            given.update(cot=cot, cls_cot=cls_cot, valid=valid)
            made.update({n: inside(*d) for n, d in held.items()})
            made.update(right=inside((rows, 2 * width + hidden), BF), g1=inside((rows, width), F32), vec=inside((8, width), F32),
                        patch_out=shape((cells, width), BF), cls_out=shape((1, width), BF))
            specs = [IN] * len(made)
        else:
            given.update(qkv_w=qkv_weight)
            made.update(x2=inside((rows, width), F32), next=inside((rows, 3 * width), BF),
                        pc_out=rim_shapes[0], pr_out=rim_shapes[1], pd_out=rim_shapes[2])
            specs = [IN] * len(made)
            spots.update({n: vm(*d) for n, d in held.items()})
            spots.update(w_qkv=vm((width, 3 * width), BF))
            stored = dict(held, **local_only, qkv=((rows, 3 * width), BF))
            made = dict({n + "_out": kept(*d) for n, d in stored.items()}, **made)
            specs = [ANY] * len(stored) + specs
        spots.update(sems=sems)
        names = list(given) + list(made) + list(spots)
        out = call(functools.partial(middle_kernel, sz, l, last, names), (1,),
                   [ANY if n == "qkv_w" else IN for n in given], specs, list(made.values()), list(spots.values()), vmem=18 if last else 28,
                   )(*given.values())
        res = dict(zip(made, out))
        keep_names = list(held) if last else list(stored)
        entry = {n: res[n if last else n + "_out"] for n in keep_names}
        entry.setdefault("qkv", qkv)
        entry.update(x=x, stats=res["stats"])
        entry["left"] = both(entry["left"])
        entry["h"] = (entry["left"], left_width // width - 1) if l == 0 else (saved[l - 1]["left"], 2 + chunks)
        saved.append(entry)
        if last:
            patch_out, cls_out, right, g1, vec = (res[n] for n in ("patch_out", "cls_out", "right", "g1", "vec"))
        else:
            x, qkv = res["x2"], res["next"]
            rims = [res[n] for n in ("pc_out", "pr_out", "pd_out")]
            got = exchange(rims)
            _, w_out, w_up, w_down, cot = call(
                lambda info, a, b: None, (1,), [ANY], [ANY], [kept((8, width), F32)],
                ahead=[(out_weight, l + 1), (up_weight, l + 1), (down_weight, l + 1), (patch_cot.reshape(cells, width), None)],
                vmem=2,
            )(x)

    def attention_back(l, right, v, also):
        return call(
            functools.partial(attention_back_kernel, sz, l),
            (1,),
            [IN] * 8,
            [IN] * 6,
            [inside((cells, width), BF), inside((cells, 2 * width), F32)] + rim_shapes + [inside((16, sz.bk), F32)],
            [vm((sz.ext_rows, width), F32)] * 2 + [vm((rows, width), F32), vm((ng, sz.bk, sz.bk), F32)],
            also=also, ahead=[(qkv_weight, l)] + ([] if l else [(patch_in.reshape(cells, width), None)]),
        )(right, v["qkv"], v["stats"], own_mask, v["p"], v["kb"], v["vb"], v["w_out"])

    back_scratch = [vm((cells, 2 * width), F32), vm((rows, width), F32)]

    def qkv_back(l, d_q, d_kv, own, got, g1, vec, table, wq):
        *e_qkv, rows_small, g, down_w, up_w = call(
            functools.partial(qkv_back_kernel, sz, l),
            (1,),
            [IN] * 12,
            [IN] * 5,
            [inside((rows, width), BF)] * 3 + [inside((24, width), F32), inside((rows, width), F32)],
            back_scratch + [vm((rows, 3 * width), BF)],
            weight=LONG, ahead=[(down_weight, l - 1), (up_weight, l - 1)],
        )(d_q, d_kv, own, *got, saved[l]["x"], g1, vec, table, gain_a, wq)
        return [both(e) for e in e_qkv], rows_small, g, up_w, down_w

    def mlp_back(l, g, up_w, down_w):
        v = saved[l]
        names = ["qkv", "p", "kb", "vb"]
        out = call(
            functools.partial(mlp_back_kernel, sz, l),
            (1,),
            [IN] * 10,
            [IN] * 3,
            [inside((rows, 2 * width + hidden), BF), inside((rows, width), F32), inside((8, width), F32)],
            [vm((rows, width), F32)],
            ahead=[(v[n], None) for n in names] + [(out_weight, l)],
        )(g, gain_m, scale_a, scale_m, v["x1"], v["br"], v["down"], v["slope"], up_w, down_w)
        near = dict(zip(names + ["w_out"], out[3:]), stats=v["stats"])
        return out[0], out[1], out[2], near

    def finish(d_q, d_kv, own, got, g1, vec, table, wq, first):
        return call(
            functools.partial(last_kernel, sz),
            (1,),
            [IN] * 13,
            [IN] * 6,
            [inside((rows, width), BF)] * 3 + [inside((24, width), F32), shape((cells, width), F32), shape((1, width), F32)],
            back_scratch + [vm((rows, width), F32), vm((rows, 3 * width), BF)],
        )(d_q, d_kv, own, *got, first, cls_in, g1, vec, table, gain_a, wq)

    piece, ff_piece = width // sz.devices, hidden // sz.devices
    half = width // 2
    quarter = sz.devices // 4

    def pair(dims):
        return [shape(dims, BF), inside(dims, BF)]

    def halves(start):
        return pl.BlockSpec((rows, half), lambda i, s: (0, 2 * start + s[1]))

    def grad_down(act, e_down, weight=1, also=()):
        lspec = pl.BlockSpec((rows, width), lambda i, s: (0, act[1] + s[1] * (chunks // 2) + i))
        rspec = pl.BlockSpec((rows, width), lambda i, s: (0, e_down[1]))
        out = pl.BlockSpec((None, quarter // 2, ff_piece, width), lambda i, s: (i ^ s[3], 0, 0, 0))
        return call(
            functools.partial(down_kernel, sz),
            (2,),
            [lspec, lspec, rspec, rspec],
            [out, out],
            pair((2, quarter // 2, ff_piece, width)),
            weight=weight, also=also,
            vmem=20, place=None,
        )(*act[0], *e_down[0])

    def grad_up(h2, e_up, also=()):
        lspec = halves(h2[1])
        rspec = pl.BlockSpec((rows, width), lambda i, s: (0, e_up[1] + i))
        out = pl.BlockSpec((quarter, None, piece, width), lambda i, s: (0, i, 0, 0))
        return call(
            functools.partial(up_kernel, sz),
            (chunks,),
            [lspec, lspec, rspec, rspec],
            [out, out],
            pair((quarter, chunks, piece, width)),
            also=also, vmem=20, place=None,
        )(*h2[0], *e_up[0])

    def grad_attn(h, e_qkv, att, e_branch):
        out = pl.BlockSpec((None, quarter, None, piece, width), lambda i, s: (i // 2, 0, i % 2, 0, 0))
        hspec, aspec = halves(h[1]), halves(att[1])
        bspec = pl.BlockSpec((rows, width), lambda i, s: (0, e_branch[1]))
        return call(
            functools.partial(attn_grad_kernel, sz),
            (4,),
            [hspec, hspec] + [row_w] * 6 + [aspec, aspec, bspec, bspec],
            [out, out],
            pair((2, quarter, 2, piece, width)),
            vmem=20, place=None,
        )(*h[0], *(v for both_e in e_qkv for v in both_e), *att[0], *e_branch[0])

    def last_route(flip):
        out = []
        for d in range(sz.devices):
            high, core = d >> top_bit, d & 1
            out.append((d, (d & ~(1 << top_bit) & ~1) | core << top_bit | (high ^ flip)))
        return out

    class ZSums:
        def __init__(self, halves_made):
            send, keep = halves_made
            self.n = quarter * 2 * piece // 2
            self.got = swap(send, next_bit).reshape(2, 2, self.n, width)
            self.keep = keep.reshape(2, 2, self.n, width)

        def second(self, weight=1):
            n = self.n
            s0, s1, k = call(
                z_second_kernel, (1,), [whole((2, 2, n, width))] * 2, [whole((n, width))] * 2 + [whole((2, n, width))],
                [shape((n, width), BF)] * 2 + [inside((2, n, width), BF)], place=None, weight=weight,
            )(self.keep, self.got)
            self.got = [swap(s0, 1), swap(s1, 2)]
            self.keep = k

        def third(self):
            n = self.n = self.n // 2
            s0, s1, k = call(
                z_third_kernel, (1,), [whole((2, 2, n, width))] + [whole((2, n, width))] * 2,
                [whole((n, width))] * 2 + [whole((2, n, width))],
                [shape((n, width), BF)] * 2 + [inside((2, n, width), BF)], place=None,
            )(self.keep.reshape(2, 2, n, width), *(g.reshape(2, n, width) for g in self.got))
            self.got = [swap(s0, 2), swap(s1, 1)]
            self.keep = k
            for bit in range(bits - 3, 2, -1):
                n = self.n = self.n // 2
                spec = whole((2, 2, n, width))
                s, k = call(
                    more_kernel, (1,), [spec, spec], [whole((2, n, width))] * 2, pair((2, n, width)), place=None,
                )(self.keep.reshape(2, 2, n, width), jnp.stack(self.got).reshape(2, 2, n, width))
                self.keep = k
                self.got = list(swap(s, bit))

        def fourth(self):
            n = self.n = self.n // 2
            a, b = call(
                functools.partial(z_fourth_kernel, sz), (1,), [whole((2, 2, n, width))] + [whole((2, n, width))] * 2,
                [whole((2, n, width))] * 2, [shape((2, n, width), BF)] * 2, place=None,
            )(self.keep.reshape(2, 2, n, width), *(g.reshape(2, n, width) for g in self.got))
            self.got = [lax.ppermute(a, ("dp", "tile"), last_route(0)), lax.ppermute(b, ("dp", "tile"), last_route(1))]

        def result(self):
            return self.got[0].astype(F32) + self.got[1].astype(F32)

    class Sums:
        def __init__(self, y_first, x_first, split):
            (s0, k0), (s1, k1) = y_first, x_first
            self.got = [swap(s0, 1), swap(s1, 2)]
            total = s0.size // width
            self.block = total // (quarter // 2)
            self.outer = split
            self.rows = total
            self.keep = [k0.reshape(1, 2, total // 2, width), k1.reshape(split, 2, total // 2 // split, width)]

        def second(self, weight=1, also=()):
            n = self.rows // 4
            got = [g.reshape(k.shape) for g, k in zip(self.got, self.keep)]
            sp = self.outer
            if sp == 1:
                other = pl.BlockSpec((1, 2, n, width), lambda i, s: (0, 0, i, 0))
                other_out = pl.BlockSpec((1, n, width), lambda i, s: (0, i, 0))
            else:
                other = pl.BlockSpec((1, 2, n, width), lambda i, s: (i, 0, 0, 0))
                other_out = pl.BlockSpec((1, n, width), lambda i, s: (i, 0, 0))
            spec = pl.BlockSpec((1, 2, n, width), lambda i, s: (0, 0, i, 0))
            spec_out = pl.BlockSpec((1, n, width), lambda i, s: (0, i, 0))
            s0, k0, s1, k1 = call(
                second_kernel, (2,), [spec, spec, other, other], [spec_out, spec_out, other_out, other_out],
                pair((1, 2 * n, width)) + pair((sp, 2 * n // sp, width)), weight=weight, place=None, also=also,
            )(self.keep[0], got[0], self.keep[1], got[1])
            self.got = [swap(s0, 2), swap(s1, 1)]
            self.keep = [k0, k1]
            self.rows //= 2

        def third(self, weight=1):
            n = self.rows // 2
            args = [v.reshape(2, n, width) for pair in zip(self.keep, self.got) for v in pair]
            s, k = call(
                third_kernel, (1,), [whole((2, n, width))] * 4, [whole((2, n, width))] * 2,
                pair((2, n, width)), weight=weight, place=None,
            )(*args)
            self.rows = n
            self.keep = k
            self.got = swap(s, bits - 2)
            for bit in range(bits - 3, 2, -1):
                n = self.rows // 2
                spec = whole((2, 2, n, width))
                s, k = call(
                    more_kernel, (1,), [spec, spec], [whole((2, n, width))] * 2, pair((2, n, width)), place=None,
                )(self.keep.reshape(2, 2, n, width), self.got.reshape(2, 2, n, width))
                self.rows = n
                self.keep = k
                self.got = swap(s, bit)

        def fourth(self):
            n = self.rows // 2
            spec = whole((2, 2, n, width))
            a, b = call(
                functools.partial(fourth_kernel, sz), (1,), [spec, spec], [whole((2, n, width))] * 2,
                [shape((2, n, width), BF)] * 2, place=None,
            )(self.keep.reshape(2, 2, n, width), self.got.reshape(2, 2, n, width))

            self.got = [lax.ppermute(a, ("dp", "tile"), last_route(0)), lax.ppermute(b, ("dp", "tile"), last_route(1))]

        def result(self):
            return self.got[0].astype(F32) + self.got[1].astype(F32)

    sums = {}
    small = [None] * layers
    early = [v["left"][1] for v in saved[:-1]]
    waiting = None
    near = dict(saved[-1], w_out=w_out)
    for l in reversed(range(layers)):
        left = saved[l]["left"]
        result = attention_back(l, right, near, early)
        d_q, d_kv, *rims, table, wq = result[:7]
        if l == 0:
            first = result[7]
        early = []
        if waiting is not None:
            right = both(lax.optimization_barrier((right, table))[0])
            got = exchange(rims)
            sums["attn", l + 1] = ZSums(grad_attn(*waiting))
            sums["mlp", l + 1].second(LONG)
        else:
            right = both(right)
            got = exchange(rims)
        x_first = grad_down((left, 2), (right, 0))
        y_first = grad_up((left, 1), (right, 1), got if waiting is not None else ())
        sums["mlp", l] = Sums(y_first, x_first, 2)
        if l > 0:
            e_qkv, small[l], g, up_w, down_w = qkv_back(l, d_q, d_kv, rims[0], got, g1, vec, table, wq)
            waiting = (saved[l]["h"], e_qkv, (left, 0), (right, 1 + chunks))
            right, g1, vec, near = mlp_back(l - 1, g, up_w, down_w)
        else:
            *e_qkv, small[0], patch_grad, cls_grad = finish(d_q, d_kv, rims[0], got, g1, vec, table, wq, first)
            waiting = (saved[0]["h"], [both(e) for e in e_qkv], (left, 0), (right, 1 + chunks))
    total = [jnp.stack(small), None, 0]

    def step():
        value, got_value, bit = total
        if got_value is not None:
            value = value + lax.optimization_barrier((got_value, before[0]))[0]
        total[:] = [value, swap(value, bit) if bit < bits else None, bit + 1]

    step()
    if layers > 1:
        sums["mlp", 1].third()
    sums["attn", 0] = ZSums(grad_attn(*waiting))
    step()
    if layers > 1:
        sums["attn", 1].second(MEDIUM)
    sums["mlp", 0].second()
    step()
    if layers > 1:
        sums["attn", 1].third()
        sums["mlp", 1].fourth()
    sums["mlp", 0].third()
    step()
    sums["attn", 0].second()
    if layers > 1:
        sums["attn", 1].fourth()
    step()
    sums["attn", 0].third()
    sums["mlp", 0].fourth()
    while total[1] is not None:
        step()
    sums["attn", 0].fourth()
    total = total[0]
    ups, downs, firsts, seconds = [], [], [], []
    for l in range(layers):
        mlp, attn = sums["mlp", l].result(), sums["attn", l].result()
        ups.append(jnp.swapaxes(mlp[0].reshape(chunks, piece, width), 0, 1).reshape(piece, hidden))
        downs.append(mlp[1])
        attn = attn.reshape(4, piece, width)
        firsts.append(jnp.swapaxes(attn[:3], 0, 1).reshape(piece, 3 * width))
        seconds.append(attn[3])
    g_qkv, g_out, g_up, g_down = (jnp.stack(v) for v in (firsts, seconds, ups, downs))
    vectors, tables = total[:, 0:4], total[:, 8 : 8 + heads, 0 : sz.bk]
    mine = lax.dynamic_slice_in_dim(vectors, me * piece, piece, axis=2)
    tables = tables[:, :, first_slot : first_slot + SPAN * sz.pitch].reshape(layers, heads, SPAN, sz.pitch)
    g_table = tables[..., :SPAN].reshape(rel_table.shape)
    return (
        patch_out.reshape(patch_in.shape),
        cls_out,
        patch_grad.reshape(patch_in.shape),
        cls_grad,
        mine[:, 3],
        g_qkv,
        g_table,
        g_out,
        mine[:, 2],
        mine[:, 1],
        g_up,
        g_down,
        mine[:, 0],
    )


def solution(mesh):
    tokens = P("dp", "tile", None, None, None)
    split = ("dp", "tile")
    in_specs = (tokens, P("dp", None), P("dp")) + (P(),) * 9 + (tokens, P("dp", None))
    out_specs = (
        tokens,
        P("dp", None),
        tokens,
        P("dp", None),
        P(None, split),
        P(None, split, None),
        P(),
        P(None, split, None),
        P(None, split),
        P(None, split),
        P(None, split, None),
        P(None, split, None),
        P(None, split),
    )
    return jax.shard_map(local, mesh=mesh, in_specs=in_specs, out_specs=out_specs, check_vma=False)
```

```python
import functools

import jax
import jax.numpy as jnp
import numpy as np
from jax import lax
from jax.experimental import pallas as pl
from jax.experimental.pallas import tpu as pltpu
from jax.sharding import PartitionSpec as P

RADIUS = 3
SPAN = 2 * RADIUS + 1
PAD = 8
EPS = 1e-06
MASKED = -1e30
BF = jnp.bfloat16
F32 = jnp.float32
MIB = 1 << 20


def dot(a, b):
    return lax.dot_general(a, b, (((1,), (0,)), ((), ())), preferred_element_type=F32)


def dot_nt(a, b):
    return lax.dot_general(a, b, (((1,), (1,)), ((), ())), preferred_element_type=F32)


def dot_tn(a, b):
    return lax.dot_general(a, b, (((0,), (0,)), ((), ())), preferred_element_type=F32)


def normalized(x):
    centred = x - jnp.mean(x, axis=-1, keepdims=True)
    inverse = lax.rsqrt(jnp.mean(centred * centred, axis=-1, keepdims=True) + EPS)
    return centred * inverse, inverse


def norm_back(x, gain, d_out):
    unit, inverse = normalized(x)
    d_unit = d_out * gain
    d_x = inverse * (
        d_unit
        - jnp.mean(d_unit, axis=-1, keepdims=True)
        - unit * jnp.mean(d_unit * unit, axis=-1, keepdims=True)
    )
    return d_x, d_out * unit


def split3(x):
    high = x.astype(BF).astype(F32)
    rest = x - high
    middle = rest.astype(BF).astype(F32)
    return high, middle, rest - middle


def lane_heads(rows, lanes, width):
    return lax.broadcasted_iota(jnp.int32, (rows, lanes), 1) // width


def head_rows(rows, lanes, width):
    return lane_heads(rows, lanes, width) == lax.broadcasted_iota(jnp.int32, (rows, lanes), 0)


def stacked_heads(block, width):
    rows, lanes = block.shape
    heads = lane_heads(rows, lanes, width)
    zero = jnp.zeros_like(block)
    return jnp.concatenate(
        [jnp.where(heads == h, block, zero) for h in range(lanes // width)], axis=0
    )


def folded_heads(stack, width):
    count = stack.shape[1] // width
    rows = stack.shape[0] // count
    heads = lane_heads(rows, stack.shape[1], width)
    out = stack[:rows]
    for h in range(1, count):
        out = jnp.where(heads == h, stack[h * rows : (h + 1) * rows], out)
    return out


def keep_rows(rows, cells, class_weight):
    row = lax.broadcasted_iota(jnp.int32, (rows, 1), 0)
    return jnp.where(row < cells, 1.0, jnp.where(row == cells, class_weight, 0.0))


class Sizes:
    def __init__(self, side, width, hidden, heads, devices):
        self.side = side
        self.cells = side * side
        self.rows = self.cells + 16
        self.width = width
        self.hidden = hidden
        self.heads = heads
        self.head = width // heads
        self.pitch = side + PAD
        self.ext = side + 2 * RADIUS
        self.ext_rows = self.pitch * self.ext + PAD
        self.brows = 4
        self.blocks = side // self.brows
        self.bq = self.brows * side
        self.bk = 256
        self.class_slot = self.bk - PAD
        self.quad = 4 * self.head
        self.groups = width // self.quad
        self.devices = devices
        self.bits = devices.bit_length() - 1


def stat_rows(values):
    width = values[0].shape[1]
    parts = [split3(v) for v in values]
    flat = [p[k] for k in range(3) for p in parts]
    if len(flat) % 2:
        flat.append(jnp.zeros_like(flat[0]))
    row = lax.broadcasted_iota(jnp.int32, (16, 2 * width), 0)
    out = jnp.zeros((16, 2 * width), F32)
    for i in range(0, len(flat), 2):
        out = jnp.where(row == i // 2, jnp.concatenate(flat[i : i + 2], axis=1), out)
    return out.astype(BF)


def read_stats(block, count, width):
    rows = block.astype(F32)

    def piece(i):
        return rows[i // 2 : i // 2 + 1, (i % 2) * width : (i % 2 + 1) * width]

    return [piece(i) + piece(count + i) + piece(2 * count + i) for i in range(count)]


def in_tile_order(info, pieces):
    me = info[0] * 2 + info[1]
    out = []
    for t in range(4):
        d = me ^ t
        out.append(
            [
                jnp.where(d == 0, a, jnp.where(d == 1, b, jnp.where(d == 2, c, e)))
                for a, b, c, e in zip(*pieces)
            ]
        )
    return out


def class_scores(sz, info, qkv_ref, mask):
    cells, width = sz.cells, sz.width
    own = head_rows(16, width, sz.head)
    class_rows = qkv_ref[cells : cells + 16, :].astype(F32)
    q_c, k_c, v_c = (class_rows[0:1, i * width : (i + 1) * width] for i in range(3))
    q_heads = jnp.where(own, q_c, 0.0)
    scale = sz.head ** (-0.5)
    scores = dot_nt(q_heads.astype(BF), qkv_ref[0:cells, width : 2 * width]) * scale + mask
    self_score = jnp.sum(q_heads * k_c, axis=1, keepdims=True) * scale
    self_score = jnp.where(info[2] == 1, self_score, MASKED)
    return own, q_heads, k_c, v_c, scores, self_score


def send_rims(sz, info, kv_half, kv_edge_rows, stats, pc_ref, pr_ref, pd_ref):
    side, width = sz.side, sz.width
    cells8 = [kv_half(r) for r in range(side)]
    pc_ref[0 : side * PAD, :] = jnp.concatenate(cells8, axis=0).astype(BF)
    pc_ref[side * PAD : side * PAD + 16, :] = stats
    edge, corner = kv_edge_rows()
    pr_ref[0 : RADIUS * side, :] = jnp.concatenate(edge, axis=0).astype(BF)
    pr_ref[RADIUS * side : RADIUS * side + 16, :] = stats
    zero = jnp.zeros((PAD, 2 * width), F32)
    pd_ref[0 : (RADIUS + 1) * PAD, :] = jnp.concatenate(corner + [zero], axis=0).astype(BF)
    pd_ref[(RADIUS + 1) * PAD : (RADIUS + 1) * PAD + 16, :] = stats


def rim_places(sz, info):
    return sz.pitch * (1 - info[1]), (sz.side + RADIUS) * (1 - info[0])


GELU_C = float(np.sqrt(2.0 / np.pi))


class Copies:
    def __init__(self, sems):
        self.sems, self.count, self.out = sems, 0, []

    def load(self, src, dst):
        copy = pltpu.make_async_copy(src, dst, self.sems.at[self.count])
        self.count += 1
        copy.start()
        return copy

    def store(self, src, dst):
        self.out.append(self.load(src, dst))

    def finish(self):
        for copy in self.out:
            copy.wait()


def qkv_part(sz, info, x, gain, wq, loads, mask, h_ref, qkv_ref, pc_ref, pr_ref, pd_ref):
    width, side, cells = sz.width, sz.side, sz.cells
    unit, _ = normalized(x)
    h = (unit * gain).astype(BF)
    h_ref[...] = h
    for i in range(3):
        loads[i].wait()
        cols = slice(i * width, (i + 1) * width)
        qkv_ref[:, cols] = dot(h, wq[:, cols]).astype(BF)
    own, q_heads, k_c, v_c, scores, self_score = class_scores(sz, info, qkv_ref, mask)
    top = jnp.maximum(jnp.max(scores, axis=1, keepdims=True), self_score)
    probs = jnp.where(mask > -1.0, jnp.exp(scores - top), 0.0)
    self_prob = jnp.where(info[2] == 1, jnp.exp(self_score - top), 0.0)
    total = jnp.sum(probs, axis=1, keepdims=True) + self_prob
    part = dot(probs.astype(BF), qkv_ref[0:cells, 2 * width :]) + self_prob * v_c

    def to_row(v):
        return jnp.sum(jnp.where(own, v, 0.0), axis=0, keepdims=True)

    stats = stat_rows([to_row(part), to_row(top), to_row(total)])
    left_col = info[1] == 0

    def half(r):
        row = qkv_ref[r * side : (r + 1) * side, width:].astype(F32)
        return jnp.where(left_col, row[PAD:], row[:PAD])

    def edges():
        first = pl.multiple_of((1 - info[0]) * (side - RADIUS) * side, 16)
        rows = qkv_ref[pl.ds(first, RADIUS * side), width:].astype(F32)
        edge = [rows[t * side : (t + 1) * side] for t in range(RADIUS)]
        return edge, [jnp.where(left_col, e[PAD:], e[:PAD]) for e in edge]

    send_rims(sz, info, half, edges, stats, pc_ref, pr_ref, pd_ref)


def first_kernel(sz, info, patch_ref, cls_ref, gain_ref, mask_ref, w_any,
                 x_ref, qkv_ref, pc_ref, pr_ref, pd_ref, h_v, wq, sems):
    copies = Copies(sems)
    width = sz.width
    loads = [copies.load(w_any.at[0, :, pl.ds(i * width, width)], wq.at[:, pl.ds(i * width, width)]) for i in range(3)]
    row = lax.broadcasted_iota(jnp.int32, (16, width), 0)
    x_ref[0 : sz.cells, :] = patch_ref[...].astype(F32)
    x_ref[sz.cells :, :] = jnp.where(row == 0, cls_ref[...].astype(F32), 0.0)
    qkv_part(sz, info, x_ref[...], gain_ref[0:1, :], wq, loads, mask_ref[0:1, :], h_v, qkv_ref, pc_ref, pr_ref, pd_ref)


def extended(sz, info, qkv_ref, rc_ref, rr_ref, rd_ref, kext, vext):
    width, side, pitch = sz.width, sz.side, sz.pitch
    beside, above = rim_places(sz, info)
    for ext, lo in ((kext, width), (vext, 2 * width)):
        at = lo - width
        ext[...] = jnp.zeros_like(ext)
        for r in range(side):
            base = pitch * (r + RADIUS)
            ext[base + PAD : base + PAD + side, :] = qkv_ref[r * side : (r + 1) * side, lo : lo + width].astype(F32)
        sides = rc_ref[0 : side * PAD, at : at + width].astype(F32)
        for r in range(side):
            ext[pl.ds(pl.multiple_of(pitch * (r + RADIUS) + beside, 8), PAD), :] = sides[r * PAD : (r + 1) * PAD]
        edge = rr_ref[0 : RADIUS * side, at : at + width].astype(F32)
        corner = rd_ref[0 : (RADIUS + 1) * PAD, at : at + width].astype(F32)
        for t in range(RADIUS):
            base = pitch * (above + t)
            ext[pl.ds(pl.multiple_of(base + PAD, 8), side), :] = edge[t * side : (t + 1) * side]
            ext[pl.ds(pl.multiple_of(base + beside, 8), PAD), :] = corner[t * PAD : (t + 1) * PAD]


def all_stats(sz, info, st_ref, rc_ref, rr_ref, rd_ref):
    side, width = sz.side, sz.width
    return in_tile_order(info, [read_stats(r, 3, width) for r in (
        st_ref[side * PAD : side * PAD + 16, :],
        rc_ref[side * PAD : side * PAD + 16, :],
        rr_ref[RADIUS * side : RADIUS * side + 16, :],
        rd_ref[(RADIUS + 1) * PAD : (RADIUS + 1) * PAD + 16, :],
    )])


def middle_kernel(sz, layer, last, names, info, *refs):
    r = dict(zip(names, refs))
    qkv_ref, rc_ref, rr_ref, rd_ref = r["qkv"], r["rc"], r["rr"], r["rd"]
    st_ref, bias_ref, mask_ref, x_ref = r["pc"], r["bias"], r["mask"], r["x"]
    scale_a_ref, gain_m_ref, scale_m_ref, gain_a_ref = r["scale_a"], r["gain_m"], r["scale_m"], r["gain_a"]
    w_out, w_up, w_down, stat_ref = r["w_out"], r["w_up"], r["w_down"], r["stats"]
    p_v, kb_v, vb_v, slope_v, x1_v, br_v, down_v, left = (r[n] for n in ("p", "kb", "vb", "slope", "x1", "br", "down", "left"))
    kext, vext, acc = r["kext"], r["vext"], r["acc"]
    width, side, cells, pitch, hidden = sz.width, sz.side, sz.cells, sz.pitch, sz.hidden
    chunks = hidden // width
    copies = Copies(r["sems"])

    def hold(name, cols=None):
        if not last:
            src, dst = r[name], r[name + "_out"]
            if cols is not None:
                at = pl.ds(cols[0], cols[1])
                src, dst = src.at[:, at], dst.at[:, at]
            copies.store(src, dst)

    if not last:
        qkv_loads = [
            copies.load(r["qkv_w"].at[layer + 1, :, pl.ds(i * width, width)], r["w_qkv"].at[:, pl.ds(i * width, width)])
            for i in range(3)
        ]
        hold("qkv")
    extended(sz, info, qkv_ref, rc_ref, rr_ref, rd_ref, kext, vext)
    if layer == 0:
        left[:, left.shape[1] - width :] = (normalized(x_ref[...])[0] * gain_a_ref[0:1, :]).astype(BF)
    class_rows = qkv_ref[cells : cells + 16, :].astype(F32)[0:PAD]
    scale = sz.head ** (-0.5)
    for b in range(sz.blocks):
        first = b * sz.brows * pitch
        kb = jnp.concatenate([kext[first : first + sz.class_slot, :], class_rows[:, width : 2 * width]], axis=0).astype(BF)
        vb = jnp.concatenate([vext[first : first + sz.class_slot, :], class_rows[:, 2 * width :]], axis=0).astype(BF)
        kb_v[b] = kb
        vb_v[b] = vb
        q = qkv_ref[b * sz.bq : (b + 1) * sz.bq, 0:width] * jnp.asarray(scale, BF)
        mask = mask_ref[b]
        mask = jnp.concatenate([mask, mask], axis=1)
        for g in range(sz.groups):
            lanes = slice(g * sz.quad, (g + 1) * sz.quad)
            scores = dot_nt(kb[:, lanes], stacked_heads(q[:, lanes], sz.head)) + bias_ref[layer, g] + mask
            top = jnp.max(scores, axis=0, keepdims=True)
            probs = jnp.exp(scores - top)
            total = jnp.sum(probs, axis=0, keepdims=True)
            probs = (probs * (1.0 / total)).astype(BF)
            p_v[b * sz.groups + g] = probs
            out = folded_heads(dot_tn(probs, vb[:, lanes]), sz.head)
            left[b * sz.bq : (b + 1) * sz.bq, lanes] = out.astype(BF)
    for name in ("p", "kb", "vb"):
        hold(name)
    ordered = all_stats(sz, info, st_ref, rc_ref, rr_ref, rd_ref)
    top = functools.reduce(jnp.maximum, [s[1] for s in ordered])
    total = jnp.zeros_like(top)
    summed = jnp.zeros_like(top)
    for part, part_top, part_total in ordered:
        factor = jnp.exp(part_top - top)
        total = total + part_total * factor
        summed = summed + part * factor
    class_out = summed / total
    stat_ref[...] = jnp.zeros_like(stat_ref)
    stat_ref[0:1, :] = top
    stat_ref[1:2, :] = total
    stat_ref[2:3, :] = class_out
    row = lax.broadcasted_iota(jnp.int32, (16, width), 0)
    left[cells : cells + 16, 0:width] = jnp.where(row == 0, class_out, 0.0).astype(BF)
    branch = dot(left[:, 0:width], w_out[...])
    br_v[...] = branch.astype(BF)
    x1_v[...] = x_ref[...] + scale_a_ref[layer : layer + 1, :] * branch
    unit, _ = normalized(x1_v[...])
    left[:, width : 2 * width] = (unit * gain_m_ref[layer : layer + 1, :]).astype(BF)
    hold("br")
    hold("x1")
    hold("left", (0, 2 * width))
    for c in range(chunks):
        at = slice(c * width, (c + 1) * width)
        u = dot(left[:, width : 2 * width], w_up[:, at])
        square = u * u
        th = jnp.tanh(GELU_C * u * (1.0 + 0.044715 * square))
        half = 0.5 * (1.0 + th)
        here = slice((c + 2) * width, (c + 3) * width)
        left[:, here] = (u * half).astype(BF)
        slope = half + (0.5 * u) * (1.0 - th * th) * (GELU_C + (3 * 0.044715 * GELU_C) * square)
        slope_v[:, at] = slope.astype(BF)
        part = dot(left[:, here], w_down[at, :])
        if c == 0:
            acc[...] = part
        else:
            acc[...] += part
    down_v[...] = acc[...].astype(BF)
    hold("slope")
    hold("down")
    hold("left", (2 * width, hidden))
    x2 = x1_v[...] + scale_m_ref[layer : layer + 1, :] * acc[...]
    if last:
        valid_ref, vec_ref = r["valid"], r["vec"]
        r["patch_out"][...] = (x2[0:cells] * valid_ref[...]).astype(BF)
        r["cls_out"][...] = x2[cells : cells + 1].astype(BF)
        g_cells = r["cot"][...].astype(F32) * valid_ref[...]
        g_class = jnp.where(row == 0, r["cls_cot"][...].astype(F32), 0.0)
        g = jnp.concatenate([g_cells, g_class], axis=0)
        keep = keep_rows(sz.rows, cells, jnp.where(info[2] == 1, 1.0, 0.0))
        vec_ref[...] = jnp.zeros_like(vec_ref)
        mlp_back_part(sz, layer, g, acc[...], keep, r["right"], r["g1"], vec_ref, x1_v, br_v, slope_v,
                      w_up, w_down, gain_m_ref, scale_a_ref, scale_m_ref, acc)
    else:
        r["x2"][...] = x2
        qkv_part(sz, info, x2, gain_a_ref[layer + 1 : layer + 2, :], r["w_qkv"], qkv_loads, r["own_mask"][0:1, :],
                 left.at[:, pl.ds(2 * width + hidden, width)], r["next"], r["pc_out"], r["pr_out"], r["pd_out"])
        hold("left", (2 * width + hidden, left.shape[1] - 2 * width - hidden))
    copies.finish()


def mlp_back_part(sz, layer, g, down, keep, right, g1_ref, vec_ref, x1_ref, br_ref, slope_ref,
                  w_up, w_down, gain_m_ref, scale_a_ref, scale_m_ref, acc):
    width = sz.width
    vec_ref[0:1, :] = jnp.sum(keep * g * down, axis=0, keepdims=True)
    right[:, 0:width] = (scale_m_ref[layer : layer + 1, :] * g).astype(BF)
    g1_ref[...] = g
    for c in range(sz.hidden // width):
        at = slice(c * width, (c + 1) * width)
        e_up = (dot_nt(right[:, 0:width], w_down[at, :]) * slope_ref[:, at].astype(F32)).astype(BF)
        here = slice((c + 1) * width, (c + 2) * width)
        right[:, here] = e_up
        part = dot_nt(right[:, here], w_up[:, at])
        if c == 0:
            acc[...] = part
        else:
            acc[...] += part
    d_x1, gain_rows = norm_back(x1_ref[...], gain_m_ref[layer : layer + 1, :], acc[...])
    vec_ref[1:2, :] = jnp.sum(keep * gain_rows, axis=0, keepdims=True)
    g1 = g1_ref[...] + d_x1
    g1_ref[...] = g1
    right[:, width + sz.hidden :] = (scale_a_ref[layer : layer + 1, :] * g1).astype(BF)
    vec_ref[2:3, :] = jnp.sum(keep * g1 * br_ref[...].astype(F32), axis=0, keepdims=True)


def attention_back_kernel(sz, layer, info, right, qkv_ref, stat_ref, own_mask_ref, p_v, kb_v, vb_v, w,
                          dq_ref, dkv_ref, pc_ref, pr_ref, pd_ref, tab_ref,
                          kext, vext, d_o, tab):
    width, side, cells, pitch = sz.width, sz.side, sz.cells, sz.pitch
    scale = sz.head ** (-0.5)
    kext[...] = jnp.zeros_like(kext)
    vext[...] = jnp.zeros_like(vext)
    d_o[...] = dot_nt(right[:, right.shape[1] - width :], w[...])
    class_k = [jnp.zeros((PAD, sz.quad), F32) for _ in range(sz.groups)]
    class_v = [jnp.zeros((PAD, sz.quad), F32) for _ in range(sz.groups)]
    for b in range(sz.blocks):
        first = b * sz.brows * pitch
        q = qkv_ref[b * sz.bq : (b + 1) * sz.bq, 0:width] * jnp.asarray(scale, BF)
        do = d_o[b * sz.bq : (b + 1) * sz.bq, :].astype(BF)
        for g in range(sz.groups):
            lanes = slice(g * sz.quad, (g + 1) * sz.quad)
            do_stack = stacked_heads(do[:, lanes], sz.head)
            q_stack = stacked_heads(q[:, lanes], sz.head)
            probs = p_v[b * sz.groups + g]
            wide = probs.astype(F32)
            d_prob = dot_nt(vb_v[b, :, lanes], do_stack)
            delta = jnp.sum(wide * d_prob, axis=0, keepdims=True)
            d_score = wide * (d_prob - delta)
            if b == 0:
                tab[g] = d_score
            else:
                tab[g] += d_score
            low = d_score.astype(BF)
            d_v = dot(probs, do_stack)
            d_k = dot(low, q_stack)
            vext[first : first + sz.class_slot, lanes] += d_v[: sz.class_slot]
            kext[first : first + sz.class_slot, lanes] += d_k[: sz.class_slot]
            class_v[g] = class_v[g] + d_v[sz.class_slot :]
            class_k[g] = class_k[g] + d_k[sz.class_slot :]
            d_q = folded_heads(dot_tn(low, kb_v[b, :, lanes]), sz.head) * scale
            dq_ref[b * sz.bq : (b + 1) * sz.bq, lanes] = d_q.astype(BF)
    mask = own_mask_ref[0:1, :]
    own, q_heads, k_c, v_c, scores, self_score = class_scores(sz, info, qkv_ref, mask)
    top = jnp.max(jnp.where(own, stat_ref[0:1, :], MASKED), axis=1, keepdims=True)
    total = jnp.max(jnp.where(own, stat_ref[1:2, :], 0.0), axis=1, keepdims=True)
    real = lax.broadcasted_iota(jnp.int32, (16, 1), 0) < sz.heads
    probs = jnp.where((mask > -1.0) & real, jnp.exp(scores - top) / total, 0.0)
    self_prob = jnp.where((info[2] == 1) & real, jnp.exp(self_score - top) / total, 0.0)
    d_class = jnp.where(own, d_o[cells : cells + 1, :], 0.0)
    delta = jnp.sum(d_class * stat_ref[2:3, :], axis=1, keepdims=True)
    d_low = d_class.astype(BF)
    d_cell = probs * (dot_nt(d_low, qkv_ref[0:cells, 2 * width :]) - delta)
    d_cell_low = d_cell.astype(BF)
    d_self = self_prob * (jnp.sum(d_class * v_c, axis=1, keepdims=True) - delta)

    def to_row(v):
        return jnp.sum(jnp.where(own, v, 0.0), axis=0, keepdims=True)

    g_q = to_row(dot(d_cell_low, qkv_ref[0:cells, width : 2 * width]) + d_self * k_c) * scale
    g_k = to_row(d_self * q_heads) * scale + jnp.concatenate([c[0:1] for c in class_k], axis=1)
    g_v = to_row(self_prob * d_class) + jnp.concatenate([c[0:1] for c in class_v], axis=1)
    add_k = dot_tn(d_cell_low, q_heads.astype(BF)) * scale
    add_v = dot_tn(probs.astype(BF), d_low)
    beside, above = rim_places(sz, info)
    for r in range(side):
        base = pitch * (r + RADIUS) + PAD
        rows = slice(r * side, (r + 1) * side)
        dkv_ref[rows, 0:width] = kext[base : base + side, :] + add_k[rows]
        dkv_ref[rows, width:] = vext[base : base + side, :] + add_v[rows]

    def pair(at, count):
        at = pl.ds(pl.multiple_of(at, 8), count)
        return jnp.concatenate([kext[at, :], vext[at, :]], axis=1)

    def edges():
        return (
            [pair(pitch * (above + t) + PAD, side) for t in range(RADIUS)],
            [pair(pitch * (above + t) + beside, PAD) for t in range(RADIUS)],
        )

    send_rims(sz, info, lambda r: pair(pitch * (r + RADIUS) + beside, PAD), edges,
              stat_rows([g_q, g_k, g_v]), pc_ref, pr_ref, pd_ref)
    per_head = sz.bq
    for g in range(sz.groups):
        turned = tab[g].T
        for h in range(4):
            total_h = jnp.zeros((side, sz.bk), F32)
            for r in range(sz.brows):
                at = h * per_head + r * side
                piece = turned[at : at + side]
                shift = (sz.bk - pitch * r) % sz.bk
                total_h = total_h + (pltpu.roll(piece, shift, 1) if shift else piece)
            tab_row = jnp.zeros((1, sz.bk), F32)
            for c in range(side):
                one = total_h[c : c + 1]
                tab_row = tab_row + (pltpu.roll(one, sz.bk - c, 1) if c else one)
            tab_ref[4 * g + h : 4 * g + h + 1, :] = tab_row
    tab_ref[sz.heads : 16, :] = jnp.zeros((16 - sz.heads, sz.bk), F32)


def qkv_back_part(sz, info, dq_ref, dkv_ref, st_ref, rc_ref, rr_ref, rd_ref, x_ref, gain, g1_ref, eq_ref, dkv, acc, wq):
    width, side, cells = sz.width, sz.side, sz.cells
    dkv[...] = dkv_ref[...]
    beside = PAD * (1 - info[1])
    edge = (1 - info[0]) * (side - RADIUS) * side
    sides = rc_ref[0 : side * PAD, :].astype(F32)
    for r in range(side):
        dkv[pl.ds(pl.multiple_of(r * side + beside, 8), PAD), :] += sides[r * PAD : (r + 1) * PAD]
    dkv[pl.ds(pl.multiple_of(edge, 8), RADIUS * side), :] += rr_ref[0 : RADIUS * side, :].astype(F32)
    corner = rd_ref[0 : (RADIUS + 1) * PAD, :].astype(F32)
    for t in range(RADIUS):
        dkv[pl.ds(pl.multiple_of(edge + t * side + beside, 8), PAD), :] += corner[t * PAD : (t + 1) * PAD]
    ordered = all_stats(sz, info, st_ref, rc_ref, rr_ref, rd_ref)
    class_row = jnp.concatenate(
        [functools.reduce(lambda a, b: a + b, [o[i] for o in ordered]) for i in range(3)], axis=1
    )
    row = lax.broadcasted_iota(jnp.int32, (16, 3 * width), 0)
    eq_ref[0:cells, 0:width] = dq_ref[...]
    eq_ref[0:cells, width:] = dkv[...].astype(BF)
    eq_ref[cells : cells + 16, :] = jnp.where(row == 0, class_row, 0.0).astype(BF)
    for i in range(3):
        cols = slice(i * width, (i + 1) * width)
        part = dot_nt(eq_ref[:, cols], wq[:, cols])
        if i == 0:
            acc[...] = part
        else:
            acc[...] += part
    d_x, gain_rows = norm_back(x_ref[...], gain, acc[...])
    return g1_ref[...] + d_x, gain_rows


def small_rows(sz, small_ref, vec_ref, tab_ref, gain_sum):
    small_ref[...] = jnp.zeros_like(small_ref)
    small_ref[0:3, :] = vec_ref[0:3, :]
    small_ref[3:4, :] = gain_sum
    small_ref[8:24, 0 : sz.bk] = tab_ref[...]


def qkv_back_kernel(sz, layer, info, dq_ref, dkv_ref, st_ref, rc_ref, rr_ref, rd_ref, x_ref, g1_ref, vec_ref, tab_ref,
                    gain_a_ref, wq, eq_ref, ek_ref, ev_ref, small_ref, g_ref, dkv, acc, eq_v):
    width = sz.width
    g, gain_rows = qkv_back_part(sz, info, dq_ref, dkv_ref, st_ref, rc_ref, rr_ref, rd_ref, x_ref,
                                 gain_a_ref[layer : layer + 1, :], g1_ref, eq_v, dkv, acc, wq)
    for i, ref in enumerate((eq_ref, ek_ref, ev_ref)):
        ref[...] = eq_v[:, i * width : (i + 1) * width]
    keep = keep_rows(sz.rows, sz.cells, jnp.where(info[2] == 1, 1.0, 0.0))
    small_rows(sz, small_ref, vec_ref, tab_ref, jnp.sum(keep * gain_rows, axis=0, keepdims=True))
    g_ref[...] = g


def mlp_back_kernel(sz, layer, info, g_ref, gain_m_ref, scale_a_ref, scale_m_ref, x1_ref, br_ref, down_ref,
                    slope_ref, w_up, w_down, right, g1_out, vec_out, acc):
    keep = keep_rows(sz.rows, sz.cells, jnp.where(info[2] == 1, 1.0, 0.0))
    vec_out[...] = jnp.zeros_like(vec_out)
    mlp_back_part(sz, layer, g_ref[...], down_ref[...].astype(F32), keep, right, g1_out, vec_out,
                  x1_ref, br_ref, slope_ref, w_up, w_down, gain_m_ref, scale_a_ref, scale_m_ref, acc)


def last_kernel(sz, info, dq_ref, dkv_ref, st_ref, rc_ref, rr_ref, rd_ref, patch_ref, cls_ref, g1_ref, vec_ref, tab_ref,
                gain_a_ref, wq, eq_ref, ek_ref, ev_ref, small_ref, pg_ref, cg_ref, dkv, acc, x_ref, eq_v):
    width = sz.width
    row = lax.broadcasted_iota(jnp.int32, (16, width), 0)
    x_ref[0 : sz.cells, :] = patch_ref[...].astype(F32)
    x_ref[sz.cells :, :] = jnp.where(row == 0, cls_ref[...].astype(F32), 0.0)
    g, gain_rows = qkv_back_part(sz, info, dq_ref, dkv_ref, st_ref, rc_ref, rr_ref, rd_ref, x_ref,
                                 gain_a_ref[0:1, :], g1_ref, eq_v, dkv, acc, wq)
    for i, ref in enumerate((eq_ref, ek_ref, ev_ref)):
        ref[...] = eq_v[:, i * width : (i + 1) * width]
    keep = keep_rows(sz.rows, sz.cells, jnp.where(info[2] == 1, 1.0, 0.0))
    small_rows(sz, small_ref, vec_ref, tab_ref, jnp.sum(keep * gain_rows, axis=0, keepdims=True))
    pg_ref[...] = g[0 : sz.cells]
    cg_ref[...] = g[sz.cells : sz.cells + 1]


def product(sz, info, left_ref, left_got, own_ref, other_ref):
    cells = sz.cells
    row = lax.broadcasted_iota(jnp.int32, (16, own_ref.shape[1]), 0)
    tail = own_ref[cells : cells + 16, :]
    tail = jnp.where((row < 0) | (info[0] == 0), tail, jnp.zeros_like(tail))
    left = jnp.concatenate([left_ref[0:cells, :], left_got[0:cells, :], left_ref[cells : cells + 16, :]], axis=0)
    right = jnp.concatenate([own_ref[0:cells, :], other_ref[0:cells, :], tail], axis=0)
    return dot_tn(left, right)


def store_pieces(value, count, pairs, bit, place, send_ref, keep_ref):
    per = value.shape[0] // count
    for a, b in pairs:
        one, two = value[a * per : (a + 1) * per], value[b * per : (b + 1) * per]
        at = place(a)
        keep_ref[at] = jnp.where(bit == 0, one, two).astype(BF)
        send_ref[at] = jnp.where(bit == 0, two, one).astype(BF)


def pairs_of(bits, bit):
    return [(a, a | 1 << bit) for a in range(1 << bits) if not a >> bit & 1]


def order_of(bits, skip, first):
    def place(a, me):
        names = list(first) + [b for b in range(bits - 1, -1, -1) if b != skip and b not in first]
        at = 0
        for b in names:
            mine = (a >> b) & 1
            at = at * 2 + (mine if b == 0 else mine ^ ((me >> b) & 1))
        return at

    return place


def down_kernel(sz, info, act_ref, act_got, own_ref, other_ref, send_ref, keep_ref):
    bits = sz.bits - 2
    me = info[4]
    value = product(sz, info, act_ref, act_got, own_ref, other_ref)
    place = order_of(bits, 2, (1,))
    store_pieces(value, 1 << bits, pairs_of(bits, 2), (me >> 2) & 1, lambda a: place(a, me), send_ref, keep_ref)


def columns_step(sz, info, bit, order, value, send_ref, keep_ref):
    bits = sz.bits - 1
    me = info[4]
    place = order_of(bits, bit, order)
    store_pieces(value, 1 << bits, pairs_of(bits, bit), (me >> bit) & 1, lambda a: place(a, me), send_ref, keep_ref)


def up_kernel(sz, info, h_ref, h_got, own_ref, other_ref, send_ref, keep_ref):
    columns_step(sz, info, 1, (2,), product(sz, info, h_ref, h_got, own_ref, other_ref), send_ref, keep_ref)


def attn_grad_kernel(sz, info, h_ref, h_got, qo, qg, ko, kg, vo, vg, a_ref, a_got, bo, bg, send_ref, keep_ref):
    step = pl.program_id(0)
    bit = sz.bits - 2
    cases = [(h_ref, h_got, qo, qg, (1, 2)), (h_ref, h_got, ko, kg, (1, 2)), (h_ref, h_got, vo, vg, (2, 1)),
             (a_ref, a_got, bo, bg, (2, 1))]
    for i, (*factors, order) in enumerate(cases):
        @pl.when(step == i)
        def _():
            columns_step(sz, info, bit, order, product(sz, info, *factors), send_ref, keep_ref)


def plus(a, b):
    return a.astype(F32) + b.astype(F32)


def second_kernel(info, k0, g0, k1, g1, s0_ref, k0_ref, s1_ref, k1_ref):
    s0_ref[...] = plus(k0[:, 1], g0[:, 1]).astype(BF)
    k0_ref[...] = plus(k0[:, 0], g0[:, 0]).astype(BF)
    s1_ref[...] = plus(k1[:, 1], g1[:, 1]).astype(BF)
    k1_ref[...] = plus(k1[:, 0], g1[:, 0]).astype(BF)


def third_kernel(info, k0, g0, k1, g1, s_ref, k_ref):
    s_ref[0] = plus(k0[1], g0[1]).astype(BF)
    k_ref[0] = plus(k0[0], g0[0]).astype(BF)
    s_ref[1] = plus(k1[1], g1[1]).astype(BF)
    k_ref[1] = plus(k1[0], g1[0]).astype(BF)


def more_kernel(info, k, g, s_ref, k_ref):
    s_ref[...] = plus(k[:, 1], g[:, 1]).astype(BF)
    k_ref[...] = plus(k[:, 0], g[:, 0]).astype(BF)


def z_second_kernel(info, k, g, s0_ref, s1_ref, k_ref):
    for i, ref in enumerate((s0_ref, s1_ref)):
        ref[...] = plus(k[i, 1], g[i, 1]).astype(BF)
        k_ref[i] = plus(k[i, 0], g[i, 0]).astype(BF)


def z_third_kernel(info, k, g0, g1, s0_ref, s1_ref, k_ref):
    for i, (g, ref) in enumerate(((g0, s0_ref), (g1, s1_ref))):
        ref[...] = plus(k[i, 1], g[1]).astype(BF)
        k_ref[i] = plus(k[i, 0], g[0]).astype(BF)


def z_fourth_kernel(sz, info, k, g0, g1, a_ref, b_ref):
    high = (info[4] >> (sz.bits - 1)) & 1
    for i, g in enumerate((g0, g1)):
        one, two = plus(k[i, 0], g[0]), plus(k[i, 1], g[1])
        a_ref[i] = jnp.where(high == 0, one, two).astype(BF)
        b_ref[i] = jnp.where(high == 0, two, one).astype(BF)


def fourth_kernel(sz, info, k, g, a_ref, b_ref):
    high = (info[4] >> (sz.bits - 1)) & 1
    one, two = plus(k[:, 0], g[:, 0]), plus(k[:, 1], g[:, 1])
    a_ref[...] = jnp.where(high == 0, one, two).astype(BF)
    b_ref[...] = jnp.where(high == 0, two, one).astype(BF)


def bias_kernel(sz, table_ref, out_ref, wide):
    slot = lax.broadcasted_iota(jnp.int32, (sz.side, sz.bk), 1)
    for g in range(sz.groups):
        for h in range(4):
            line = jnp.broadcast_to(table_ref[4 * g + h : 4 * g + h + 1, :], (sz.side, sz.bk))
            line = pltpu.roll(line, 0, 1, stride=1, stride_axis=0)
            for r in range(sz.brows):
                piece = pltpu.roll(line, sz.pitch * r, 1) if r else line
                at = h * sz.bq + r * sz.side
                wide[at : at + sz.side, :] = jnp.where(slot == sz.class_slot, 0.0, piece)
        out_ref[g] = wide[...].T


def shape(dims, dtype):
    return jax.ShapeDtypeStruct(dims, dtype)


def kept(dims, dtype):
    return pltpu.HBM(dims, dtype)


def inside(dims, dtype):
    return pltpu.VMEM(dims, dtype)


def whole(dims):
    return pl.BlockSpec(dims, lambda *_: (0,) * len(dims))


IN = pl.BlockSpec(memory_space=pltpu.VMEM)


ANY = pl.BlockSpec(memory_space=pl.ANY)
MEDIUM = 4 * 10**9
LONG = 10**11


def local(patch_in, cls_in, page_side, norm_attn, qkv_weight, rel_table, out_weight, scale_attn,
          norm_mlp, up_weight, down_weight, scale_mlp, patch_cot, cls_cot):
    tiles = lax.axis_size("tile")
    pages = lax.axis_size("dp")
    layers, heads = rel_table.shape[:2]
    sz = Sizes(patch_in.shape[2], patch_in.shape[4], up_weight.shape[2], heads, tiles * pages)
    side, cells, rows, width, hidden = sz.side, sz.cells, sz.rows, sz.width, sz.hidden
    chunks = hidden // width
    tile = lax.axis_index("tile")
    me = lax.axis_index("dp") * tiles + tile
    tile_row, tile_col = tile // 2, tile % 2
    page = page_side[0]
    bits = sz.bits
    top_bit, next_bit = bits - 1, bits - 2
    info = jnp.stack([tile_row, tile_col, (tile == 0).astype(jnp.int32), (me >> next_bit) & 1, me]).astype(jnp.int32)

    cell = np.arange(cells)
    own_ok = (tile_row * side + cell // side < page) & (tile_col * side + cell % side < page)
    own_mask = jnp.broadcast_to(jnp.where(own_ok, 0.0, MASKED).astype(F32), (8, cells))
    valid = own_ok.astype(F32)[:, None]
    slot = np.arange(sz.bk)[None] + np.arange(sz.blocks)[:, None] * sz.brows * sz.pitch - PAD + RADIUS
    key_row = tile_row * side + slot // sz.pitch - RADIUS
    key_col = tile_col * side + slot % sz.pitch - RADIUS
    is_class = (np.arange(sz.bk) == sz.class_slot)[None]
    key_ok = (key_row >= 0) & (key_row < page) & (key_col >= 0) & (key_col < page) | is_class
    key_mask = jnp.broadcast_to(
        jnp.where(key_ok, 0.0, MASKED).astype(F32)[:, :, None], (sz.blocks, sz.bk, sz.bk // 2)
    )
    lines = jnp.pad(rel_table.reshape(layers, heads, SPAN, SPAN), ((0, 0), (0, 16 - heads), (0, 0), (0, sz.pitch - SPAN)),
                    constant_values=MASKED).reshape(layers, 16, SPAN * sz.pitch)
    first_slot = PAD - RADIUS
    lines = jnp.pad(lines, ((0, 0), (0, 0), (first_slot, sz.bk - first_slot - SPAN * sz.pitch)), constant_values=MASKED)

    resident = {}
    before = []

    def call(kernel, grid, in_specs, out_specs, out_shape, scratch=(), vmem=12, weight=1, also=(), place=pltpu.HBM, ahead=()):
        deps = [pltpu.with_memory_space_constraint(a, pltpu.HBM) for a in before] + list(also)
        count = len(in_specs)

        results = list(out_shape) if isinstance(out_shape, (list, tuple)) else [out_shape]
        result_specs = list(out_specs) if isinstance(out_specs, (list, tuple)) else [out_specs]
        results.append(kept((8, 128), F32))
        result_specs.append(ANY)
        more, own = len(ahead), len(results)

        def body(*refs):
            refs = list(refs)
            mine, refs = refs[: 1 + count], refs[1 + count + len(deps) :]
            sources, refs = refs[:more], refs[more:]
            made, refs = refs[:own], refs[own:]
            targets, refs = refs[:more], refs[more:]
            made.pop()
            if not more:
                return kernel(*mine, *made, *refs)
            sem = refs.pop()
            copies = [
                pltpu.make_async_copy(src if index is None else src.at[index], dst, sem.at[n])
                for n, (src, dst, (_, index)) in enumerate(zip(sources, targets, ahead))
            ]

            @pl.when(pl.program_id(0) == 0)
            def _():
                for copy in copies:
                    copy.start()

            kernel(*mine, *made, *refs)

            @pl.when(pl.program_id(0) == pl.num_programs(0) - 1)
            def _():
                for copy in copies:
                    copy.wait()

        results += [inside(a.shape if index is None else a.shape[1:], a.dtype) for a, index in ahead]
        if more:
            scratch = list(scratch) + [pltpu.SemaphoreType.DMA((more,))]

        run = pl.pallas_call(
            body,
            grid_spec=pltpu.PrefetchScalarGridSpec(
                num_scalar_prefetch=1,
                grid=grid,
                in_specs=list(in_specs) + [ANY] * (len(deps) + more),
                out_specs=result_specs + [IN] * more,
                scratch_shapes=list(scratch),
            ),
            out_shape=results,
            compiler_params=pltpu.CompilerParams(vmem_limit_bytes=vmem * MIB),
            cost_estimate=pl.CostEstimate(flops=weight, bytes_accessed=1, transcendentals=0),
        )

        def go(*args):
            pinned = []
            for a, spec in zip(args, in_specs):
                if id(a) in resident:
                    a = pltpu.with_memory_space_constraint(a, pltpu.VMEM)
                elif spec is not IN and place is not None:
                    a = pltpu.with_memory_space_constraint(a, pltpu.HBM if spec is ANY else place)
                pinned.append(a)
            sources = [pltpu.with_memory_space_constraint(a, pltpu.HBM) for a, _ in ahead]
            out = run(info, *pinned, *deps, *sources)
            for a, like in zip(out, results):
                if not isinstance(like, jax.ShapeDtypeStruct) and like.memory_space == pltpu.VMEM:
                    resident[id(a)] = a
            out = list(out)
            before[:] = [out.pop(own - 1)]
            return out if len(out) > 1 else out[0]

        return go

    def partner(value, x):
        return lax.ppermute(value, "tile", [(t, t ^ x) for t in range(tiles)])

    def exchange(rims):
        return [partner(v, x + 1) for x, v in enumerate(rims)]

    def swap(value, bit):
        if bit < 2:
            return partner(value, 1 << bit)
        return lax.ppermute(value, "dp", [(d, d ^ (1 << (bit - 2))) for d in range(pages)])

    def both(value):
        return value, partner(value, 1)

    def vm(dims, dtype):
        return pltpu.VMEM(dims, dtype)

    sems = pltpu.SemaphoreType.DMA((40,))
    row_w, par = whole((rows, width)), whole((layers, width))
    wide = whole((rows, 3 * width))
    pc_rows, pr_rows, pd_rows = side * PAD + 16, RADIUS * side + 16, (RADIUS + 1) * PAD + 16
    rim_shapes = [shape((n, 2 * width), BF) for n in (pc_rows, pr_rows, pd_rows)]
    rim_specs = [whole(s.shape) for s in rim_shapes]
    stat_spec = pl.BlockSpec((16, 2 * width), lambda *_: (side * PAD // 16, 0))
    nb, ng = sz.blocks, sz.groups
    square = (width, width)

    x, qkv, *rims = call(
        functools.partial(first_kernel, sz),
        (1,),
        [whole((cells, width)), whole((1, width)), par, whole((8, cells)), ANY],
        [IN] * 5,
        [inside((rows, width), F32), inside((rows, 3 * width), BF)] + rim_shapes,
        [vm((rows, width), BF), vm((width, 3 * width), BF), sems],
    )(patch_in.reshape(cells, width), cls_in, norm_attn, own_mask, qkv_weight)
    got = exchange(rims)
    bias, w_out, w_up, w_down, gain_a, scale_a, gain_m, scale_m = call(
        lambda info, *refs: bias_kernel(sz, *refs),
        (layers,),
        [pl.BlockSpec((None, 16, sz.bk), lambda l, s: (l, 0, 0))],
        pl.BlockSpec((None, ng, sz.bk, sz.bk), lambda l, s: (l, 0, 0, 0)),
        inside((layers, ng, sz.bk, sz.bk), F32),
        [vm((sz.bk, sz.bk), F32)],
        ahead=[(out_weight, 0), (up_weight, 0), (down_weight, 0)]
        + [(v, None) for v in (norm_attn, scale_attn, norm_mlp, scale_mlp)],
    )(lines)
    saved = []
    for l in range(layers):
        last = l == layers - 1
        given = dict(qkv=qkv, pc=rims[0], rc=got[0], rr=got[1], rd=got[2], bias=bias, mask=key_mask, x=x, own_mask=own_mask,
                     scale_a=scale_a, gain_m=gain_m, scale_m=scale_m, gain_a=gain_a,
                     w_out=w_out, w_up=w_up, w_down=w_down)
        left_width = 2 * width + hidden + (0 if last else width) + (0 if l else width)
        held = dict(p=((nb * ng, sz.bk, sz.bk), BF), kb=((nb, sz.bk, width), BF), vb=((nb, sz.bk, width), BF),
                    left=((rows, left_width), BF))
        local_only = dict(slope=((rows, hidden), BF), x1=((rows, width), F32), br=((rows, width), BF), down=((rows, width), BF))
        made = dict(stats=inside((8, width), F32))
        spots = dict(kext=vm((sz.ext_rows, width), F32), vext=vm((sz.ext_rows, width), F32), acc=vm((rows, width), F32))
        spots.update({n: vm(*d) for n, d in local_only.items()})
        if last:
            given.update(cot=cot, cls_cot=cls_cot, valid=valid)
            made.update({n: inside(*d) for n, d in held.items()})
            made.update(right=inside((rows, 2 * width + hidden), BF), g1=inside((rows, width), F32), vec=inside((8, width), F32),
                        patch_out=shape((cells, width), BF), cls_out=shape((1, width), BF))
            specs = [IN] * len(made)
        else:
            given.update(qkv_w=qkv_weight)
            made.update(x2=inside((rows, width), F32), next=inside((rows, 3 * width), BF),
                        pc_out=rim_shapes[0], pr_out=rim_shapes[1], pd_out=rim_shapes[2])
            specs = [IN] * len(made)
            spots.update({n: vm(*d) for n, d in held.items()})
            spots.update(w_qkv=vm((width, 3 * width), BF))
            stored = dict(held, **local_only, qkv=((rows, 3 * width), BF))
            made = dict({n + "_out": kept(*d) for n, d in stored.items()}, **made)
            specs = [ANY] * len(stored) + specs
        spots.update(sems=sems)
        names = list(given) + list(made) + list(spots)
        out = call(functools.partial(middle_kernel, sz, l, last, names), (1,),
                   [ANY if n == "qkv_w" else IN for n in given], specs, list(made.values()), list(spots.values()), vmem=18 if last else 28,
                   )(*given.values())
        res = dict(zip(made, out))
        keep_names = list(held) if last else list(stored)
        entry = {n: res[n if last else n + "_out"] for n in keep_names}
        entry.setdefault("qkv", qkv)
        entry.update(x=x, stats=res["stats"])
        entry["left"] = both(entry["left"])
        entry["h"] = (entry["left"], left_width // width - 1) if l == 0 else (saved[l - 1]["left"], 2 + chunks)
        saved.append(entry)
        if last:
            patch_out, cls_out, right, g1, vec = (res[n] for n in ("patch_out", "cls_out", "right", "g1", "vec"))
        else:
            x, qkv = res["x2"], res["next"]
            rims = [res[n] for n in ("pc_out", "pr_out", "pd_out")]
            got = exchange(rims)
            w_out, w_up, w_down, cot = call(
                lambda info, a: None, (1,), [IN], [], [],
                ahead=[(out_weight, l + 1), (up_weight, l + 1), (down_weight, l + 1), (patch_cot.reshape(cells, width), None)],
                vmem=2,
            )(own_mask)

    def attention_back(l, right, v, also):
        return call(
            functools.partial(attention_back_kernel, sz, l),
            (1,),
            [IN] * 8,
            [IN] * 6,
            [inside((cells, width), BF), inside((cells, 2 * width), F32)] + rim_shapes + [inside((16, sz.bk), F32)],
            [vm((sz.ext_rows, width), F32)] * 2 + [vm((rows, width), F32), vm((ng, sz.bk, sz.bk), F32)],
            also=also,
        )(right, v["qkv"], v["stats"], own_mask, v["p"], v["kb"], v["vb"], v["w_out"])

    back_scratch = [vm((cells, 2 * width), F32), vm((rows, width), F32)]

    def qkv_back(l, d_q, d_kv, own, got, g1, vec, table, wq):
        *e_qkv, rows_small, g, down_w, up_w = call(
            functools.partial(qkv_back_kernel, sz, l),
            (1,),
            [IN] * 12,
            [IN] * 5,
            [inside((rows, width), BF)] * 3 + [inside((24, width), F32), inside((rows, width), F32)],
            back_scratch + [vm((rows, 3 * width), BF)],
            weight=LONG, ahead=[(down_weight, l - 1), (up_weight, l - 1)],
        )(d_q, d_kv, own, *got, saved[l]["x"], g1, vec, table, gain_a, wq)
        return [both(e) for e in e_qkv], rows_small, g, up_w, down_w

    def mlp_back(l, g, up_w, down_w):
        v = saved[l]
        names = ["qkv", "p", "kb", "vb"]
        out = call(
            functools.partial(mlp_back_kernel, sz, l),
            (1,),
            [IN] * 10,
            [IN] * 3,
            [inside((rows, 2 * width + hidden), BF), inside((rows, width), F32), inside((8, width), F32)],
            [vm((rows, width), F32)],
            ahead=[(v[n], None) for n in names] + [(out_weight, l)],
        )(g, gain_m, scale_a, scale_m, v["x1"], v["br"], v["down"], v["slope"], up_w, down_w)
        near = dict(zip(names + ["w_out"], out[3:]), stats=v["stats"])
        return out[0], out[1], out[2], near

    def finish(d_q, d_kv, own, got, g1, vec, table, wq, first):
        return call(
            functools.partial(last_kernel, sz),
            (1,),
            [IN] * 13,
            [IN] * 6,
            [inside((rows, width), BF)] * 3 + [inside((24, width), F32), shape((cells, width), F32), shape((1, width), F32)],
            back_scratch + [vm((rows, width), F32), vm((rows, 3 * width), BF)],
        )(d_q, d_kv, own, *got, first, cls_in, g1, vec, table, gain_a, wq)

    piece, ff_piece = width // sz.devices, hidden // sz.devices
    half = width // 2
    quarter = sz.devices // 4

    def pair(dims):
        return [shape(dims, BF), inside(dims, BF)]

    def halves(start):
        return pl.BlockSpec((rows, half), lambda i, s: (0, 2 * start + s[1]))

    def grad_down(act, e_down, weight=1, also=()):
        lspec = pl.BlockSpec((rows, width), lambda i, s: (0, act[1] + s[1] * (chunks // 2) + i))
        rspec = pl.BlockSpec((rows, width), lambda i, s: (0, e_down[1]))
        out = pl.BlockSpec((None, quarter // 2, ff_piece, width), lambda i, s: (i ^ s[3], 0, 0, 0))
        return call(
            functools.partial(down_kernel, sz),
            (2,),
            [lspec, lspec, rspec, rspec],
            [out, out],
            pair((2, quarter // 2, ff_piece, width)),
            weight=weight, also=also,
            vmem=20, place=None,
        )(*act[0], *e_down[0])

    def grad_up(h2, e_up, also, ahead):
        lspec = halves(h2[1])
        rspec = pl.BlockSpec((rows, width), lambda i, s: (0, e_up[1] + i))
        out = pl.BlockSpec((quarter, None, piece, width), lambda i, s: (0, i, 0, 0))
        return call(
            functools.partial(up_kernel, sz),
            (chunks,),
            [lspec, lspec, rspec, rspec],
            [out, out],
            pair((quarter, chunks, piece, width)),
            also=also, vmem=20, place=None, ahead=ahead,
        )(*h2[0], *e_up[0])

    def grad_attn(h, e_qkv, att, e_branch):
        out = pl.BlockSpec((None, quarter, None, piece, width), lambda i, s: (i // 2, 0, i % 2, 0, 0))
        hspec, aspec = halves(h[1]), halves(att[1])
        bspec = pl.BlockSpec((rows, width), lambda i, s: (0, e_branch[1]))
        return call(
            functools.partial(attn_grad_kernel, sz),
            (4,),
            [hspec, hspec] + [row_w] * 6 + [aspec, aspec, bspec, bspec],
            [out, out],
            pair((2, quarter, 2, piece, width)),
            vmem=20, place=None,
        )(*h[0], *(v for both_e in e_qkv for v in both_e), *att[0], *e_branch[0])

    def last_route(flip):
        out = []
        for d in range(sz.devices):
            high, core = d >> top_bit, d & 1
            out.append((d, (d & ~(1 << top_bit) & ~1) | core << top_bit | (high ^ flip)))
        return out

    class ZSums:
        def __init__(self, halves_made):
            send, keep = halves_made
            self.n = quarter * 2 * piece // 2
            self.got = swap(send, next_bit).reshape(2, 2, self.n, width)
            self.keep = keep.reshape(2, 2, self.n, width)

        def second(self, weight=1):
            n = self.n
            s0, s1, k = call(
                z_second_kernel, (1,), [whole((2, 2, n, width))] * 2, [whole((n, width))] * 2 + [whole((2, n, width))],
                [shape((n, width), BF)] * 2 + [inside((2, n, width), BF)], place=None, weight=weight,
            )(self.keep, self.got)
            self.got = [swap(s0, 1), swap(s1, 2)]
            self.keep = k

        def third(self):
            n = self.n = self.n // 2
            s0, s1, k = call(
                z_third_kernel, (1,), [whole((2, 2, n, width))] + [whole((2, n, width))] * 2,
                [whole((n, width))] * 2 + [whole((2, n, width))],
                [shape((n, width), BF)] * 2 + [inside((2, n, width), BF)], place=None,
            )(self.keep.reshape(2, 2, n, width), *(g.reshape(2, n, width) for g in self.got))
            self.got = [swap(s0, 2), swap(s1, 1)]
            self.keep = k
            for bit in range(bits - 3, 2, -1):
                n = self.n = self.n // 2
                spec = whole((2, 2, n, width))
                s, k = call(
                    more_kernel, (1,), [spec, spec], [whole((2, n, width))] * 2, pair((2, n, width)), place=None,
                )(self.keep.reshape(2, 2, n, width), jnp.stack(self.got).reshape(2, 2, n, width))
                self.keep = k
                self.got = list(swap(s, bit))

        def fourth(self):
            n = self.n = self.n // 2
            a, b = call(
                functools.partial(z_fourth_kernel, sz), (1,), [whole((2, 2, n, width))] + [whole((2, n, width))] * 2,
                [whole((2, n, width))] * 2, [shape((2, n, width), BF)] * 2, place=None,
            )(self.keep.reshape(2, 2, n, width), *(g.reshape(2, n, width) for g in self.got))
            self.got = [lax.ppermute(a, ("dp", "tile"), last_route(0)), lax.ppermute(b, ("dp", "tile"), last_route(1))]

        def result(self):
            return self.got[0].astype(F32) + self.got[1].astype(F32)

    class Sums:
        def __init__(self, y_first, x_first, split):
            (s0, k0), (s1, k1) = y_first, x_first
            self.got = [swap(s0, 1), swap(s1, 2)]
            total = s0.size // width
            self.block = total // (quarter // 2)
            self.outer = split
            self.rows = total
            self.keep = [k0.reshape(1, 2, total // 2, width), k1.reshape(split, 2, total // 2 // split, width)]

        def second(self, weight=1, also=()):
            n = self.rows // 4
            got = [g.reshape(k.shape) for g, k in zip(self.got, self.keep)]
            sp = self.outer
            if sp == 1:
                other = pl.BlockSpec((1, 2, n, width), lambda i, s: (0, 0, i, 0))
                other_out = pl.BlockSpec((1, n, width), lambda i, s: (0, i, 0))
            else:
                other = pl.BlockSpec((1, 2, n, width), lambda i, s: (i, 0, 0, 0))
                other_out = pl.BlockSpec((1, n, width), lambda i, s: (i, 0, 0))
            spec = pl.BlockSpec((1, 2, n, width), lambda i, s: (0, 0, i, 0))
            spec_out = pl.BlockSpec((1, n, width), lambda i, s: (0, i, 0))
            s0, k0, s1, k1 = call(
                second_kernel, (2,), [spec, spec, other, other], [spec_out, spec_out, other_out, other_out],
                pair((1, 2 * n, width)) + pair((sp, 2 * n // sp, width)), weight=weight, place=None, also=also,
            )(self.keep[0], got[0], self.keep[1], got[1])
            self.got = [swap(s0, 2), swap(s1, 1)]
            self.keep = [k0, k1]
            self.rows //= 2

        def third(self, weight=1):
            n = self.rows // 2
            args = [v.reshape(2, n, width) for pair in zip(self.keep, self.got) for v in pair]
            s, k = call(
                third_kernel, (1,), [whole((2, n, width))] * 4, [whole((2, n, width))] * 2,
                pair((2, n, width)), weight=weight, place=None,
            )(*args)
            self.rows = n
            self.keep = k
            self.got = swap(s, bits - 2)
            for bit in range(bits - 3, 2, -1):
                n = self.rows // 2
                spec = whole((2, 2, n, width))
                s, k = call(
                    more_kernel, (1,), [spec, spec], [whole((2, n, width))] * 2, pair((2, n, width)), place=None,
                )(self.keep.reshape(2, 2, n, width), self.got.reshape(2, 2, n, width))
                self.rows = n
                self.keep = k
                self.got = swap(s, bit)

        def fourth(self):
            n = self.rows // 2
            spec = whole((2, 2, n, width))
            a, b = call(
                functools.partial(fourth_kernel, sz), (1,), [spec, spec], [whole((2, n, width))] * 2,
                [shape((2, n, width), BF)] * 2, place=None,
            )(self.keep.reshape(2, 2, n, width), self.got.reshape(2, 2, n, width))

            self.got = [lax.ppermute(a, ("dp", "tile"), last_route(0)), lax.ppermute(b, ("dp", "tile"), last_route(1))]

        def result(self):
            return self.got[0].astype(F32) + self.got[1].astype(F32)

    sums = {}
    small = [None] * layers
    early = [v["left"][1] for v in saved[:-1]]
    waiting = None
    near = dict(saved[-1], w_out=w_out)
    for l in reversed(range(layers)):
        left = saved[l]["left"]
        result = attention_back(l, right, near, early)
        d_q, d_kv, *rims, table = result
        early = []
        if waiting is not None:
            right = both(lax.optimization_barrier((right, table))[0])
            got = exchange(rims)
            sums["attn", l + 1] = ZSums(grad_attn(*waiting))
            sums["mlp", l + 1].second(LONG)
        else:
            right = both(right)
            got = exchange(rims)
        x_first = grad_down((left, 2), (right, 0))
        *y_first, wq = grad_up((left, 1), (right, 1), got if waiting is not None else (), [(qkv_weight, l)])
        sums["mlp", l] = Sums(y_first, x_first, 2)
        if l > 0:
            e_qkv, small[l], g, up_w, down_w = qkv_back(l, d_q, d_kv, rims[0], got, g1, vec, table, wq)
            waiting = (saved[l]["h"], e_qkv, (left, 0), (right, 1 + chunks))
            right, g1, vec, near = mlp_back(l - 1, g, up_w, down_w)
        else:
            *e_qkv, small[0], patch_grad, cls_grad = finish(d_q, d_kv, rims[0], got, g1, vec, table, wq, patch_in.reshape(cells, width))
            waiting = (saved[0]["h"], [both(e) for e in e_qkv], (left, 0), (right, 1 + chunks))
    total = [jnp.stack(small), None, 0]

    def step():
        value, got_value, bit = total
        if got_value is not None:
            value = value + lax.optimization_barrier((got_value, before[0]))[0]
        total[:] = [value, swap(value, bit) if bit < bits else None, bit + 1]

    step()
    if layers > 1:
        sums["mlp", 1].third()
    sums["attn", 0] = ZSums(grad_attn(*waiting))
    step()
    if layers > 1:
        sums["attn", 1].second(MEDIUM)
    sums["mlp", 0].second()
    step()
    if layers > 1:
        sums["attn", 1].third()
        sums["mlp", 1].fourth()
    sums["mlp", 0].third()
    step()
    sums["attn", 0].second()
    if layers > 1:
        sums["attn", 1].fourth()
    step()
    sums["attn", 0].third()
    sums["mlp", 0].fourth()
    while total[1] is not None:
        step()
    sums["attn", 0].fourth()
    total = total[0]
    ups, downs, firsts, seconds = [], [], [], []
    for l in range(layers):
        mlp, attn = sums["mlp", l].result(), sums["attn", l].result()
        ups.append(jnp.swapaxes(mlp[0].reshape(chunks, piece, width), 0, 1).reshape(piece, hidden))
        downs.append(mlp[1])
        attn = attn.reshape(4, piece, width)
        firsts.append(jnp.swapaxes(attn[:3], 0, 1).reshape(piece, 3 * width))
        seconds.append(attn[3])
    g_qkv, g_out, g_up, g_down = (jnp.stack(v) for v in (firsts, seconds, ups, downs))
    vectors, tables = total[:, 0:4], total[:, 8 : 8 + heads, 0 : sz.bk]
    mine = lax.dynamic_slice_in_dim(vectors, me * piece, piece, axis=2)
    tables = tables[:, :, first_slot : first_slot + SPAN * sz.pitch].reshape(layers, heads, SPAN, sz.pitch)
    g_table = tables[..., :SPAN].reshape(rel_table.shape)
    return (
        patch_out.reshape(patch_in.shape),
        cls_out,
        patch_grad.reshape(patch_in.shape),
        cls_grad,
        mine[:, 3],
        g_qkv,
        g_table,
        g_out,
        mine[:, 2],
        mine[:, 1],
        g_up,
        g_down,
        mine[:, 0],
    )


def solution(mesh):
    tokens = P("dp", "tile", None, None, None)
    split = ("dp", "tile")
    in_specs = (tokens, P("dp", None), P("dp")) + (P(),) * 9 + (tokens, P("dp", None))
    out_specs = (
        tokens,
        P("dp", None),
        tokens,
        P("dp", None),
        P(None, split),
        P(None, split, None),
        P(),
        P(None, split, None),
        P(None, split),
        P(None, split),
        P(None, split, None),
        P(None, split, None),
        P(None, split),
    )
    return jax.shard_map(local, mesh=mesh, in_specs=in_specs, out_specs=out_specs, check_vma=False)
```

```python
import functools

import jax
import jax.numpy as jnp
import numpy as np
from jax import lax
from jax.experimental import pallas as pl
from jax.experimental.pallas import tpu as pltpu
from jax.sharding import PartitionSpec as P

RADIUS = 3
SPAN = 2 * RADIUS + 1
PAD = 8
EPS = 1e-06
MASKED = -1e30
BF = jnp.bfloat16
F32 = jnp.float32
MIB = 1 << 20


def dot(a, b):
    return lax.dot_general(a, b, (((1,), (0,)), ((), ())), preferred_element_type=F32)


def dot_nt(a, b):
    return lax.dot_general(a, b, (((1,), (1,)), ((), ())), preferred_element_type=F32)


def dot_tn(a, b):
    return lax.dot_general(a, b, (((0,), (0,)), ((), ())), preferred_element_type=F32)


def normalized(x):
    centred = x - jnp.mean(x, axis=-1, keepdims=True)
    inverse = lax.rsqrt(jnp.mean(centred * centred, axis=-1, keepdims=True) + EPS)
    return centred * inverse, inverse


def norm_back(x, gain, d_out):
    unit, inverse = normalized(x)
    d_unit = d_out * gain
    d_x = inverse * (
        d_unit
        - jnp.mean(d_unit, axis=-1, keepdims=True)
        - unit * jnp.mean(d_unit * unit, axis=-1, keepdims=True)
    )
    return d_x, d_out * unit


def split3(x):
    high = x.astype(BF).astype(F32)
    rest = x - high
    middle = rest.astype(BF).astype(F32)
    return high, middle, rest - middle


def lane_heads(rows, lanes, width):
    return lax.broadcasted_iota(jnp.int32, (rows, lanes), 1) // width


def head_rows(rows, lanes, width):
    return lane_heads(rows, lanes, width) == lax.broadcasted_iota(jnp.int32, (rows, lanes), 0)


def stacked_heads(block, width):
    rows, lanes = block.shape
    heads = lane_heads(rows, lanes, width)
    zero = jnp.zeros_like(block)
    return jnp.concatenate(
        [jnp.where(heads == h, block, zero) for h in range(lanes // width)], axis=0
    )


def folded_heads(stack, width):
    count = stack.shape[1] // width
    rows = stack.shape[0] // count
    heads = lane_heads(rows, stack.shape[1], width)
    out = stack[:rows]
    for h in range(1, count):
        out = jnp.where(heads == h, stack[h * rows : (h + 1) * rows], out)
    return out


def keep_rows(rows, cells, class_weight):
    row = lax.broadcasted_iota(jnp.int32, (rows, 1), 0)
    return jnp.where(row < cells, 1.0, jnp.where(row == cells, class_weight, 0.0))


class Sizes:
    def __init__(self, side, width, hidden, heads, devices):
        self.side = side
        self.cells = side * side
        self.rows = self.cells + 16
        self.width = width
        self.hidden = hidden
        self.heads = heads
        self.head = width // heads
        self.pitch = side + PAD
        self.ext = side + 2 * RADIUS
        self.ext_rows = self.pitch * self.ext + PAD
        self.brows = 4
        self.blocks = side // self.brows
        self.bq = self.brows * side
        self.bk = 256
        self.class_slot = self.bk - PAD
        self.quad = 4 * self.head
        self.groups = width // self.quad
        self.devices = devices
        self.bits = devices.bit_length() - 1


def stat_rows(values):
    width = values[0].shape[1]
    parts = [split3(v) for v in values]
    flat = [p[k] for k in range(3) for p in parts]
    if len(flat) % 2:
        flat.append(jnp.zeros_like(flat[0]))
    row = lax.broadcasted_iota(jnp.int32, (16, 2 * width), 0)
    out = jnp.zeros((16, 2 * width), F32)
    for i in range(0, len(flat), 2):
        out = jnp.where(row == i // 2, jnp.concatenate(flat[i : i + 2], axis=1), out)
    return out.astype(BF)


def read_stats(block, count, width):
    rows = block.astype(F32)

    def piece(i):
        return rows[i // 2 : i // 2 + 1, (i % 2) * width : (i % 2 + 1) * width]

    return [piece(i) + piece(count + i) + piece(2 * count + i) for i in range(count)]


def in_tile_order(info, pieces):
    me = info[0] * 2 + info[1]
    out = []
    for t in range(4):
        d = me ^ t
        out.append(
            [
                jnp.where(d == 0, a, jnp.where(d == 1, b, jnp.where(d == 2, c, e)))
                for a, b, c, e in zip(*pieces)
            ]
        )
    return out


def class_scores(sz, info, qkv_ref, mask):
    cells, width = sz.cells, sz.width
    own = head_rows(16, width, sz.head)
    class_rows = qkv_ref[cells : cells + 16, :].astype(F32)
    q_c, k_c, v_c = (class_rows[0:1, i * width : (i + 1) * width] for i in range(3))
    q_heads = jnp.where(own, q_c, 0.0)
    scale = sz.head ** (-0.5)
    scores = dot_nt(q_heads.astype(BF), qkv_ref[0:cells, width : 2 * width]) * scale + mask
    self_score = jnp.sum(q_heads * k_c, axis=1, keepdims=True) * scale
    self_score = jnp.where(info[2] == 1, self_score, MASKED)
    return own, q_heads, k_c, v_c, scores, self_score


def send_rims(sz, info, kv_half, kv_edge_rows, stats, pc_ref, pr_ref, pd_ref):
    side, width = sz.side, sz.width
    cells8 = [kv_half(r) for r in range(side)]
    pc_ref[0 : side * PAD, :] = jnp.concatenate(cells8, axis=0).astype(BF)
    pc_ref[side * PAD : side * PAD + 16, :] = stats
    edge, corner = kv_edge_rows()
    pr_ref[0 : RADIUS * side, :] = jnp.concatenate(edge, axis=0).astype(BF)
    pr_ref[RADIUS * side : RADIUS * side + 16, :] = stats
    zero = jnp.zeros((PAD, 2 * width), F32)
    pd_ref[0 : (RADIUS + 1) * PAD, :] = jnp.concatenate(corner + [zero], axis=0).astype(BF)
    pd_ref[(RADIUS + 1) * PAD : (RADIUS + 1) * PAD + 16, :] = stats


def rim_places(sz, info):
    return sz.pitch * (1 - info[1]), (sz.side + RADIUS) * (1 - info[0])


GELU_C = float(np.sqrt(2.0 / np.pi))


class Copies:
    def __init__(self, sems):
        self.sems, self.count, self.out = sems, 0, []

    def load(self, src, dst):
        copy = pltpu.make_async_copy(src, dst, self.sems.at[self.count])
        self.count += 1
        copy.start()
        return copy

    def store(self, src, dst):
        self.out.append(self.load(src, dst))

    def finish(self):
        for copy in self.out:
            copy.wait()


def qkv_part(sz, info, x, gain, wq, loads, mask, h_ref, qkv_ref, pc_ref, pr_ref, pd_ref):
    width, side, cells = sz.width, sz.side, sz.cells
    unit, _ = normalized(x)
    h = (unit * gain).astype(BF)
    h_ref[...] = h
    for i in range(3):
        loads[i].wait()
        cols = slice(i * width, (i + 1) * width)
        qkv_ref[:, cols] = dot(h, wq[:, cols]).astype(BF)
    own, q_heads, k_c, v_c, scores, self_score = class_scores(sz, info, qkv_ref, mask)
    top = jnp.maximum(jnp.max(scores, axis=1, keepdims=True), self_score)
    probs = jnp.where(mask > -1.0, jnp.exp(scores - top), 0.0)
    self_prob = jnp.where(info[2] == 1, jnp.exp(self_score - top), 0.0)
    total = jnp.sum(probs, axis=1, keepdims=True) + self_prob
    part = dot(probs.astype(BF), qkv_ref[0:cells, 2 * width :]) + self_prob * v_c

    def to_row(v):
        return jnp.sum(jnp.where(own, v, 0.0), axis=0, keepdims=True)

    stats = stat_rows([to_row(part), to_row(top), to_row(total)])
    left_col = info[1] == 0

    def half(r):
        row = qkv_ref[r * side : (r + 1) * side, width:].astype(F32)
        return jnp.where(left_col, row[PAD:], row[:PAD])

    def edges():
        first = pl.multiple_of((1 - info[0]) * (side - RADIUS) * side, 16)
        rows = qkv_ref[pl.ds(first, RADIUS * side), width:].astype(F32)
        edge = [rows[t * side : (t + 1) * side] for t in range(RADIUS)]
        return edge, [jnp.where(left_col, e[PAD:], e[:PAD]) for e in edge]

    send_rims(sz, info, half, edges, stats, pc_ref, pr_ref, pd_ref)


def first_kernel(sz, info, patch_ref, cls_ref, gain_ref, mask_ref, w_any,
                 x_ref, qkv_ref, pc_ref, pr_ref, pd_ref, h_v, wq, sems):
    copies = Copies(sems)
    width = sz.width
    loads = [copies.load(w_any.at[0, :, pl.ds(i * width, width)], wq.at[:, pl.ds(i * width, width)]) for i in range(3)]
    row = lax.broadcasted_iota(jnp.int32, (16, width), 0)
    x_ref[0 : sz.cells, :] = patch_ref[...].astype(F32)
    x_ref[sz.cells :, :] = jnp.where(row == 0, cls_ref[...].astype(F32), 0.0)
    qkv_part(sz, info, x_ref[...], gain_ref[0:1, :], wq, loads, mask_ref[0:1, :], h_v, qkv_ref, pc_ref, pr_ref, pd_ref)


def extended(sz, info, qkv_ref, rc_ref, rr_ref, rd_ref, kext, vext):
    width, side, pitch = sz.width, sz.side, sz.pitch
    beside, above = rim_places(sz, info)
    for ext, lo in ((kext, width), (vext, 2 * width)):
        at = lo - width
        ext[...] = jnp.zeros_like(ext)
        for r in range(side):
            base = pitch * (r + RADIUS)
            ext[base + PAD : base + PAD + side, :] = qkv_ref[r * side : (r + 1) * side, lo : lo + width].astype(F32)
        sides = rc_ref[0 : side * PAD, at : at + width].astype(F32)
        for r in range(side):
            ext[pl.ds(pl.multiple_of(pitch * (r + RADIUS) + beside, 8), PAD), :] = sides[r * PAD : (r + 1) * PAD]
        edge = rr_ref[0 : RADIUS * side, at : at + width].astype(F32)
        corner = rd_ref[0 : (RADIUS + 1) * PAD, at : at + width].astype(F32)
        for t in range(RADIUS):
            base = pitch * (above + t)
            ext[pl.ds(pl.multiple_of(base + PAD, 8), side), :] = edge[t * side : (t + 1) * side]
            ext[pl.ds(pl.multiple_of(base + beside, 8), PAD), :] = corner[t * PAD : (t + 1) * PAD]


def all_stats(sz, info, st_ref, rc_ref, rr_ref, rd_ref):
    side, width = sz.side, sz.width
    return in_tile_order(info, [read_stats(r, 3, width) for r in (
        st_ref[side * PAD : side * PAD + 16, :],
        rc_ref[side * PAD : side * PAD + 16, :],
        rr_ref[RADIUS * side : RADIUS * side + 16, :],
        rd_ref[(RADIUS + 1) * PAD : (RADIUS + 1) * PAD + 16, :],
    )])


def middle_kernel(sz, layer, last, names, info, *refs):
    r = dict(zip(names, refs))
    qkv_ref, rc_ref, rr_ref, rd_ref = r["qkv"], r["rc"], r["rr"], r["rd"]
    st_ref, bias_ref, mask_ref, x_ref = r["pc"], r["bias"], r["mask"], r["x"]
    scale_a_ref, gain_m_ref, scale_m_ref, gain_a_ref = r["scale_a"], r["gain_m"], r["scale_m"], r["gain_a"]
    w_out, w_up, w_down, stat_ref = r["w_out"], r["w_up"], r["w_down"], r["stats"]
    p_v, kb_v, vb_v, slope_v, x1_v, br_v, down_v, left = (r[n] for n in ("p", "kb", "vb", "slope", "x1", "br", "down", "left"))
    kext, vext, acc = r["kext"], r["vext"], r["acc"]
    width, side, cells, pitch, hidden = sz.width, sz.side, sz.cells, sz.pitch, sz.hidden
    chunks = hidden // width
    copies = Copies(r["sems"])

    def hold(name, cols=None):
        if not last:
            src, dst = r[name], r[name + "_out"]
            if cols is not None:
                at = pl.ds(cols[0], cols[1])
                src, dst = src.at[:, at], dst.at[:, at]
            copies.store(src, dst)

    if not last:
        qkv_loads = [
            copies.load(r["qkv_w"].at[layer + 1, :, pl.ds(i * width, width)], r["w_qkv"].at[:, pl.ds(i * width, width)])
            for i in range(3)
        ]
        hold("qkv")
    extended(sz, info, qkv_ref, rc_ref, rr_ref, rd_ref, kext, vext)
    if layer == 0:
        left[:, left.shape[1] - width :] = (normalized(x_ref[...])[0] * gain_a_ref[0:1, :]).astype(BF)
    class_rows = qkv_ref[cells : cells + 16, :].astype(F32)[0:PAD]
    scale = sz.head ** (-0.5)
    for b in range(sz.blocks):
        first = b * sz.brows * pitch
        kb = jnp.concatenate([kext[first : first + sz.class_slot, :], class_rows[:, width : 2 * width]], axis=0).astype(BF)
        vb = jnp.concatenate([vext[first : first + sz.class_slot, :], class_rows[:, 2 * width :]], axis=0).astype(BF)
        kb_v[b] = kb
        vb_v[b] = vb
        q = qkv_ref[b * sz.bq : (b + 1) * sz.bq, 0:width] * jnp.asarray(scale, BF)
        mask = mask_ref[b]
        mask = jnp.concatenate([mask, mask], axis=1)
        for g in range(sz.groups):
            lanes = slice(g * sz.quad, (g + 1) * sz.quad)
            scores = dot_nt(kb[:, lanes], stacked_heads(q[:, lanes], sz.head)) + bias_ref[layer, g] + mask
            top = jnp.max(scores, axis=0, keepdims=True)
            probs = jnp.exp(scores - top)
            total = jnp.sum(probs, axis=0, keepdims=True)
            probs = (probs * (1.0 / total)).astype(BF)
            p_v[b * sz.groups + g] = probs
            out = folded_heads(dot_tn(probs, vb[:, lanes]), sz.head)
            left[b * sz.bq : (b + 1) * sz.bq, lanes] = out.astype(BF)
    for name in ("p", "kb", "vb"):
        hold(name)
    ordered = all_stats(sz, info, st_ref, rc_ref, rr_ref, rd_ref)
    top = functools.reduce(jnp.maximum, [s[1] for s in ordered])
    total = jnp.zeros_like(top)
    summed = jnp.zeros_like(top)
    for part, part_top, part_total in ordered:
        factor = jnp.exp(part_top - top)
        total = total + part_total * factor
        summed = summed + part * factor
    class_out = summed / total
    stat_ref[...] = jnp.zeros_like(stat_ref)
    stat_ref[0:1, :] = top
    stat_ref[1:2, :] = total
    stat_ref[2:3, :] = class_out
    row = lax.broadcasted_iota(jnp.int32, (16, width), 0)
    left[cells : cells + 16, 0:width] = jnp.where(row == 0, class_out, 0.0).astype(BF)
    branch = dot(left[:, 0:width], w_out[...])
    br_v[...] = branch.astype(BF)
    x1_v[...] = x_ref[...] + scale_a_ref[layer : layer + 1, :] * branch
    unit, _ = normalized(x1_v[...])
    left[:, width : 2 * width] = (unit * gain_m_ref[layer : layer + 1, :]).astype(BF)
    hold("br")
    hold("x1")
    hold("left", (0, 2 * width))
    for c in range(chunks):
        at = slice(c * width, (c + 1) * width)
        u = dot(left[:, width : 2 * width], w_up[:, at])
        square = u * u
        th = jnp.tanh(GELU_C * u * (1.0 + 0.044715 * square))
        half = 0.5 * (1.0 + th)
        here = slice((c + 2) * width, (c + 3) * width)
        left[:, here] = (u * half).astype(BF)
        slope = half + (0.5 * u) * (1.0 - th * th) * (GELU_C + (3 * 0.044715 * GELU_C) * square)
        slope_v[:, at] = slope.astype(BF)
        part = dot(left[:, here], w_down[at, :])
        if c == 0:
            acc[...] = part
        else:
            acc[...] += part
    down_v[...] = acc[...].astype(BF)
    hold("slope")
    hold("down")
    hold("left", (2 * width, hidden))
    x2 = x1_v[...] + scale_m_ref[layer : layer + 1, :] * acc[...]
    if last:
        valid_ref, vec_ref = r["valid"], r["vec"]
        r["patch_out"][...] = (x2[0:cells] * valid_ref[...]).astype(BF)
        r["cls_out"][...] = x2[cells : cells + 1].astype(BF)
        g_cells = r["cot"][...].astype(F32) * valid_ref[...]
        g_class = jnp.where(row == 0, r["cls_cot"][...].astype(F32), 0.0)
        g = jnp.concatenate([g_cells, g_class], axis=0)
        keep = keep_rows(sz.rows, cells, jnp.where(info[2] == 1, 1.0, 0.0))
        vec_ref[...] = jnp.zeros_like(vec_ref)
        mlp_back_part(sz, layer, g, acc[...], keep, r["right"], r["g1"], vec_ref, x1_v, br_v, slope_v,
                      w_up, w_down, gain_m_ref, scale_a_ref, scale_m_ref, acc)
    else:
        r["x2"][...] = x2
        qkv_part(sz, info, x2, gain_a_ref[layer + 1 : layer + 2, :], r["w_qkv"], qkv_loads, r["own_mask"][0:1, :],
                 left.at[:, pl.ds(2 * width + hidden, width)], r["next"], r["pc_out"], r["pr_out"], r["pd_out"])
        hold("left", (2 * width + hidden, left.shape[1] - 2 * width - hidden))
    copies.finish()


def mlp_back_part(sz, layer, g, down, keep, right, g1_ref, vec_ref, x1_ref, br_ref, slope_ref,
                  w_up, w_down, gain_m_ref, scale_a_ref, scale_m_ref, acc):
    width = sz.width
    vec_ref[0:1, :] = jnp.sum(keep * g * down, axis=0, keepdims=True)
    right[:, 0:width] = (scale_m_ref[layer : layer + 1, :] * g).astype(BF)
    g1_ref[...] = g
    for c in range(sz.hidden // width):
        at = slice(c * width, (c + 1) * width)
        e_up = (dot_nt(right[:, 0:width], w_down[at, :]) * slope_ref[:, at].astype(F32)).astype(BF)
        here = slice((c + 1) * width, (c + 2) * width)
        right[:, here] = e_up
        part = dot_nt(right[:, here], w_up[:, at])
        if c == 0:
            acc[...] = part
        else:
            acc[...] += part
    d_x1, gain_rows = norm_back(x1_ref[...], gain_m_ref[layer : layer + 1, :], acc[...])
    vec_ref[1:2, :] = jnp.sum(keep * gain_rows, axis=0, keepdims=True)
    g1 = g1_ref[...] + d_x1
    g1_ref[...] = g1
    right[:, width + sz.hidden :] = (scale_a_ref[layer : layer + 1, :] * g1).astype(BF)
    vec_ref[2:3, :] = jnp.sum(keep * g1 * br_ref[...].astype(F32), axis=0, keepdims=True)


def attention_back_kernel(sz, layer, info, right, qkv_ref, stat_ref, own_mask_ref, p_v, kb_v, vb_v, w,
                          dq_ref, dkv_ref, pc_ref, pr_ref, pd_ref, tab_ref,
                          kext, vext, d_o, tab):
    width, side, cells, pitch = sz.width, sz.side, sz.cells, sz.pitch
    scale = sz.head ** (-0.5)
    kext[...] = jnp.zeros_like(kext)
    vext[...] = jnp.zeros_like(vext)
    d_o[...] = dot_nt(right[:, right.shape[1] - width :], w[...])
    class_k = [jnp.zeros((PAD, sz.quad), F32) for _ in range(sz.groups)]
    class_v = [jnp.zeros((PAD, sz.quad), F32) for _ in range(sz.groups)]
    for b in range(sz.blocks):
        first = b * sz.brows * pitch
        q = qkv_ref[b * sz.bq : (b + 1) * sz.bq, 0:width] * jnp.asarray(scale, BF)
        do = d_o[b * sz.bq : (b + 1) * sz.bq, :].astype(BF)
        for g in range(sz.groups):
            lanes = slice(g * sz.quad, (g + 1) * sz.quad)
            do_stack = stacked_heads(do[:, lanes], sz.head)
            q_stack = stacked_heads(q[:, lanes], sz.head)
            probs = p_v[b * sz.groups + g]
            wide = probs.astype(F32)
            d_prob = dot_nt(vb_v[b, :, lanes], do_stack)
            delta = jnp.sum(wide * d_prob, axis=0, keepdims=True)
            d_score = wide * (d_prob - delta)
            if b == 0:
                tab[g] = d_score
            else:
                tab[g] += d_score
            low = d_score.astype(BF)
            d_v = dot(probs, do_stack)
            d_k = dot(low, q_stack)
            vext[first : first + sz.class_slot, lanes] += d_v[: sz.class_slot]
            kext[first : first + sz.class_slot, lanes] += d_k[: sz.class_slot]
            class_v[g] = class_v[g] + d_v[sz.class_slot :]
            class_k[g] = class_k[g] + d_k[sz.class_slot :]
            d_q = folded_heads(dot_tn(low, kb_v[b, :, lanes]), sz.head) * scale
            dq_ref[b * sz.bq : (b + 1) * sz.bq, lanes] = d_q.astype(BF)
    mask = own_mask_ref[0:1, :]
    own, q_heads, k_c, v_c, scores, self_score = class_scores(sz, info, qkv_ref, mask)
    top = jnp.max(jnp.where(own, stat_ref[0:1, :], MASKED), axis=1, keepdims=True)
    total = jnp.max(jnp.where(own, stat_ref[1:2, :], 0.0), axis=1, keepdims=True)
    real = lax.broadcasted_iota(jnp.int32, (16, 1), 0) < sz.heads
    probs = jnp.where((mask > -1.0) & real, jnp.exp(scores - top) / total, 0.0)
    self_prob = jnp.where((info[2] == 1) & real, jnp.exp(self_score - top) / total, 0.0)
    d_class = jnp.where(own, d_o[cells : cells + 1, :], 0.0)
    delta = jnp.sum(d_class * stat_ref[2:3, :], axis=1, keepdims=True)
    d_low = d_class.astype(BF)
    d_cell = probs * (dot_nt(d_low, qkv_ref[0:cells, 2 * width :]) - delta)
    d_cell_low = d_cell.astype(BF)
    d_self = self_prob * (jnp.sum(d_class * v_c, axis=1, keepdims=True) - delta)

    def to_row(v):
        return jnp.sum(jnp.where(own, v, 0.0), axis=0, keepdims=True)

    g_q = to_row(dot(d_cell_low, qkv_ref[0:cells, width : 2 * width]) + d_self * k_c) * scale
    g_k = to_row(d_self * q_heads) * scale + jnp.concatenate([c[0:1] for c in class_k], axis=1)
    g_v = to_row(self_prob * d_class) + jnp.concatenate([c[0:1] for c in class_v], axis=1)
    add_k = dot_tn(d_cell_low, q_heads.astype(BF)) * scale
    add_v = dot_tn(probs.astype(BF), d_low)
    beside, above = rim_places(sz, info)
    for r in range(side):
        base = pitch * (r + RADIUS) + PAD
        rows = slice(r * side, (r + 1) * side)
        dkv_ref[rows, 0:width] = kext[base : base + side, :] + add_k[rows]
        dkv_ref[rows, width:] = vext[base : base + side, :] + add_v[rows]

    def pair(at, count):
        at = pl.ds(pl.multiple_of(at, 8), count)
        return jnp.concatenate([kext[at, :], vext[at, :]], axis=1)

    def edges():
        return (
            [pair(pitch * (above + t) + PAD, side) for t in range(RADIUS)],
            [pair(pitch * (above + t) + beside, PAD) for t in range(RADIUS)],
        )

    send_rims(sz, info, lambda r: pair(pitch * (r + RADIUS) + beside, PAD), edges,
              stat_rows([g_q, g_k, g_v]), pc_ref, pr_ref, pd_ref)
    per_head = sz.bq
    for g in range(sz.groups):
        turned = tab[g].T
        for h in range(4):
            total_h = jnp.zeros((side, sz.bk), F32)
            for r in range(sz.brows):
                at = h * per_head + r * side
                piece = turned[at : at + side]
                shift = (sz.bk - pitch * r) % sz.bk
                total_h = total_h + (pltpu.roll(piece, shift, 1) if shift else piece)
            tab_row = jnp.zeros((1, sz.bk), F32)
            for c in range(side):
                one = total_h[c : c + 1]
                tab_row = tab_row + (pltpu.roll(one, sz.bk - c, 1) if c else one)
            tab_ref[4 * g + h : 4 * g + h + 1, :] = tab_row
    tab_ref[sz.heads : 16, :] = jnp.zeros((16 - sz.heads, sz.bk), F32)


def qkv_back_part(sz, info, dq_ref, dkv_ref, st_ref, rc_ref, rr_ref, rd_ref, x_ref, gain, g1_ref, eq_ref, dkv, acc, wq):
    width, side, cells = sz.width, sz.side, sz.cells
    dkv[...] = dkv_ref[...]
    beside = PAD * (1 - info[1])
    edge = (1 - info[0]) * (side - RADIUS) * side
    sides = rc_ref[0 : side * PAD, :].astype(F32)
    for r in range(side):
        dkv[pl.ds(pl.multiple_of(r * side + beside, 8), PAD), :] += sides[r * PAD : (r + 1) * PAD]
    dkv[pl.ds(pl.multiple_of(edge, 8), RADIUS * side), :] += rr_ref[0 : RADIUS * side, :].astype(F32)
    corner = rd_ref[0 : (RADIUS + 1) * PAD, :].astype(F32)
    for t in range(RADIUS):
        dkv[pl.ds(pl.multiple_of(edge + t * side + beside, 8), PAD), :] += corner[t * PAD : (t + 1) * PAD]
    ordered = all_stats(sz, info, st_ref, rc_ref, rr_ref, rd_ref)
    class_row = jnp.concatenate(
        [functools.reduce(lambda a, b: a + b, [o[i] for o in ordered]) for i in range(3)], axis=1
    )
    row = lax.broadcasted_iota(jnp.int32, (16, 3 * width), 0)
    eq_ref[0:cells, 0:width] = dq_ref[...]
    eq_ref[0:cells, width:] = dkv[...].astype(BF)
    eq_ref[cells : cells + 16, :] = jnp.where(row == 0, class_row, 0.0).astype(BF)
    for i in range(3):
        cols = slice(i * width, (i + 1) * width)
        part = dot_nt(eq_ref[:, cols], wq[:, cols])
        if i == 0:
            acc[...] = part
        else:
            acc[...] += part
    d_x, gain_rows = norm_back(x_ref[...], gain, acc[...])
    return g1_ref[...] + d_x, gain_rows


def small_rows(sz, small_ref, vec_ref, tab_ref, gain_sum):
    small_ref[...] = jnp.zeros_like(small_ref)
    small_ref[0:3, :] = vec_ref[0:3, :]
    small_ref[3:4, :] = gain_sum
    small_ref[8:24, 0 : sz.bk] = tab_ref[...]


def qkv_back_kernel(sz, layer, info, dq_ref, dkv_ref, st_ref, rc_ref, rr_ref, rd_ref, x_ref, g1_ref, vec_ref, tab_ref,
                    gain_a_ref, wq, eq_ref, ek_ref, ev_ref, small_ref, g_ref, dkv, acc, eq_v):
    width = sz.width
    g, gain_rows = qkv_back_part(sz, info, dq_ref, dkv_ref, st_ref, rc_ref, rr_ref, rd_ref, x_ref,
                                 gain_a_ref[layer : layer + 1, :], g1_ref, eq_v, dkv, acc, wq)
    for i, ref in enumerate((eq_ref, ek_ref, ev_ref)):
        ref[...] = eq_v[:, i * width : (i + 1) * width]
    keep = keep_rows(sz.rows, sz.cells, jnp.where(info[2] == 1, 1.0, 0.0))
    small_rows(sz, small_ref, vec_ref, tab_ref, jnp.sum(keep * gain_rows, axis=0, keepdims=True))
    g_ref[...] = g


def mlp_back_kernel(sz, layer, info, g_ref, gain_m_ref, scale_a_ref, scale_m_ref, x1_ref, br_ref, down_ref,
                    slope_ref, w_up, w_down, right, g1_out, vec_out, acc):
    keep = keep_rows(sz.rows, sz.cells, jnp.where(info[2] == 1, 1.0, 0.0))
    vec_out[...] = jnp.zeros_like(vec_out)
    mlp_back_part(sz, layer, g_ref[...], down_ref[...].astype(F32), keep, right, g1_out, vec_out,
                  x1_ref, br_ref, slope_ref, w_up, w_down, gain_m_ref, scale_a_ref, scale_m_ref, acc)


def last_kernel(sz, info, dq_ref, dkv_ref, st_ref, rc_ref, rr_ref, rd_ref, patch_ref, cls_ref, g1_ref, vec_ref, tab_ref,
                gain_a_ref, wq, eq_ref, ek_ref, ev_ref, small_ref, pg_ref, cg_ref, dkv, acc, x_ref, eq_v):
    width = sz.width
    row = lax.broadcasted_iota(jnp.int32, (16, width), 0)
    x_ref[0 : sz.cells, :] = patch_ref[...].astype(F32)
    x_ref[sz.cells :, :] = jnp.where(row == 0, cls_ref[...].astype(F32), 0.0)
    g, gain_rows = qkv_back_part(sz, info, dq_ref, dkv_ref, st_ref, rc_ref, rr_ref, rd_ref, x_ref,
                                 gain_a_ref[0:1, :], g1_ref, eq_v, dkv, acc, wq)
    for i, ref in enumerate((eq_ref, ek_ref, ev_ref)):
        ref[...] = eq_v[:, i * width : (i + 1) * width]
    keep = keep_rows(sz.rows, sz.cells, jnp.where(info[2] == 1, 1.0, 0.0))
    small_rows(sz, small_ref, vec_ref, tab_ref, jnp.sum(keep * gain_rows, axis=0, keepdims=True))
    pg_ref[...] = g[0 : sz.cells]
    cg_ref[...] = g[sz.cells : sz.cells + 1]


def product(sz, info, left_ref, left_got, own_ref, other_ref):
    cells = sz.cells
    row = lax.broadcasted_iota(jnp.int32, (16, own_ref.shape[1]), 0)
    tail = own_ref[cells : cells + 16, :]
    tail = jnp.where((row < 0) | (info[0] == 0), tail, jnp.zeros_like(tail))
    left = jnp.concatenate([left_ref[0:cells, :], left_got[0:cells, :], left_ref[cells : cells + 16, :]], axis=0)
    right = jnp.concatenate([own_ref[0:cells, :], other_ref[0:cells, :], tail], axis=0)
    return dot_tn(left, right)


def store_pieces(value, count, pairs, bit, place, send_ref, keep_ref):
    per = value.shape[0] // count
    for a, b in pairs:
        one, two = value[a * per : (a + 1) * per], value[b * per : (b + 1) * per]
        at = place(a)
        keep_ref[at] = jnp.where(bit == 0, one, two).astype(BF)
        send_ref[at] = jnp.where(bit == 0, two, one).astype(BF)


def pairs_of(bits, bit):
    return [(a, a | 1 << bit) for a in range(1 << bits) if not a >> bit & 1]


def order_of(bits, skip, first):
    def place(a, me):
        names = list(first) + [b for b in range(bits - 1, -1, -1) if b != skip and b not in first]
        at = 0
        for b in names:
            mine = (a >> b) & 1
            at = at * 2 + (mine if b == 0 else mine ^ ((me >> b) & 1))
        return at

    return place


def down_kernel(sz, info, act_ref, act_got, own_ref, other_ref, send_ref, keep_ref):
    bits = sz.bits - 2
    me = info[4]
    value = product(sz, info, act_ref, act_got, own_ref, other_ref)
    place = order_of(bits, 2, (1,))
    store_pieces(value, 1 << bits, pairs_of(bits, 2), (me >> 2) & 1, lambda a: place(a, me), send_ref, keep_ref)


def columns_step(sz, info, bit, order, value, send_ref, keep_ref):
    bits = sz.bits - 1
    me = info[4]
    place = order_of(bits, bit, order)
    store_pieces(value, 1 << bits, pairs_of(bits, bit), (me >> bit) & 1, lambda a: place(a, me), send_ref, keep_ref)


def up_kernel(sz, info, h_ref, h_got, own_ref, other_ref, send_ref, keep_ref):
    columns_step(sz, info, 1, (2,), product(sz, info, h_ref, h_got, own_ref, other_ref), send_ref, keep_ref)


def attn_grad_kernel(sz, info, h_ref, h_got, qo, qg, ko, kg, vo, vg, a_ref, a_got, bo, bg, send_ref, keep_ref):
    step = pl.program_id(0)
    bit = sz.bits - 2
    cases = [(h_ref, h_got, qo, qg, (1, 2)), (h_ref, h_got, ko, kg, (1, 2)), (h_ref, h_got, vo, vg, (2, 1)),
             (a_ref, a_got, bo, bg, (2, 1))]
    for i, (*factors, order) in enumerate(cases):
        @pl.when(step == i)
        def _():
            columns_step(sz, info, bit, order, product(sz, info, *factors), send_ref, keep_ref)


def plus(a, b):
    return a.astype(F32) + b.astype(F32)


def second_kernel(info, k0, g0, k1, g1, s0_ref, k0_ref, s1_ref, k1_ref):
    s0_ref[...] = plus(k0[:, 1], g0[:, 1]).astype(BF)
    k0_ref[...] = plus(k0[:, 0], g0[:, 0]).astype(BF)
    s1_ref[...] = plus(k1[:, 1], g1[:, 1]).astype(BF)
    k1_ref[...] = plus(k1[:, 0], g1[:, 0]).astype(BF)


def third_kernel(info, k0, g0, k1, g1, s_ref, k_ref):
    s_ref[0] = plus(k0[1], g0[1]).astype(BF)
    k_ref[0] = plus(k0[0], g0[0]).astype(BF)
    s_ref[1] = plus(k1[1], g1[1]).astype(BF)
    k_ref[1] = plus(k1[0], g1[0]).astype(BF)


def more_kernel(info, k, g, s_ref, k_ref):
    s_ref[...] = plus(k[:, 1], g[:, 1]).astype(BF)
    k_ref[...] = plus(k[:, 0], g[:, 0]).astype(BF)


def z_second_kernel(info, k, g, s0_ref, s1_ref, k_ref):
    for i, ref in enumerate((s0_ref, s1_ref)):
        ref[...] = plus(k[i, 1], g[i, 1]).astype(BF)
        k_ref[i] = plus(k[i, 0], g[i, 0]).astype(BF)


def z_third_kernel(info, k, g0, g1, s0_ref, s1_ref, k_ref):
    for i, (g, ref) in enumerate(((g0, s0_ref), (g1, s1_ref))):
        ref[...] = plus(k[i, 1], g[1]).astype(BF)
        k_ref[i] = plus(k[i, 0], g[0]).astype(BF)


def z_fourth_kernel(sz, info, k, g0, g1, a_ref, b_ref):
    high = (info[4] >> (sz.bits - 1)) & 1
    for i, g in enumerate((g0, g1)):
        one, two = plus(k[i, 0], g[0]), plus(k[i, 1], g[1])
        a_ref[i] = jnp.where(high == 0, one, two).astype(BF)
        b_ref[i] = jnp.where(high == 0, two, one).astype(BF)


def fourth_kernel(sz, info, k, g, a_ref, b_ref):
    high = (info[4] >> (sz.bits - 1)) & 1
    one, two = plus(k[:, 0], g[:, 0]), plus(k[:, 1], g[:, 1])
    a_ref[...] = jnp.where(high == 0, one, two).astype(BF)
    b_ref[...] = jnp.where(high == 0, two, one).astype(BF)


def bias_kernel(sz, table_ref, out_ref, wide):
    slot = lax.broadcasted_iota(jnp.int32, (sz.side, sz.bk), 1)
    for g in range(sz.groups):
        for h in range(4):
            line = jnp.broadcast_to(table_ref[4 * g + h : 4 * g + h + 1, :], (sz.side, sz.bk))
            line = pltpu.roll(line, 0, 1, stride=1, stride_axis=0)
            for r in range(sz.brows):
                piece = pltpu.roll(line, sz.pitch * r, 1) if r else line
                at = h * sz.bq + r * sz.side
                wide[at : at + sz.side, :] = jnp.where(slot == sz.class_slot, 0.0, piece)
        out_ref[g] = wide[...].T


def shape(dims, dtype):
    return jax.ShapeDtypeStruct(dims, dtype)


def kept(dims, dtype):
    return pltpu.HBM(dims, dtype)


def inside(dims, dtype):
    return pltpu.VMEM(dims, dtype)


def whole(dims):
    return pl.BlockSpec(dims, lambda *_: (0,) * len(dims))


IN = pl.BlockSpec(memory_space=pltpu.VMEM)


ANY = pl.BlockSpec(memory_space=pl.ANY)
MEDIUM = 4 * 10**9
LONG = 10**11


def local(patch_in, cls_in, page_side, norm_attn, qkv_weight, rel_table, out_weight, scale_attn,
          norm_mlp, up_weight, down_weight, scale_mlp, patch_cot, cls_cot):
    tiles = lax.axis_size("tile")
    pages = lax.axis_size("dp")
    layers, heads = rel_table.shape[:2]
    sz = Sizes(patch_in.shape[2], patch_in.shape[4], up_weight.shape[2], heads, tiles * pages)
    side, cells, rows, width, hidden = sz.side, sz.cells, sz.rows, sz.width, sz.hidden
    chunks = hidden // width
    tile = lax.axis_index("tile")
    me = lax.axis_index("dp") * tiles + tile
    tile_row, tile_col = tile // 2, tile % 2
    page = page_side[0]
    bits = sz.bits
    top_bit, next_bit = bits - 1, bits - 2
    info = jnp.stack([tile_row, tile_col, (tile == 0).astype(jnp.int32), (me >> next_bit) & 1, me]).astype(jnp.int32)

    cell = np.arange(cells)
    own_ok = (tile_row * side + cell // side < page) & (tile_col * side + cell % side < page)
    own_mask = jnp.broadcast_to(jnp.where(own_ok, 0.0, MASKED).astype(F32), (8, cells))
    valid = own_ok.astype(F32)[:, None]
    slot = np.arange(sz.bk)[None] + np.arange(sz.blocks)[:, None] * sz.brows * sz.pitch - PAD + RADIUS
    key_row = tile_row * side + slot // sz.pitch - RADIUS
    key_col = tile_col * side + slot % sz.pitch - RADIUS
    is_class = (np.arange(sz.bk) == sz.class_slot)[None]
    key_ok = (key_row >= 0) & (key_row < page) & (key_col >= 0) & (key_col < page) | is_class
    key_mask = jnp.broadcast_to(
        jnp.where(key_ok, 0.0, MASKED).astype(F32)[:, :, None], (sz.blocks, sz.bk, sz.bk // 2)
    )
    lines = jnp.pad(rel_table.reshape(layers, heads, SPAN, SPAN), ((0, 0), (0, 16 - heads), (0, 0), (0, sz.pitch - SPAN)),
                    constant_values=MASKED).reshape(layers, 16, SPAN * sz.pitch)
    first_slot = PAD - RADIUS
    lines = jnp.pad(lines, ((0, 0), (0, 0), (first_slot, sz.bk - first_slot - SPAN * sz.pitch)), constant_values=MASKED)

    resident = {}
    before = []

    def call(kernel, grid, in_specs, out_specs, out_shape, scratch=(), vmem=12, weight=1, also=(), place=pltpu.HBM, ahead=()):
        deps = [pltpu.with_memory_space_constraint(a, pltpu.HBM) for a in before] + list(also)
        count = len(in_specs)

        results = list(out_shape) if isinstance(out_shape, (list, tuple)) else [out_shape]
        result_specs = list(out_specs) if isinstance(out_specs, (list, tuple)) else [out_specs]
        results.append(kept((8, 128), F32))
        result_specs.append(ANY)
        more, own = len(ahead), len(results)

        def body(*refs):
            refs = list(refs)
            mine, refs = refs[: 1 + count], refs[1 + count + len(deps) :]
            sources, refs = refs[:more], refs[more:]
            made, refs = refs[:own], refs[own:]
            targets, refs = refs[:more], refs[more:]
            made.pop()
            if not more:
                return kernel(*mine, *made, *refs)
            sem = refs.pop()
            copies = [
                pltpu.make_async_copy(src if index is None else src.at[index], dst, sem.at[n])
                for n, (src, dst, (_, index)) in enumerate(zip(sources, targets, ahead))
            ]

            @pl.when(pl.program_id(0) == 0)
            def _():
                for copy in copies:
                    copy.start()

            kernel(*mine, *made, *refs)

            @pl.when(pl.program_id(0) == pl.num_programs(0) - 1)
            def _():
                for copy in copies:
                    copy.wait()

        results += [inside(a.shape if index is None else a.shape[1:], a.dtype) for a, index in ahead]
        if more:
            scratch = list(scratch) + [pltpu.SemaphoreType.DMA((more,))]

        run = pl.pallas_call(
            body,
            grid_spec=pltpu.PrefetchScalarGridSpec(
                num_scalar_prefetch=1,
                grid=grid,
                in_specs=list(in_specs) + [ANY] * (len(deps) + more),
                out_specs=result_specs + [IN] * more,
                scratch_shapes=list(scratch),
            ),
            out_shape=results,
            compiler_params=pltpu.CompilerParams(vmem_limit_bytes=vmem * MIB),
            cost_estimate=pl.CostEstimate(flops=weight, bytes_accessed=1, transcendentals=0),
        )

        def go(*args):
            pinned = []
            for a, spec in zip(args, in_specs):
                if id(a) in resident:
                    a = pltpu.with_memory_space_constraint(a, pltpu.VMEM)
                elif place is pltpu.VMEM and a.size <= 2 * sz.ext_rows * width:
                    a = pltpu.with_memory_space_constraint(a, pltpu.VMEM)
                elif spec is not IN and place is pltpu.HBM:
                    a = pltpu.with_memory_space_constraint(a, pltpu.HBM if spec is ANY else place)
                pinned.append(a)
            sources = [pltpu.with_memory_space_constraint(a, pltpu.HBM) for a, _ in ahead]
            out = run(info, *pinned, *deps, *sources)
            for a, like in zip(out, results):
                if not isinstance(like, jax.ShapeDtypeStruct) and like.memory_space == pltpu.VMEM:
                    resident[id(a)] = a
            out = list(out)
            before[:] = [out.pop(own - 1)]
            return out if len(out) > 1 else out[0]

        return go

    def partner(value, x):
        return lax.ppermute(value, "tile", [(t, t ^ x) for t in range(tiles)])

    def exchange(rims):
        return [partner(v, x + 1) for x, v in enumerate(rims)]

    def swap(value, bit):
        if bit < 2:
            return partner(value, 1 << bit)
        return lax.ppermute(value, "dp", [(d, d ^ (1 << (bit - 2))) for d in range(pages)])

    def both(value):
        return value, partner(value, 1)

    def vm(dims, dtype):
        return pltpu.VMEM(dims, dtype)

    sems = pltpu.SemaphoreType.DMA((40,))
    row_w, par = whole((rows, width)), whole((layers, width))
    wide = whole((rows, 3 * width))
    pc_rows, pr_rows, pd_rows = side * PAD + 16, RADIUS * side + 16, (RADIUS + 1) * PAD + 16
    rim_shapes = [shape((n, 2 * width), BF) for n in (pc_rows, pr_rows, pd_rows)]
    rim_specs = [whole(s.shape) for s in rim_shapes]
    stat_spec = pl.BlockSpec((16, 2 * width), lambda *_: (side * PAD // 16, 0))
    nb, ng = sz.blocks, sz.groups
    square = (width, width)

    x, qkv, *rims = call(
        functools.partial(first_kernel, sz),
        (1,),
        [whole((cells, width)), whole((1, width)), par, whole((8, cells)), ANY],
        [IN] * 5,
        [inside((rows, width), F32), inside((rows, 3 * width), BF)] + rim_shapes,
        [vm((rows, width), BF), vm((width, 3 * width), BF), sems],
    )(patch_in.reshape(cells, width), cls_in, norm_attn, own_mask, qkv_weight)
    got = exchange(rims)
    bias, w_out, w_up, w_down, gain_a, scale_a, gain_m, scale_m = call(
        lambda info, *refs: bias_kernel(sz, *refs),
        (layers,),
        [pl.BlockSpec((None, 16, sz.bk), lambda l, s: (l, 0, 0))],
        pl.BlockSpec((None, ng, sz.bk, sz.bk), lambda l, s: (l, 0, 0, 0)),
        inside((layers, ng, sz.bk, sz.bk), F32),
        [vm((sz.bk, sz.bk), F32)],
        ahead=[(out_weight, 0), (up_weight, 0), (down_weight, 0)]
        + [(v, None) for v in (norm_attn, scale_attn, norm_mlp, scale_mlp)],
    )(lines)
    saved = []
    for l in range(layers):
        last = l == layers - 1
        given = dict(qkv=qkv, pc=rims[0], rc=got[0], rr=got[1], rd=got[2], bias=bias, mask=key_mask, x=x, own_mask=own_mask,
                     scale_a=scale_a, gain_m=gain_m, scale_m=scale_m, gain_a=gain_a,
                     w_out=w_out, w_up=w_up, w_down=w_down)
        left_width = 2 * width + hidden + (0 if last else width) + (0 if l else width)
        held = dict(p=((nb * ng, sz.bk, sz.bk), BF), kb=((nb, sz.bk, width), BF), vb=((nb, sz.bk, width), BF),
                    left=((rows, left_width), BF))
        local_only = dict(slope=((rows, hidden), BF), x1=((rows, width), F32), br=((rows, width), BF), down=((rows, width), BF))
        made = dict(stats=inside((8, width), F32))
        spots = dict(kext=vm((sz.ext_rows, width), F32), vext=vm((sz.ext_rows, width), F32), acc=vm((rows, width), F32))
        spots.update({n: vm(*d) for n, d in local_only.items()})
        if last:
            given.update(cot=cot, cls_cot=cls_cot, valid=valid)
            made.update({n: inside(*d) for n, d in held.items()})
            made.update(right=inside((rows, 2 * width + hidden), BF), g1=inside((rows, width), F32), vec=inside((8, width), F32),
                        patch_out=shape((cells, width), BF), cls_out=shape((1, width), BF))
            specs = [IN] * len(made)
        else:
            given.update(qkv_w=qkv_weight)
            made.update(x2=inside((rows, width), F32), next=inside((rows, 3 * width), BF),
                        pc_out=rim_shapes[0], pr_out=rim_shapes[1], pd_out=rim_shapes[2])
            specs = [IN] * len(made)
            spots.update({n: vm(*d) for n, d in held.items()})
            spots.update(w_qkv=vm((width, 3 * width), BF))
            stored = dict(held, **local_only, qkv=((rows, 3 * width), BF))
            made = dict({n + "_out": kept(*d) for n, d in stored.items()}, **made)
            specs = [ANY] * len(stored) + specs
        spots.update(sems=sems)
        names = list(given) + list(made) + list(spots)
        out = call(functools.partial(middle_kernel, sz, l, last, names), (1,),
                   [ANY if n == "qkv_w" else IN for n in given], specs, list(made.values()), list(spots.values()), vmem=18 if last else 28,
                   )(*given.values())
        res = dict(zip(made, out))
        keep_names = list(held) if last else list(stored)
        entry = {n: res[n if last else n + "_out"] for n in keep_names}
        entry.setdefault("qkv", qkv)
        entry.update(x=x, stats=res["stats"])
        entry["left"] = both(entry["left"])
        entry["h"] = (entry["left"], left_width // width - 1) if l == 0 else (saved[l - 1]["left"], 2 + chunks)
        saved.append(entry)
        if last:
            patch_out, cls_out, right, g1, vec = (res[n] for n in ("patch_out", "cls_out", "right", "g1", "vec"))
        else:
            x, qkv = res["x2"], res["next"]
            rims = [res[n] for n in ("pc_out", "pr_out", "pd_out")]
            got = exchange(rims)
            w_out, w_up, w_down, cot = call(
                lambda info, a: None, (1,), [IN], [], [],
                ahead=[(out_weight, l + 1), (up_weight, l + 1), (down_weight, l + 1), (patch_cot.reshape(cells, width), None)],
                vmem=2,
            )(own_mask)

    def attention_back(l, right, v, also):
        return call(
            functools.partial(attention_back_kernel, sz, l),
            (1,),
            [IN] * 8,
            [IN] * 6,
            [inside((cells, width), BF), inside((cells, 2 * width), F32)] + rim_shapes + [inside((16, sz.bk), F32)],
            [vm((sz.ext_rows, width), F32)] * 2 + [vm((rows, width), F32), vm((ng, sz.bk, sz.bk), F32)],
            also=also,
        )(right, v["qkv"], v["stats"], own_mask, v["p"], v["kb"], v["vb"], v["w_out"])

    back_scratch = [vm((cells, 2 * width), F32), vm((rows, width), F32)]

    def qkv_back(l, d_q, d_kv, own, got, g1, vec, table, wq):
        *e_qkv, rows_small, g, down_w, up_w = call(
            functools.partial(qkv_back_kernel, sz, l),
            (1,),
            [IN] * 12,
            [IN] * 5,
            [inside((rows, width), BF)] * 3 + [inside((24, width), F32), inside((rows, width), F32)],
            back_scratch + [vm((rows, 3 * width), BF)],
            weight=LONG, ahead=[(down_weight, l - 1), (up_weight, l - 1)],
        )(d_q, d_kv, own, *got, saved[l]["x"], g1, vec, table, gain_a, wq)
        return [both(e) for e in e_qkv], rows_small, g, up_w, down_w

    def mlp_back(l, g, up_w, down_w):
        v = saved[l]
        names = ["qkv", "p", "kb", "vb"]
        out = call(
            functools.partial(mlp_back_kernel, sz, l),
            (1,),
            [IN] * 10,
            [IN] * 3,
            [inside((rows, 2 * width + hidden), BF), inside((rows, width), F32), inside((8, width), F32)],
            [vm((rows, width), F32)],
            ahead=[(v[n], None) for n in names] + [(out_weight, l)],
        )(g, gain_m, scale_a, scale_m, v["x1"], v["br"], v["down"], v["slope"], up_w, down_w)
        near = dict(zip(names + ["w_out"], out[3:]), stats=v["stats"])
        return out[0], out[1], out[2], near

    def finish(d_q, d_kv, own, got, g1, vec, table, wq, first):
        return call(
            functools.partial(last_kernel, sz),
            (1,),
            [IN] * 13,
            [IN] * 6,
            [inside((rows, width), BF)] * 3 + [inside((24, width), F32), shape((cells, width), F32), shape((1, width), F32)],
            back_scratch + [vm((rows, width), F32), vm((rows, 3 * width), BF)],
        )(d_q, d_kv, own, *got, first, cls_in, g1, vec, table, gain_a, wq)

    piece, ff_piece = width // sz.devices, hidden // sz.devices
    half = width // 2
    quarter = sz.devices // 4

    def pair(dims):
        return [shape(dims, BF), inside(dims, BF)]

    def halves(start):
        return pl.BlockSpec((rows, half), lambda i, s: (0, 2 * start + s[1]))

    def grad_down(act, e_down, weight=1, also=()):
        lspec = pl.BlockSpec((rows, width), lambda i, s: (0, act[1] + s[1] * (chunks // 2) + i))
        rspec = pl.BlockSpec((rows, width), lambda i, s: (0, e_down[1]))
        out = pl.BlockSpec((None, quarter // 2, ff_piece, width), lambda i, s: (i ^ s[3], 0, 0, 0))
        return call(
            functools.partial(down_kernel, sz),
            (2,),
            [lspec, lspec, rspec, rspec],
            [out, out],
            pair((2, quarter // 2, ff_piece, width)),
            weight=weight, also=also,
            vmem=20, place=None,
        )(*act[0], *e_down[0])

    def grad_up(h2, e_up, also, ahead):
        lspec = halves(h2[1])
        rspec = pl.BlockSpec((rows, width), lambda i, s: (0, e_up[1] + i))
        out = pl.BlockSpec((quarter, None, piece, width), lambda i, s: (0, i, 0, 0))
        return call(
            functools.partial(up_kernel, sz),
            (chunks,),
            [lspec, lspec, rspec, rspec],
            [out, out],
            pair((quarter, chunks, piece, width)),
            also=also, vmem=20, place=None, ahead=ahead,
        )(*h2[0], *e_up[0])

    def grad_attn(h, e_qkv, att, e_branch):
        out = pl.BlockSpec((None, quarter, None, piece, width), lambda i, s: (i // 2, 0, i % 2, 0, 0))
        hspec, aspec = halves(h[1]), halves(att[1])
        bspec = pl.BlockSpec((rows, width), lambda i, s: (0, e_branch[1]))
        return call(
            functools.partial(attn_grad_kernel, sz),
            (4,),
            [hspec, hspec] + [row_w] * 6 + [aspec, aspec, bspec, bspec],
            [out, out],
            pair((2, quarter, 2, piece, width)),
            vmem=20, place=None,
        )(*h[0], *(v for both_e in e_qkv for v in both_e), *att[0], *e_branch[0])

    def last_route(flip):
        out = []
        for d in range(sz.devices):
            high, core = d >> top_bit, d & 1
            out.append((d, (d & ~(1 << top_bit) & ~1) | core << top_bit | (high ^ flip)))
        return out

    class ZSums:
        def __init__(self, halves_made):
            send, keep = halves_made
            self.n = quarter * 2 * piece // 2
            self.got = swap(send, next_bit).reshape(2, 2, self.n, width)
            self.keep = keep.reshape(2, 2, self.n, width)

        def second(self, weight=1):
            n = self.n
            s0, s1, k = call(
                z_second_kernel, (1,), [whole((2, 2, n, width))] * 2, [whole((n, width))] * 2 + [whole((2, n, width))],
                [shape((n, width), BF)] * 2 + [inside((2, n, width), BF)], place=pltpu.VMEM, weight=weight,
            )(self.keep, self.got)
            self.got = [swap(s0, 1), swap(s1, 2)]
            self.keep = k

        def third(self):
            n = self.n = self.n // 2
            s0, s1, k = call(
                z_third_kernel, (1,), [whole((2, 2, n, width))] + [whole((2, n, width))] * 2,
                [whole((n, width))] * 2 + [whole((2, n, width))],
                [shape((n, width), BF)] * 2 + [inside((2, n, width), BF)], place=pltpu.VMEM,
            )(self.keep.reshape(2, 2, n, width), *(g.reshape(2, n, width) for g in self.got))
            self.got = [swap(s0, 2), swap(s1, 1)]
            self.keep = k
            for bit in range(bits - 3, 2, -1):
                n = self.n = self.n // 2
                spec = whole((2, 2, n, width))
                s, k = call(
                    more_kernel, (1,), [spec, spec], [whole((2, n, width))] * 2, pair((2, n, width)), place=pltpu.VMEM,
                )(self.keep.reshape(2, 2, n, width), jnp.stack(self.got).reshape(2, 2, n, width))
                self.keep = k
                self.got = list(swap(s, bit))

        def fourth(self):
            n = self.n = self.n // 2
            a, b = call(
                functools.partial(z_fourth_kernel, sz), (1,), [whole((2, 2, n, width))] + [whole((2, n, width))] * 2,
                [whole((2, n, width))] * 2, [shape((2, n, width), BF)] * 2, place=pltpu.VMEM,
            )(self.keep.reshape(2, 2, n, width), *(g.reshape(2, n, width) for g in self.got))
            self.got = [lax.ppermute(a, ("dp", "tile"), last_route(0)), lax.ppermute(b, ("dp", "tile"), last_route(1))]

        def result(self):
            return self.got[0].astype(F32) + self.got[1].astype(F32)

    class Sums:
        def __init__(self, y_first, x_first, split):
            (s0, k0), (s1, k1) = y_first, x_first
            self.got = [swap(s0, 1), swap(s1, 2)]
            total = s0.size // width
            self.block = total // (quarter // 2)
            self.outer = split
            self.rows = total
            self.keep = [k0.reshape(1, 2, total // 2, width), k1.reshape(split, 2, total // 2 // split, width)]

        def second(self, weight=1, also=()):
            n = self.rows // 4
            got = [g.reshape(k.shape) for g, k in zip(self.got, self.keep)]
            sp = self.outer
            if sp == 1:
                other = pl.BlockSpec((1, 2, n, width), lambda i, s: (0, 0, i, 0))
                other_out = pl.BlockSpec((1, n, width), lambda i, s: (0, i, 0))
            else:
                other = pl.BlockSpec((1, 2, n, width), lambda i, s: (i, 0, 0, 0))
                other_out = pl.BlockSpec((1, n, width), lambda i, s: (i, 0, 0))
            spec = pl.BlockSpec((1, 2, n, width), lambda i, s: (0, 0, i, 0))
            spec_out = pl.BlockSpec((1, n, width), lambda i, s: (0, i, 0))
            s0, k0, s1, k1 = call(
                second_kernel, (2,), [spec, spec, other, other], [spec_out, spec_out, other_out, other_out],
                pair((1, 2 * n, width)) + pair((sp, 2 * n // sp, width)), weight=weight, place=pltpu.VMEM, also=also,
            )(self.keep[0], got[0], self.keep[1], got[1])
            self.got = [swap(s0, 2), swap(s1, 1)]
            self.keep = [k0, k1]
            self.rows //= 2

        def third(self, weight=1):
            n = self.rows // 2
            args = [v.reshape(2, n, width) for pair in zip(self.keep, self.got) for v in pair]
            s, k = call(
                third_kernel, (1,), [whole((2, n, width))] * 4, [whole((2, n, width))] * 2,
                pair((2, n, width)), weight=weight, place=pltpu.VMEM,
            )(*args)
            self.rows = n
            self.keep = k
            self.got = swap(s, bits - 2)
            for bit in range(bits - 3, 2, -1):
                n = self.rows // 2
                spec = whole((2, 2, n, width))
                s, k = call(
                    more_kernel, (1,), [spec, spec], [whole((2, n, width))] * 2, pair((2, n, width)), place=pltpu.VMEM,
                )(self.keep.reshape(2, 2, n, width), self.got.reshape(2, 2, n, width))
                self.rows = n
                self.keep = k
                self.got = swap(s, bit)

        def fourth(self):
            n = self.rows // 2
            spec = whole((2, 2, n, width))
            a, b = call(
                functools.partial(fourth_kernel, sz), (1,), [spec, spec], [whole((2, n, width))] * 2,
                [shape((2, n, width), BF)] * 2, place=pltpu.VMEM,
            )(self.keep.reshape(2, 2, n, width), self.got.reshape(2, 2, n, width))

            self.got = [lax.ppermute(a, ("dp", "tile"), last_route(0)), lax.ppermute(b, ("dp", "tile"), last_route(1))]

        def result(self):
            return self.got[0].astype(F32) + self.got[1].astype(F32)

    sums = {}
    small = [None] * layers
    early = [v["left"][1] for v in saved[:-1]]
    waiting = None
    near = dict(saved[-1], w_out=w_out)
    for l in reversed(range(layers)):
        left = saved[l]["left"]
        result = attention_back(l, right, near, early)
        d_q, d_kv, *rims, table = result
        early = []
        if waiting is not None:
            right = both(lax.optimization_barrier((right, table))[0])
            got = exchange(rims)
            sums["attn", l + 1] = ZSums(grad_attn(*waiting))
            sums["mlp", l + 1].second(LONG)
        else:
            right = both(right)
            got = exchange(rims)
        x_first = grad_down((left, 2), (right, 0))
        *y_first, wq = grad_up((left, 1), (right, 1), got if waiting is not None else (), [(qkv_weight, l)])
        sums["mlp", l] = Sums(y_first, x_first, 2)
        if l > 0:
            e_qkv, small[l], g, up_w, down_w = qkv_back(l, d_q, d_kv, rims[0], got, g1, vec, table, wq)
            waiting = (saved[l]["h"], e_qkv, (left, 0), (right, 1 + chunks))
            right, g1, vec, near = mlp_back(l - 1, g, up_w, down_w)
        else:
            *e_qkv, small[0], patch_grad, cls_grad = finish(d_q, d_kv, rims[0], got, g1, vec, table, wq, patch_in.reshape(cells, width))
            waiting = (saved[0]["h"], [both(e) for e in e_qkv], (left, 0), (right, 1 + chunks))
    total = [jnp.stack(small), None, 0]

    def step():
        value, got_value, bit = total
        if got_value is not None:
            value = value + lax.optimization_barrier((got_value, before[0]))[0]
        total[:] = [value, swap(value, bit) if bit < bits else None, bit + 1]

    step()
    if layers > 1:
        sums["mlp", 1].third()
    sums["attn", 0] = ZSums(grad_attn(*waiting))
    step()
    if layers > 1:
        sums["attn", 1].second(MEDIUM)
    sums["mlp", 0].second()
    step()
    if layers > 1:
        sums["attn", 1].third()
        sums["mlp", 1].fourth()
    sums["mlp", 0].third()
    step()
    sums["attn", 0].second()
    if layers > 1:
        sums["attn", 1].fourth()
    step()
    sums["attn", 0].third()
    sums["mlp", 0].fourth()
    while total[1] is not None:
        step()
    sums["attn", 0].fourth()
    total = total[0]
    ups, downs, firsts, seconds = [], [], [], []
    for l in range(layers):
        mlp, attn = sums["mlp", l].result(), sums["attn", l].result()
        ups.append(jnp.swapaxes(mlp[0].reshape(chunks, piece, width), 0, 1).reshape(piece, hidden))
        downs.append(mlp[1])
        attn = attn.reshape(4, piece, width)
        firsts.append(jnp.swapaxes(attn[:3], 0, 1).reshape(piece, 3 * width))
        seconds.append(attn[3])
    g_qkv, g_out, g_up, g_down = (jnp.stack(v) for v in (firsts, seconds, ups, downs))
    vectors, tables = total[:, 0:4], total[:, 8 : 8 + heads, 0 : sz.bk]
    mine = lax.dynamic_slice_in_dim(vectors, me * piece, piece, axis=2)
    tables = tables[:, :, first_slot : first_slot + SPAN * sz.pitch].reshape(layers, heads, SPAN, sz.pitch)
    g_table = tables[..., :SPAN].reshape(rel_table.shape)
    return (
        patch_out.reshape(patch_in.shape),
        cls_out,
        patch_grad.reshape(patch_in.shape),
        cls_grad,
        mine[:, 3],
        g_qkv,
        g_table,
        g_out,
        mine[:, 2],
        mine[:, 1],
        g_up,
        g_down,
        mine[:, 0],
    )


def solution(mesh):
    tokens = P("dp", "tile", None, None, None)
    split = ("dp", "tile")
    in_specs = (tokens, P("dp", None), P("dp")) + (P(),) * 9 + (tokens, P("dp", None))
    out_specs = (
        tokens,
        P("dp", None),
        tokens,
        P("dp", None),
        P(None, split),
        P(None, split, None),
        P(),
        P(None, split, None),
        P(None, split),
        P(None, split),
        P(None, split, None),
        P(None, split, None),
        P(None, split),
    )
    return jax.shard_map(local, mesh=mesh, in_specs=in_specs, out_specs=out_specs, check_vma=False)
```
